32 devices in a mesh: head: 4 (over y, x), blk: 8 (over z, core).
Axes of the slice: x: 2, y: 2, z: 4, core: 2. Of those that a mesh axis runs over, the one named last changes fastest.
Arguments:
- inputs: bfloat16 [4096, 2048], P(('blk', 'head')), may hold values from -6 to 6
- dealing: int32 [4096], replicated, may hold values from 0 to 4095, each once
- lengths: int32 [3], replicated, may hold values from 1024 to 2048, as said below
- input_gain: bfloat16 [2048], P(('head', 'blk')), may hold values from 0.099609375 to 1.8984375
- w_query: bfloat16 [2048, 2048], P(None, ('head', 'blk')), may hold values from -0.125 to 0.125
- w_key: bfloat16 [2048, 1024], P(None, ('head', 'blk')), may hold values from -0.125 to 0.125
- w_value: bfloat16 [2048, 1024], P(None, ('head', 'blk')), may hold values from -0.125 to 0.125
- query_gain: bfloat16 [128], P(('head', 'blk')), may hold values from 0.099609375 to 1.8984375
- key_gain: bfloat16 [128], P(('head', 'blk')), may hold values from 0.099609375 to 1.8984375
- w_out: bfloat16 [2048, 2048], P(('head', 'blk')), may hold values from -2 to 2
- hidden_gain: bfloat16 [2048], P('blk'), may hold values from 0.099609375 to 1.8984375
- w_gate: bfloat16 [2048, 6144], P(None, ('head', 'blk')), may hold values from -0.125 to 0.125
- w_up: bfloat16 [2048, 6144], P(None, ('head', 'blk')), may hold values from -0.125 to 0.125
- w_down: bfloat16 [6144, 2048], P(('head', 'blk')), may hold values from -0.3125 to 0.3125
- cotangent: bfloat16 [4096, 2048], P('blk'), may hold values from -6 to 6
Outputs:
- layer_out: bfloat16 [4096, 2048], P(('blk', 'head'))
- grad_input: float32 [4096, 2048], P(('blk', 'head'))
- grad_input_gain: float32 [2048], P(('head', 'blk'))
- grad_query: float32 [2048, 2048], P(None, ('head', 'blk'))
- grad_key: float32 [2048, 1024], P(None, ('head', 'blk'))
- grad_value: float32 [2048, 1024], P(None, ('head', 'blk'))
- grad_query_gain: float32 [128], P(('head', 'blk'))
- grad_key_gain: float32 [128], P(('head', 'blk'))
- grad_out: float32 [2048, 2048], P(('head', 'blk'))
- grad_hidden_gain: float32 [2048], P('blk')
- grad_gate: float32 [2048, 6144], P(None, ('head', 'blk'))
- grad_up: float32 [2048, 6144], P(None, ('head', 'blk'))
- grad_down: float32 [6144, 2048], P(('head', 'blk'))
The draws below stay inside these ranges and needn't reach their ends.
Inputs may be any that keep to these rules, and one draw needn't show every extreme that they name: 3 lengths that sum to 4096; one of them is 2048, at a place drawn from the seed. `dealing`: a permutation of the packed tokens.
All inputs are finite; a program needn't handle non-finite values.
Results may differ from the reference program's by a relative error of at most 0.04.
Values may be sent and summed in bfloat16 or wider, within the bound.
No kernel may reach another device: no remote copies, remote signals or barrier semaphores. Data moves between devices by JAX's collectives and lax.ppermute only.
A program may use at most 256 MiB of HBM per device.

```python
import math
import jax
import jax.numpy as jnp
from jax import lax

D = 2048
QH = 16
KVH = 8
HD = 128
FF = 6144
TOKENS = 4096
SEQ_MAX = 2048
SEQ_MIN = 1024


def draw_lengths(key, part):
    key = jax.random.fold_in(key, 11)
    pair_count = TOKENS // SEQ_MAX - 1
    first_key, second_key = jax.random.split(key)
    shorter = jax.random.randint(first_key, (pair_count,), SEQ_MIN, SEQ_MAX - SEQ_MIN + 1)
    shorter = jnp.where(jnp.arange(pair_count) == 0, SEQ_MIN, shorter)
    longest = jnp.full((1,), SEQ_MAX, jnp.int32)
    pieces = jnp.concatenate([longest, shorter.astype(jnp.int32), (SEQ_MAX - shorter).astype(jnp.int32)])
    order = jax.random.permutation(second_key, pieces.shape[0])
    return pieces[order].astype(jnp.int32)


def levels(stream_key, extent, cuts, least, top_value):
    level = 1.0
    for position, shards_of in cuts:
        heights = jax.random.uniform(jax.random.fold_in(jax.random.fold_in(stream_key, 6), position), (shards_of,), jnp.float32, least / len(cuts), top_value / len(cuts))
        level = level * jnp.repeat(jnp.exp(heights), extent[position] // shards_of).reshape((-1,) + (1,) * (len(extent) - 1 - position))
    return level


def scatter_about(own_key, extent, width, limit, cuts=(), kind=jnp.bfloat16):
    array = width * jax.random.normal(own_key, extent, jnp.float32)
    if cuts:
        array = array * levels(own_key, extent, cuts, -0.22, 0.18)
    return jnp.clip(array, -limit, limit).astype(kind)


def setup_inputs(seed: int = 0) -> dict:
    seeds = jax.random.split(jax.random.key(seed), 16)
    return {
        "inputs": scatter_about(seeds[0], (TOKENS, D), 1.0, 6.0, ((0, 32),)),
        "dealing": jax.random.permutation(seeds[1], TOKENS).astype(jnp.int32),
        "lengths": draw_lengths(jax.random.fold_in(seeds[15], 71), 0),
        "input_gain": jnp.clip(1.0 + 0.18 * jax.random.normal(seeds[3], (D,), jnp.float32), 0.099609375, 1.8984375).astype(jnp.bfloat16),
        "w_query": scatter_about(seeds[4], (D, QH * HD), D ** -0.5, 0.125, ((1, 32),)),
        "w_key": scatter_about(seeds[5], (D, KVH * HD), D ** -0.5, 0.125, ((1, 32),)),
        "w_value": scatter_about(seeds[6], (D, KVH * HD), D ** -0.5, 0.125, ((1, 32),)),
        "query_gain": jnp.clip(1.0 + 0.18 * jax.random.normal(seeds[7], (HD,), jnp.float32), 0.099609375, 1.8984375).astype(jnp.bfloat16),
        "key_gain": jnp.clip(1.0 + 0.18 * jax.random.normal(seeds[8], (HD,), jnp.float32), 0.099609375, 1.8984375).astype(jnp.bfloat16),
        "w_out": scatter_about(seeds[9], (QH * HD, D), (QH * HD // 256) ** -0.5, 2.0, ((0, 32),)),
        "hidden_gain": jnp.clip(1.0 + 0.18 * jax.random.normal(seeds[10], (D,), jnp.float32), 0.099609375, 1.8984375).astype(jnp.bfloat16),
        "w_gate": scatter_about(seeds[11], (D, FF), D ** -0.5, 0.125, ((1, 32),)),
        "w_up": scatter_about(seeds[12], (D, FF), D ** -0.5, 0.125, ((1, 32),)),
        "w_down": scatter_about(seeds[13], (FF, D), (FF // 16) ** -0.5, 0.3125, ((0, 32),)),
        "cotangent": scatter_about(seeds[14], (TOKENS, D), 1.0, 6.0, ((0, 8),)),
    }


EPSILON = 1e-06
ROPE_BASE = 1000000.0
PRECISE = lax.Precision.HIGHEST

@jax.custom_vjp
def low(v):
    return lax.optimization_barrier(v.astype(jnp.bfloat16)).astype(jnp.float32)

@jax.custom_vjp
def low_back(v):
    return v

def low_keep(v):
    return (low(v), None)

def low_pass(kept, grad):
    return (grad,)

def back_keep(v):
    return (v, None)

def back_low(kept, grad):
    return (low(grad),)
low.defvjp(low_keep, low_pass)
low_back.defvjp(back_keep, back_low)

def rms_scale(values):
    return lax.rsqrt(lax.optimization_barrier(jnp.mean(values * values, axis=-1, keepdims=True)) + EPSILON)

def norm_rope(projected, gain, cosine, sine):
    heads = projected.reshape(projected.shape[0], -1, HD)
    normed = heads * rms_scale(heads) * gain
    half_dim = HD // 2
    turned = jnp.concatenate([-normed[..., half_dim:], normed[..., :half_dim]], axis=-1)
    rotated = normed * cosine[:, None, :] + turned * sine[:, None, :]
    return rotated.reshape(projected.shape)

def rope_tables(places):
    half_dim = HD // 2
    ladder = jnp.arange(half_dim, dtype=jnp.float32)
    rates = jnp.exp(ladder * (-2.0 * math.log(ROPE_BASE) / HD))
    angles = places.astype(jnp.float32)[:, None] * rates[None, :]
    angles = jnp.concatenate([angles, angles], axis=1)
    return (jnp.cos(angles), jnp.sin(angles))

def token_starts(anchors, lengths):
    ends = jnp.cumsum(lengths)
    seq_starts = ends - lengths
    inside = seq_starts[None, :] <= anchors[:, None]
    return lax.optimization_barrier(jnp.max(jnp.where(inside, seq_starts[None, :], 0), axis=1)).astype(jnp.int32)

def attention(query, keys, values, anchors, starts):
    token_total = query.shape[0]
    block_rows = min(256, token_total)
    key_grid = keys.reshape(token_total, KVH, HD)
    value_grid = values.reshape(token_total, KVH, HD)

    def one_block(pieces):
        query_block, anchor_block, start_block = pieces
        query_grid = query_block.reshape(block_rows, KVH, QH // KVH, HD)
        scores = low_back(jnp.einsum('qkgd,tkd->qkgt', query_grid, key_grid, precision=PRECISE) * HD ** (-0.5))
        allowed = (anchors[None, :] <= anchor_block[:, None]) & (anchors[None, :] >= start_block[:, None])
        scores = jnp.where(allowed[:, None, None, :], scores, -1e+30)
        weights = low(jax.nn.softmax(scores, axis=-1))
        mixed_values = jnp.einsum('qkgt,tkd->qkgd', weights, value_grid, precision=PRECISE)
        return mixed_values.reshape(block_rows, QH * HD)
    blocks = lax.map(jax.checkpoint(one_block), (query.reshape(-1, block_rows, QH * HD), anchors.reshape(-1, block_rows), starts.reshape(-1, block_rows)))
    return blocks.reshape(token_total, QH * HD)

def forward(inputs, input_gain, w_query, w_key, w_value, query_gain, key_gain, w_out, hidden_gain, w_gate, w_up, w_down, anchors, starts, cosine, sine):
    normed = low(inputs * rms_scale(inputs) * input_gain)
    query_raw = low(low_back(jnp.dot(normed, w_query, precision=PRECISE)))
    key_raw = low(low_back(jnp.dot(normed, w_key, precision=PRECISE)))
    value_raw = low(low_back(jnp.dot(normed, w_value, precision=PRECISE)))
    query = low(norm_rope(query_raw, query_gain, cosine, sine))
    keys = low(norm_rope(key_raw, key_gain, cosine, sine))
    mixed = low(low_back(attention(query, keys, value_raw, anchors, starts)))
    middle = inputs + low_back(jnp.dot(mixed, w_out, precision=PRECISE))
    hidden_in = low(middle * rms_scale(middle) * hidden_gain)
    gate = low_back(jnp.dot(hidden_in, w_gate, precision=PRECISE))
    up_proj = low_back(jnp.dot(hidden_in, w_up, precision=PRECISE))
    activated = low(jax.nn.silu(gate) * up_proj)
    return middle + jnp.dot(activated, w_down, precision=PRECISE)

def reference(inputs, dealing, lengths, input_gain, w_query, w_key, w_value, query_gain, key_gain, w_out, hidden_gain, w_gate, w_up, w_down, cotangent):
    starts = token_starts(dealing, lengths)
    cosine, sine = rope_tables(dealing - starts)

    def layer(*arrays):
        return forward(*arrays, dealing, starts, cosine, sine)
    floats = tuple((array_item.astype(jnp.float32) for array_item in (inputs, input_gain, w_query, w_key, w_value, query_gain, key_gain, w_out, hidden_gain, w_gate, w_up, w_down)))
    result, pullback = jax.vjp(layer, *floats)
    gradients = pullback(cotangent.astype(jnp.float32))
    return (result.astype(jnp.bfloat16), gradients[0], gradients[1], gradients[2], gradients[3], gradients[4], gradients[5], gradients[6], gradients[7], gradients[8], gradients[9], gradients[10], gradients[11])
```

```python
import functools
import math

import jax
import jax.numpy as jnp
from jax import lax
from jax.experimental import pallas as pl
from jax.experimental.pallas import tpu as pltpu
from jax.sharding import PartitionSpec as P

QH = 16
KVH = 8
HD = 128
HALF = HD // 2
EPSILON = 1e-06
ROPE_BASE = 1000000.0
SCORE_SCALE = HD ** (-0.5)
EXP2_SCALE = SCORE_SCALE * math.log2(math.e)
CONTRACT_ROWS = (((0,), (0,)), ((), ()))
CONTRACT_COLS = (((1,), (1,)), ((), ()))
BF16 = jnp.bfloat16
F32 = jnp.float32
VMEM_LIMIT = 40 * 1024 * 1024


def dot(left, right):
    return jnp.dot(left, right, preferred_element_type=F32)


def row_outer(left, right):
    return lax.dot_general(left, right, CONTRACT_ROWS, preferred_element_type=F32)


def col_inner(left, right):
    return lax.dot_general(left, right, CONTRACT_COLS, preferred_element_type=F32)


def rms_scale(values):
    return lax.rsqrt(jnp.mean(values * values, axis=-1, keepdims=True) + EPSILON)


def norm_back(upstream, source, scale_rows, gain):
    scaled = upstream * gain
    return scale_rows * scaled - source * scale_rows**3 * jnp.mean(
        scaled * source, axis=-1, keepdims=True
    )


def core_swap(value):
    count = lax.axis_size("blk")
    return lax.ppermute(value, "blk", [(i, i ^ 1) for i in range(count)])


def chip_shift(value, steps=1, flip=0):
    count = lax.axis_size("blk")
    return lax.ppermute(
        value, "blk", [(i, ((i + 2 * steps) % count) ^ flip) for i in range(count)]
    )


def column_gather(value):
    chips = lax.axis_size("blk") // 2
    blocks = []
    for step in range(chips):
        blocks.append(jnp.concatenate([value, core_swap(value)], axis=0))
        if step < chips - 1:
            value = chip_shift(value)
    return blocks


def column_scatter(part_of):
    chips = lax.axis_size("blk") // 2
    arrived = None
    for step in list(range(1, chips)) + [0]:
        part = part_of(step)
        rows = part.shape[0] // 2
        total = part[:rows] + core_swap(part[rows:].astype(BF16)).astype(F32)
        if arrived is not None:
            total = total + arrived.astype(F32)
        if step:
            arrived = chip_shift(total.astype(BF16))
    return total


def head_bits():
    count = lax.axis_size("head")
    return [1 << i for i in range(count.bit_length() - 1)]


def head_flip(value, bit):
    count = lax.axis_size("head")
    return lax.ppermute(value, "head", [(i, i ^ bit) for i in range(count)])


def head_gather(value, backwards):
    pieces = {0: value}
    bits = head_bits()
    for bit in bits[::-1] if backwards else bits:
        for place in sorted(pieces):
            pieces[place ^ bit] = head_flip(pieces[place], bit)
    return [pieces[i] for i in range(len(pieces))]


def head_scatter(parts, backwards):
    pieces = dict(enumerate(parts))
    bits = head_bits()
    for bit in bits if backwards else bits[::-1]:
        for place in sorted(pieces):
            if place & bit:
                gone = head_flip(pieces.pop(place).astype(BF16), bit)
                pieces[place ^ bit] = pieces[place ^ bit] + gone.astype(F32)
    return pieces[0]


def sum_everywhere(value):
    for bit in head_bits():
        value = value + head_flip(value, bit)
    count = lax.axis_size("blk")
    for shift in range(count.bit_length() - 1):
        bit = 1 << shift
        value = value + lax.ppermute(value, "blk", [(i, i ^ bit) for i in range(count)])
    return value


def pick(stack, index):
    return lax.dynamic_index_in_dim(stack, index, 0, keepdims=False)


def token_starts(anchors, lengths):
    ends = jnp.cumsum(lengths)
    seq_starts = ends - lengths
    inside = seq_starts[None, :] <= anchors[:, None]
    return jnp.max(jnp.where(inside, seq_starts[None, :], 0), axis=1)


def rope_tables(places):
    ladder = jnp.arange(HALF, dtype=F32)
    rates = jnp.exp(ladder * (-2.0 * math.log(ROPE_BASE) / HD))
    angles = rates[:, None] * places.astype(F32)[None, :]
    return (jnp.cos(angles), jnp.sin(angles))


def rope_forward(raw, gain, cosine, sine):
    heads = raw.astype(F32)
    scale = lax.rsqrt(jnp.mean(heads * heads, axis=-2, keepdims=True) + EPSILON)
    normed = heads * scale * gain[:, None]
    low, high = normed[..., :HALF, :], normed[..., HALF:, :]
    return jnp.concatenate([low * cosine - high * sine, high * cosine + low * sine], axis=-2)


def rope_backward(raw, gain, cosine, sine, upstream):
    heads = raw.astype(F32)
    scale = lax.rsqrt(jnp.mean(heads * heads, axis=-2, keepdims=True) + EPSILON)
    low, high = upstream[..., :HALF, :], upstream[..., HALF:, :]
    turned = jnp.concatenate([low * cosine + high * sine, high * cosine - low * sine], axis=-2)
    gain_grad = jnp.sum(turned * heads * scale, axis=-1)
    scaled = turned * gain[:, None]
    back = scale * scaled - heads * scale**3 * jnp.mean(scaled * heads, axis=-2, keepdims=True)
    return back, gain_grad


def attend_kernel(chunk, q_ref, k_ref, v_ref, qpos_ref, qlow_ref, kpos_ref, out_ref, log_ref):
    rows = q_ref.shape[0]
    query = q_ref[...]
    qpos = qpos_ref[...]
    qlow = qlow_ref[...]

    def body(i, total):
        at = pl.multiple_of(i * chunk, chunk)
        scores = col_inner(query, k_ref[pl.ds(at, chunk), :])
        kpos = kpos_ref[:, pl.ds(at, chunk)]
        allowed = (kpos <= qpos) & (kpos >= qlow)
        lifted = jnp.where(allowed, jnp.exp2(scores * EXP2_SCALE), 0.0).astype(BF16)
        values = jnp.concatenate(
            [v_ref[pl.ds(at, chunk), :], jnp.ones((chunk, HD), BF16)], axis=1
        )
        return total + dot(lifted, values)

    total = lax.fori_loop(
        0, k_ref.shape[0] // chunk, body, jnp.zeros((rows, 2 * HD), F32), unroll=True
    )
    weight = total[:, HD:]
    out_ref[...] = total[:, :HD] / weight
    log_ref[...] = jnp.log2(weight).T[:8, :]


def attend(query, keys, values, qpos, qlow, kpos):
    rows, tokens = query.shape[0], keys.shape[0]
    own = qpos.shape[0]
    block = 256
    wrap = own // block
    cost = pl.CostEstimate(
        flops=4 * rows * tokens * HD, bytes_accessed=4 * tokens * HD, transcendentals=rows * tokens
    )
    return pl.pallas_call(
        functools.partial(attend_kernel, min(1024, tokens)),
        grid=(rows // block,),
        in_specs=[
            pl.BlockSpec((block, HD), lambda i: (i, 0)),
            pl.BlockSpec((tokens, HD), lambda i: (0, 0)),
            pl.BlockSpec((tokens, HD), lambda i: (0, 0)),
            pl.BlockSpec((block, 1), lambda i: (i % wrap, 0)),
            pl.BlockSpec((block, 1), lambda i: (i % wrap, 0)),
            pl.BlockSpec((1, tokens), lambda i: (0, 0)),
        ],
        out_specs=[
            pl.BlockSpec((block, HD), lambda i: (i, 0)),
            pl.BlockSpec((8, block), lambda i: (0, i)),
        ],
        out_shape=[
            jax.ShapeDtypeStruct((rows, HD), F32),
            jax.ShapeDtypeStruct((8, rows), F32),
        ],
        compiler_params=pltpu.CompilerParams(vmem_limit_bytes=VMEM_LIMIT),
        cost_estimate=cost,
    )(query, keys, values, qpos[:, None], qlow[:, None], kpos[None, :])


def attend_back_kernel(
    chunk, own, q_ref, g_ref, o_ref, log_ref, qpos_ref, qlow_ref, k_ref, v_ref, kpos_ref,
    dq_ref, dk_ref, dv_ref, delta_ref,
):
    rows = q_ref.shape[0]

    @pl.when(pl.program_id(0) == 0)
    def _():
        dq_ref[...] = jnp.zeros_like(dq_ref)
        for i in range(rows // chunk):
            at = pl.ds(i * chunk, chunk)
            product = g_ref[at, :].astype(F32) * o_ref[at, :]
            sums = jnp.sum(product.T, axis=0, keepdims=True)
            delta_ref[:, at] = jnp.broadcast_to(sums, (8, chunk))

    keys = k_ref[...]
    values = v_ref[...]
    kpos = kpos_ref[...]
    key_sum = jnp.zeros(keys.shape, F32)
    value_sum = jnp.zeros(keys.shape, F32)
    for i in range(rows // chunk):
        at = pl.ds(i * chunk, chunk)
        place = pl.ds((i * chunk) % own, chunk)
        query = q_ref[at, :]
        upstream = g_ref[at, :]
        scores = col_inner(keys, query)
        allowed = (kpos <= qpos_ref[:, place]) & (kpos >= qlow_ref[:, place])
        probs = jnp.where(allowed, jnp.exp2(scores * EXP2_SCALE - log_ref[0:1, at]), 0.0)
        prob_grad = col_inner(values, upstream)
        score_grad = (probs * (prob_grad - delta_ref[0:1, at])).astype(BF16)
        value_sum = value_sum + dot(probs.astype(BF16), upstream)
        key_sum = key_sum + dot(score_grad, query)
        dq_ref[at, :] += row_outer(score_grad, keys) * SCORE_SCALE
    dk_ref[...] = key_sum * SCORE_SCALE
    dv_ref[...] = value_sum


def attend_back(query, upstream, out, logs, qpos, qlow, keys, values, kpos):
    rows, tokens = query.shape[0], keys.shape[0]
    own = qpos.shape[0]
    block = 512
    cost = pl.CostEstimate(
        flops=10 * rows * tokens * HD, bytes_accessed=8 * tokens * HD, transcendentals=rows * tokens
    )
    whole = lambda i: (0, 0)
    return pl.pallas_call(
        functools.partial(attend_back_kernel, 512, own),
        grid=(tokens // block,),
        in_specs=[
            pl.BlockSpec((rows, HD), whole),
            pl.BlockSpec((rows, HD), whole),
            pl.BlockSpec((rows, HD), whole),
            pl.BlockSpec((8, rows), whole),
            pl.BlockSpec((1, own), whole),
            pl.BlockSpec((1, own), whole),
            pl.BlockSpec((block, HD), lambda i: (i, 0)),
            pl.BlockSpec((block, HD), lambda i: (i, 0)),
            pl.BlockSpec((block, 1), lambda i: (i, 0)),
        ],
        out_specs=[
            pl.BlockSpec((rows, HD), whole),
            pl.BlockSpec((block, HD), lambda i: (i, 0)),
            pl.BlockSpec((block, HD), lambda i: (i, 0)),
        ],
        out_shape=[
            jax.ShapeDtypeStruct((rows, HD), F32),
            jax.ShapeDtypeStruct((tokens, HD), F32),
            jax.ShapeDtypeStruct((tokens, HD), F32),
        ],
        scratch_shapes=[pltpu.VMEM((8, rows), F32)],
        compiler_params=pltpu.CompilerParams(vmem_limit_bytes=VMEM_LIMIT),
        cost_estimate=cost,
    )(query, upstream, out, logs, qpos[None, :], qlow[None, :], keys, values, kpos[:, None])


def local(
    inputs,
    dealing,
    lengths,
    input_gain,
    w_query,
    w_key,
    w_value,
    query_gain,
    key_gain,
    w_out,
    hidden_gain,
    w_gate,
    w_up,
    w_down,
    cotangent,
):
    heads, blks = lax.axis_size("head"), lax.axis_size("blk")
    head, blk = lax.axis_index("head"), lax.axis_index("blk")
    shards = heads * blks
    chips = blks // 2
    chip, core = blk // 2, blk % 2
    shard = head * blks + blk
    rows, width = inputs.shape
    column = rows * blks
    pair = 2 * rows
    per_device = QH // blks
    query_rows, key_rows = w_query.shape[1], w_key.shape[1]
    qkv_rows = query_rows + 2 * key_rows
    in_pair = shards // KVH == heads and blks == 2 * heads

    gains = jnp.zeros((2 * width + 2 * HD,), F32)
    hidden_part = jnp.where(head == 0, hidden_gain.astype(F32), 0.0)
    for at, part in (
        (shard * input_gain.shape[0], input_gain),
        (width + blk * hidden_gain.shape[0], hidden_part),
        (2 * width + shard * query_gain.shape[0], query_gain),
        (2 * width + HD + shard * key_gain.shape[0], key_gain),
    ):
        gains = lax.dynamic_update_slice(gains, part.astype(F32), (at,))
    gains = sum_everywhere(gains.reshape(-1, 128)).reshape(-1)
    input_norm = gains[:width]
    hidden_norm = gains[width : 2 * width]
    query_norm = gains[2 * width : 2 * width + HD]
    key_norm = gains[2 * width + HD :]

    query_pieces = head_gather(w_query.T, False)
    key_value_pieces = head_gather(jnp.concatenate([w_key.T, w_value.T], axis=0), True)
    qkv_weights = jnp.concatenate(
        [part for pieces in zip(query_pieces, key_value_pieces) for part in pieces], axis=0
    )
    full_out = lax.all_gather(w_out, ("head", "blk"), axis=0, tiled=True)
    gate_weights = jnp.concatenate(head_gather(w_gate.T, False), axis=0)
    up_weights = jnp.concatenate(head_gather(w_up.T, True), axis=0)
    half_down = w_down.shape[0] // 2
    down_low = head_gather(w_down[:half_down], False)
    down_high = head_gather(w_down[half_down:], True)
    down_weights = jnp.concatenate(
        [part for pieces in zip(down_low, down_high) for part in pieces], axis=0
    )

    deals = dealing.reshape(blks, heads, rows)
    deals = jnp.concatenate(
        [
            lax.dynamic_index_in_dim(deals, ((chip - step) % chips) * 2 + (core ^ flip), 0)
            for step in range(chips)
            for flip in range(2)
        ],
        axis=0,
    )
    key_places = jnp.concatenate(
        [
            lax.dynamic_index_in_dim(deals, head ^ place, 1, keepdims=False).reshape(-1)
            for place in range(heads)
        ]
    )
    query_places = key_places[:column]
    query_starts = token_starts(query_places, lengths)
    cosine, sine = rope_tables(query_places - query_starts)

    token_blocks = column_gather(inputs)
    normed_blocks = []
    raw_blocks = []
    for block in token_blocks:
        values = block.astype(F32)
        normed = (values * rms_scale(values) * input_norm).astype(BF16)
        normed_blocks.append(normed)
        raw_blocks.append(col_inner(qkv_weights, normed).astype(BF16))
    normed_column = jnp.concatenate(normed_blocks, axis=0)
    raw = jnp.concatenate(raw_blocks, axis=1).reshape(heads, qkv_rows, column)

    def from_member(piece, flip):
        piece = lax.ppermute(piece, "blk", [(i, i ^ flip) for i in range(blks)])
        if flip & 1:
            cuts = [piece[..., i * rows : (i + 1) * rows] for i in range(blks)]
            piece = jnp.concatenate([cuts[i ^ 1] for i in range(blks)], axis=-1)
        if flip & 2:
            later = jnp.concatenate([piece[..., pair:], piece[..., :pair]], axis=-1)
            sooner = jnp.concatenate([piece[..., -pair:], piece[..., :-pair]], axis=-1)
            piece = jnp.where(chip % 2 == 0, later, sooner)
        return piece

    if in_pair:
        member = blk % heads
        mine = pick(raw, head ^ member)
        arrived = jnp.stack(
            [mine]
            + [
                from_member(pick(raw, head ^ member ^ flip), flip)
                for flip in range(1, heads)
            ]
        )
        quarters = jnp.stack([pick(arrived, member ^ place) for place in range(heads)])
        query_raw = quarters[:, :query_rows].reshape(per_device, HD, column)
        key_raw = quarters[:, query_rows : query_rows + key_rows].reshape(HD, column)
        value_raw = quarters[:, query_rows + key_rows :].reshape(HD, column)
        unit_blk = [(unit % 2) * heads + unit // 2 for unit in range(blks)]
    else:
        by_head = jnp.stack([pick(raw, head ^ place) for place in range(heads)])
        every = jnp.swapaxes(lax.all_gather(by_head, "blk", axis=0), 0, 1)
        every = every.reshape(shards, qkv_rows, column)
        query_all = every[:, :query_rows].reshape(QH, HD, column)
        key_all = every[:, query_rows : query_rows + key_rows].reshape(KVH, HD, column)
        value_all = every[:, query_rows + key_rows :].reshape(KVH, HD, column)
        query_raw = lax.dynamic_slice_in_dim(query_all, blk * per_device, per_device, 0)
        key_raw = pick(key_all, blk * KVH // blks)
        value_raw = pick(value_all, blk * KVH // blks)
        unit_blk = list(range(blks))

    query = rope_forward(query_raw, query_norm, cosine, sine).astype(BF16)
    keys = rope_forward(key_raw, key_norm, cosine, sine).astype(BF16)
    query = jnp.swapaxes(query, 1, 2).reshape(per_device * column, HD)
    all_keys = jnp.concatenate(head_gather(keys.T, False), axis=0)
    all_values = jnp.concatenate(head_gather(value_raw.T, True), axis=0)

    heads_out, logs = attend(query, all_keys, all_values, query_places, query_starts, key_places)

    def head_blocks(step, flip):
        block = heads_out.reshape(per_device, blks, rows, HD)[:, 2 * step + flip]
        return jnp.swapaxes(block, 0, 1).reshape(rows, per_device * HD).astype(BF16)

    mixed_parts = jnp.stack(
        [
            head_blocks(step, flip)
            if step + flip == 0
            else chip_shift(head_blocks(step, flip), -step, flip)
            for step in range(chips)
            for flip in range(2)
        ]
    )
    mixed = jnp.concatenate(
        [
            pick(mixed_parts, ((source // 2 - chip) % chips) * 2 + ((source % 2) ^ core))
            for source in unit_blk
        ],
        axis=1,
    )
    token_values = inputs.astype(F32)
    middle = token_values + dot(mixed, full_out)
    scale_two = rms_scale(middle)
    hidden_in = (middle * scale_two * hidden_norm).astype(BF16)

    own_cotangent = lax.dynamic_slice_in_dim(cotangent, head * rows, rows, 0)
    cotangent_blocks = column_gather(own_cotangent)
    act_grads = [col_inner(block, down_weights) for block in cotangent_blocks]
    hidden_blocks = column_gather(hidden_in)
    activated_blocks, gate_grads, up_grads = [], [], []
    for block, act_grad in zip(hidden_blocks, act_grads):
        gate = col_inner(block, gate_weights)
        up_proj = col_inner(block, up_weights)
        sigmoid_gate = jax.nn.sigmoid(gate)
        silu_gate = gate * sigmoid_gate
        activated_blocks.append((silu_gate * up_proj).astype(BF16))
        gate_grads.append(
            (act_grad * up_proj * sigmoid_gate * (1.0 + gate * (1.0 - sigmoid_gate))).astype(BF16)
        )
        up_grads.append((act_grad * silu_gate).astype(BF16))
    hidden_grad = column_scatter(
        lambda step: dot(gate_grads[step], gate_weights) + dot(up_grads[step], up_weights)
    )
    feed_out = column_scatter(lambda step: dot(activated_blocks[step], down_weights))
    layer_out = (middle + feed_out).astype(BF16)

    hidden_gain_grad = jnp.sum(hidden_grad * middle * scale_two, axis=0)
    middle_grad = own_cotangent.astype(F32) + norm_back(hidden_grad, middle, scale_two, hidden_norm)
    branch_grad = middle_grad.astype(BF16)
    grad_out = lax.psum_scatter(
        row_outer(mixed, branch_grad).astype(BF16), ("head", "blk"), scatter_dimension=0, tiled=True
    ).astype(F32)
    mixed_grad = col_inner(branch_grad, full_out).astype(BF16)
    mixed_grad = jnp.swapaxes(mixed_grad.reshape(rows, blks, per_device * HD), 0, 1)
    blk_unit = [unit_blk.index(place) for place in range(blks)]
    unit_of = jnp.asarray(blk_unit, jnp.int32)

    def tokens_to_heads(step, flip):
        target = ((chip + step) % chips) * 2 + (core ^ flip)
        part = pick(mixed_grad, pick(unit_of, target))
        return part if step + flip == 0 else chip_shift(part, step, flip)

    upstream = jnp.concatenate(
        [tokens_to_heads(step, flip) for step in range(chips) for flip in range(2)], axis=0
    )
    upstream = jnp.swapaxes(upstream.reshape(column, per_device, HD), 0, 1)
    query_grad, key_grads, value_grads = attend_back(
        query,
        upstream.reshape(per_device * column, HD),
        heads_out,
        logs,
        query_places,
        query_starts,
        all_keys,
        all_values,
        key_places,
    )

    hidden_column = jnp.concatenate(hidden_blocks, axis=0)
    cotangent_column = jnp.concatenate(cotangent_blocks, axis=0)
    grad_gate = row_outer(jnp.concatenate(gate_grads, axis=0), hidden_column)
    grad_up = row_outer(jnp.concatenate(up_grads, axis=0), hidden_column)
    grad_down = row_outer(jnp.concatenate(activated_blocks, axis=0), cotangent_column)
    grad_gate = head_scatter(grad_gate.reshape((heads, -1, width)), False).T
    grad_up = head_scatter(grad_up.reshape((heads, -1, width)), True).T
    grad_down = grad_down.reshape((heads, 2, half_down, width))
    grad_down = jnp.concatenate(
        [head_scatter(grad_down[:, 0], False), head_scatter(grad_down[:, 1], True)], axis=0
    )

    key_grad = head_scatter(key_grads.reshape(heads, column, HD), False).T
    value_grad = head_scatter(value_grads.reshape(heads, column, HD), True).T
    query_grad = jnp.swapaxes(query_grad.reshape(per_device, column, HD), 1, 2)
    query_raw_grad, query_gain_grad = rope_backward(
        query_raw, query_norm, cosine, sine, query_grad
    )
    key_raw_grad, key_gain_grad = rope_backward(key_raw, key_norm, cosine, sine, key_grad)
    query_raw_grad = query_raw_grad.astype(BF16)
    key_raw_grad = key_raw_grad.astype(BF16)
    value_raw_grad = value_grad.astype(BF16)
    if in_pair:
        quarters = jnp.concatenate(
            [
                query_raw_grad.reshape(heads, query_rows, column),
                key_raw_grad.reshape(heads, key_rows, column),
                value_raw_grad.reshape(heads, key_rows, column),
            ],
            axis=1,
        )
        arrived = jnp.stack(
            [pick(quarters, member)]
            + [from_member(pick(quarters, member ^ flip), flip) for flip in range(1, heads)]
        )
        raw_grad = jnp.concatenate(
            [pick(arrived, head ^ member ^ place) for place in range(heads)], axis=0
        )
    else:
        def spread(part, count, index):
            empty = jnp.zeros((count,) + part.shape[1:], BF16)
            return lax.dynamic_update_slice_in_dim(empty, part, index, 0)

        every = jnp.concatenate(
            [
                spread(query_raw_grad, QH, blk * per_device).reshape(shards, query_rows, column),
                spread(key_raw_grad[None], KVH, blk * KVH // blks).reshape(
                    shards, key_rows, column
                ),
                spread(value_raw_grad[None], KVH, blk * KVH // blks).reshape(
                    shards, key_rows, column
                ),
            ],
            axis=1,
        ).reshape(heads, blks, qkv_rows, column)
        by_head = lax.psum_scatter(
            jnp.swapaxes(every, 0, 1), "blk", scatter_dimension=0, tiled=False
        )
        raw_grad = jnp.concatenate(
            [pick(by_head, head ^ place) for place in range(heads)], axis=0
        )

    qkv_grad = dot(raw_grad, normed_column)
    input_gain_grad = jnp.sum(qkv_grad * qkv_weights.astype(F32), axis=0) / input_norm
    normed_grad = column_scatter(
        lambda step: row_outer(raw_grad[:, step * pair : (step + 1) * pair], qkv_weights)
    )
    grad_input = middle_grad + norm_back(
        normed_grad, token_values, rms_scale(token_values), input_norm
    )
    qkv_grad = qkv_grad.reshape(heads, qkv_rows, width)
    grad_query = head_scatter(qkv_grad[:, :query_rows], False)
    grad_key_value = head_scatter(qkv_grad[:, query_rows:], True)

    sums = jnp.concatenate(
        [
            input_gain_grad,
            hidden_gain_grad,
            jnp.sum(query_gain_grad, axis=0),
            key_gain_grad,
        ]
    )
    sums = sum_everywhere(sums.reshape(-1, 128)).reshape(-1)

    def own_part(at, size):
        return lax.dynamic_slice_in_dim(sums, at, size)

    return (
        layer_out,
        grad_input,
        own_part(shard * input_gain.shape[0], input_gain.shape[0]),
        grad_query.T,
        grad_key_value[:key_rows].T,
        grad_key_value[key_rows:].T,
        own_part(2 * width + shard * query_gain.shape[0], query_gain.shape[0]),
        own_part(2 * width + HD + shard * key_gain.shape[0], key_gain.shape[0]),
        grad_out,
        own_part(width + blk * hidden_gain.shape[0], hidden_gain.shape[0]),
        grad_gate,
        grad_up,
        grad_down,
    )


def solution(mesh):
    return jax.shard_map(
        local,
        mesh=mesh,
        in_specs=(
            P(("blk", "head"), None),
            P(),
            P(),
            P(("head", "blk")),
            P(None, ("head", "blk")),
            P(None, ("head", "blk")),
            P(None, ("head", "blk")),
            P(("head", "blk")),
            P(("head", "blk")),
            P(("head", "blk"), None),
            P("blk"),
            P(None, ("head", "blk")),
            P(None, ("head", "blk")),
            P(("head", "blk"), None),
            P("blk", None),
        ),
        out_specs=(
            P(("blk", "head"), None),
            P(("blk", "head"), None),
            P(("head", "blk")),
            P(None, ("head", "blk")),
            P(None, ("head", "blk")),
            P(None, ("head", "blk")),
            P(("head", "blk")),
            P(("head", "blk")),
            P(("head", "blk"), None),
            P("blk"),
            P(None, ("head", "blk")),
            P(None, ("head", "blk")),
            P(("head", "blk"), None),
        ),
        check_vma=False,
    )
```

```python
import functools
import math

import jax
import jax.numpy as jnp
import numpy as np
from jax import lax
from jax.experimental import pallas as pl
from jax.experimental.pallas import tpu as pltpu
from jax.sharding import PartitionSpec as P

QH = 16
KVH = 8
HD = 128
HALF = HD // 2
EPSILON = 1e-06
ROPE_BASE = 1000000.0
SCORE_SCALE = HD ** (-0.5)
EXP2_SCALE = SCORE_SCALE * math.log2(math.e)
CONTRACT_ROWS = (((0,), (0,)), ((), ()))
CONTRACT_COLS = (((1,), (1,)), ((), ()))
BF16 = jnp.bfloat16
F32 = jnp.float32
VMEM_LIMIT = 40 * 1024 * 1024


def dot(left, right):
    return jnp.dot(left, right, preferred_element_type=F32)


def row_outer(left, right):
    return lax.dot_general(left, right, CONTRACT_ROWS, preferred_element_type=F32)


def col_inner(left, right):
    return lax.dot_general(left, right, CONTRACT_COLS, preferred_element_type=F32)


def rms_scale(values):
    return lax.rsqrt(jnp.mean(values * values, axis=-1, keepdims=True) + EPSILON)


def norm_back(upstream, source, scale_rows, gain):
    scaled = upstream * gain
    return scale_rows * scaled - source * scale_rows**3 * jnp.mean(
        scaled * source, axis=-1, keepdims=True
    )


def head_bits():
    count = lax.axis_size("head")
    return [1 << i for i in range(count.bit_length() - 1)]


def head_move(bit):
    count = lax.axis_size("head")
    return ("head", [(i, i ^ bit) for i in range(count)], bit)


def blk_move(steps, flip, link):
    count = lax.axis_size("blk")
    return ("blk", [(i, ((i + 2 * steps) % count) ^ flip) for i in range(count)], link)


def swap_move():
    return blk_move(0, 1, None)


def ring_move():
    return blk_move(1, 0, "z")


def member_move(flip):
    count = lax.axis_size("blk")
    return ("blk", [(i, i ^ flip) for i in range(count)], "z" if flip > 1 else None)


class Job:
    def __init__(self, steps):
        self.steps = steps
        self.wanted = None
        self.result = None
        self.advance(None)

    def advance(self, got):
        try:
            self.wanted = self.steps.send(got)
        except StopIteration as end:
            self.wanted = None
            self.result = end.value


class Wire:
    def __init__(self, token):
        self.token = token
        self.jobs = []

    def add(self, steps):
        job = Job(steps)
        self.jobs.append(job)
        return job

    def tie(self, *arrays):
        *arrays, self.token = lax.optimization_barrier(arrays + (self.token,))
        return arrays

    def phase(self, items, behind=False, riders=()):
        items = list(items)
        count = len(items)
        taken = []
        for job in (self.jobs if behind else []) + list(riders):
            if job.wanted is not None:
                taken.append((job, len(items), len(items) + len(job.wanted)))
                items.extend(job.wanted)
        if not items:
            return []
        values = self.tie(*[value for value, move in items])
        outs = self.tie(
            *[lax.ppermute(value, move[0], move[1]) for value, (same, move) in zip(values, items)]
        )
        for job, start, end in taken:
            job.advance(outs[start:end])
        self.jobs = [job for job in self.jobs if job.wanted is not None]
        return outs[:count]

    def drive(self, steps, hooks=(), riders=()):
        job = Job(steps)
        riders = list(riders)
        hooks = list(hooks)
        while job.wanted is not None or any(rider.wanted is not None for rider in riders):
            got = self.phase(job.wanted or [], riders=riders)
            if job.wanted is not None:
                job.advance(got)
            if hooks:
                riders.extend(hooks.pop(0)() or [])
        return job.result


def column_gather(value, blocks=None):
    chips = lax.axis_size("blk") // 2
    blocks = [] if blocks is None else blocks
    for step in range(chips):
        items = [(value, swap_move())]
        if step < chips - 1:
            items.append((value, ring_move()))
        got = yield items
        blocks.append([value, got[0]])
        value = got[-1]
    return blocks


def join_blocks(blocks):
    return [jnp.concatenate(block, axis=0) for block in blocks]


def column_scatter(part_of, apart=False):
    chips = lax.axis_size("blk") // 2
    order = list(range(1, chips)) + [0]

    def halves(step):
        part = part_of(step)
        rows = part.shape[0] // 2
        return part[:rows], part[rows:]

    own, other = halves(order[0])
    got = yield [(other.astype(BF16), swap_move())]
    total = own + got[0].astype(F32)
    for step in order[1:]:
        if apart:
            got = yield [(total.astype(BF16), ring_move())]
            own, other = halves(step)
            got = got + (yield [(other.astype(BF16), swap_move())])
            apart = False
        else:
            own, other = halves(step)
            got = yield [(total.astype(BF16), ring_move()), (other.astype(BF16), swap_move())]
        total = own + got[1].astype(F32) + got[0].astype(F32)
    return total


def plane_steps(backwards):
    bits = head_bits()
    order = bits[::-1] if backwards else bits
    steps = []
    for weight in range(1, len(bits) + 1):
        step = []
        for place in range(1 << len(bits)):
            if bin(place).count("1") == weight:
                last = [bit for bit in order if place & bit][-1]
                step.append((place, place ^ last, last))
        steps.append(step)
    return steps


def plane_gather(value, backwards):
    pieces = {0: value}
    for step in plane_steps(backwards):
        got = yield [(pieces[source], head_move(bit)) for place, source, bit in step]
        for (place, source, bit), piece in zip(step, got):
            pieces[place] = piece
    return [pieces[i] for i in range(len(pieces))]


def plane_scatter(parts, backwards):
    pieces = list(parts)
    for step in plane_steps(backwards)[::-1]:
        got = yield [(pieces[place].astype(BF16), head_move(bit)) for place, source, bit in step]
        for (place, source, bit), piece in zip(step, got):
            pieces[source] = pieces[source] + piece.astype(F32)
    return pieces[0]


def sum_everywhere(value):
    chips = lax.axis_size("blk") // 2
    for moves in (
        [head_move(flip) for flip in range(1, lax.axis_size("head"))],
        [swap_move()],
        [blk_move(steps, 0, None) for steps in range(1, chips)],
    ):
        got = yield [(value, move) for move in moves]
        for part in got:
            value = value + part
    return value


def pick(stack, index):
    return lax.dynamic_index_in_dim(stack, index, 0, keepdims=False)


def token_starts(anchors, lengths):
    ends = jnp.cumsum(lengths)
    seq_starts = ends - lengths
    inside = seq_starts[None, :] <= anchors[:, None]
    return jnp.max(jnp.where(inside, seq_starts[None, :], 0), axis=1)


def rope_tables(places):
    ladder = jnp.arange(HALF, dtype=F32)
    rates = jnp.exp(ladder * (-2.0 * math.log(ROPE_BASE) / HD))
    angles = rates[:, None] * places.astype(F32)[None, :]
    return (jnp.cos(angles), jnp.sin(angles))


def rope_forward(raw, gain, cosine, sine):
    heads = raw.astype(F32)
    scale = lax.rsqrt(jnp.mean(heads * heads, axis=-2, keepdims=True) + EPSILON)
    normed = heads * scale * gain[:, None]
    low, high = normed[..., :HALF, :], normed[..., HALF:, :]
    return jnp.concatenate([low * cosine - high * sine, high * cosine + low * sine], axis=-2)


def rope_backward(raw, gain, cosine, sine, upstream):
    heads = raw.astype(F32)
    scale = lax.rsqrt(jnp.mean(heads * heads, axis=-2, keepdims=True) + EPSILON)
    low, high = upstream[..., :HALF, :], upstream[..., HALF:, :]
    turned = jnp.concatenate([low * cosine + high * sine, high * cosine - low * sine], axis=-2)
    gain_grad = jnp.sum(turned * heads * scale, axis=-1)
    scaled = turned * gain[:, None]
    back = scale * scaled - heads * scale**3 * jnp.mean(scaled * heads, axis=-2, keepdims=True)
    return back, gain_grad


def small_call(kernel, outs, scalars, arrays, scratch=()):
    vmem = pl.BlockSpec(memory_space=pltpu.VMEM)
    return pl.pallas_call(
        kernel,
        in_specs=[pl.BlockSpec(memory_space=pltpu.SMEM)] + [vmem] * len(arrays),
        out_specs=[vmem] * len(outs),
        out_shape=[jax.ShapeDtypeStruct(shape, dtype) for shape, dtype in outs],
        scratch_shapes=[pltpu.VMEM(shape, dtype) for shape, dtype in scratch],
        compiler_params=pltpu.CompilerParams(vmem_limit_bytes=VMEM_LIMIT),
        cost_estimate=pl.CostEstimate(
            flops=0,
            bytes_accessed=3 * sum(array.size * array.dtype.itemsize for array in arrays),
            transcendentals=0,
        ),
    )(scalars, *arrays)


def table_kernel(blocks, sequences, index_ref, deal_ref, rate_ref, key_ref, start_ref, cos_ref, sin_ref):
    heads, column = key_ref.shape
    rows = column // blocks
    for place in range(heads):
        for block in range(blocks):
            row = deal_ref[pl.ds(index_ref[place * blocks + block], 1), :]
            key_ref[place : place + 1, block * rows : (block + 1) * rows] = row
    own = key_ref[0:1, :]
    starts = jnp.zeros_like(own)
    first = jnp.int32(0)
    for sequence in range(sequences - 1):
        first = first + index_ref[heads * blocks + sequence]
        starts = jnp.where(own >= first, first, starts)
    start_ref[...] = starts
    angles = rate_ref[:, :1] * (own - starts).astype(F32)
    cos_ref[...] = jnp.cos(angles)
    sin_ref[...] = jnp.sin(angles)


def tables(index, lengths, deals, column, heads):
    rates = np.exp(
        np.arange(HALF, dtype=np.float32) * np.float32(-2.0 * math.log(ROPE_BASE) / HD)
    ).astype(np.float32)
    return small_call(
        functools.partial(table_kernel, column // deals.shape[1], lengths.shape[0]),
        [
            ((heads, column), jnp.int32),
            ((1, column), jnp.int32),
            ((HALF, column), F32),
            ((HALF, column), F32),
        ],
        jnp.concatenate([index, lengths]),
        [deals, jnp.asarray(np.broadcast_to(rates[:, None], (HALF, 128)))],
    )


def put_in_order(out_ref, scalar_ref, pieces, rows, finish):
    base = scalar_ref[0]
    for flip, piece in enumerate(pieces):
        value = piece[...]
        column = value.shape[1]
        if flip & 1:
            cuts = [value[:, i * rows : (i + 1) * rows] for i in range(column // rows)]
            value = jnp.concatenate([cuts[i ^ 1] for i in range(column // rows)], axis=1)
        at = pl.ds(base ^ flip, 1)
        if flip & 2:
            pair = 2 * rows

            @pl.when(scalar_ref[1] == 0)
            def _(at=at, value=value, pair=pair):
                out_ref[at] = jnp.concatenate([value[:, pair:], value[:, :pair]], axis=1)[None]

            @pl.when(scalar_ref[1] != 0)
            def _(at=at, value=value, pair=pair):
                out_ref[at] = jnp.concatenate([value[:, -pair:], value[:, :-pair]], axis=1)[None]

        else:
            out_ref[at] = value[None]
    finish()


def join_members(base, odd, pieces, rows):
    count = len(pieces)

    def kernel(scalar_ref, *refs):
        put_in_order(refs[count], scalar_ref, refs[:count], rows, lambda: None)

    return small_call(
        kernel,
        [((count,) + pieces[0].shape, BF16)],
        jnp.stack([base, odd]).astype(jnp.int32),
        pieces,
    )[0]


def split_blocks(base, blocks, count):
    size = blocks[0].shape[0] // count
    width = blocks[0].shape[1]

    def kernel(scalar_ref, *refs):
        for flip in range(count):
            start = pl.multiple_of((scalar_ref[0] ^ flip) * size, size)
            for index in range(len(blocks)):
                refs[len(blocks) + flip][:, index * width : (index + 1) * width] = refs[index][
                    pl.ds(start, size), :
                ]

    return small_call(
        kernel,
        [((size, width * len(blocks)), BF16)] * count,
        base.reshape(1).astype(jnp.int32),
        blocks,
    )


def rope_kernel(rows, query_rows, key_rows, scalar_ref, *refs):
    pieces = refs[:-6]
    cos_ref, sin_ref, gain_ref, raw_ref, query_ref, pair_ref = refs[-6:]
    count, column = len(pieces), cos_ref.shape[1]
    put_in_order(raw_ref, scalar_ref, pieces, rows, lambda: None)
    cosine, sine = cos_ref[...], sin_ref[...]

    def rotate(parts, gain):
        heads = jnp.concatenate(parts, axis=0).astype(F32)
        scale = lax.rsqrt(jnp.mean(heads * heads, axis=0, keepdims=True) + EPSILON)
        normed = heads * scale * gain
        low, high = normed[:HALF], normed[HALF:]
        turned = jnp.concatenate([low * cosine - high * sine, high * cosine + low * sine], axis=0)
        return turned.T.astype(BF16)

    per_head = HD // query_rows
    for head in range(count // per_head):
        parts = [raw_ref[head * per_head + i, :query_rows, :] for i in range(per_head)]
        query_ref[head * column : (head + 1) * column, :] = rotate(parts, gain_ref[:, 0:1])
    parts = [raw_ref[i, query_rows : query_rows + key_rows, :] for i in range(count)]
    pair_ref[:, :HD] = rotate(parts, gain_ref[:, 1:2])
    parts = [raw_ref[i, query_rows + key_rows :, :] for i in range(count)]
    pair_ref[:, HD:] = jnp.concatenate(parts, axis=0).astype(F32).T.astype(BF16)


def rope_members(base, odd, pieces, cosine, sine, gains, rows, query_rows, key_rows):
    count, column = len(pieces), cosine.shape[1]
    return small_call(
        functools.partial(rope_kernel, rows, query_rows, key_rows),
        [
            ((count,) + pieces[0].shape, BF16),
            ((count * query_rows // HD * column, HD), BF16),
            ((column, 2 * HD), BF16),
        ],
        jnp.stack([base, odd]).astype(jnp.int32),
        list(pieces) + [cosine, sine, gains],
    )


def mixed_kernel(scalar_ref, in_ref, *refs):
    outs, parts_ref = refs[:-1], refs[-1]
    count, size, column = parts_ref.shape
    for head in range(in_ref.shape[0] // column):
        part = in_ref[head * column : (head + 1) * column, :].T.astype(BF16)
        per_head = HD // size
        for i in range(per_head):
            parts_ref[head * per_head + i] = part[i * size : (i + 1) * size]
    for flip, out_ref in enumerate(outs):
        out_ref[...] = parts_ref[scalar_ref[0] ^ flip]


def mixed_members(base, heads_out, count, column):
    size = heads_out.shape[0] // column * HD // count
    return small_call(
        mixed_kernel,
        [((size, column), BF16)] * count,
        base.reshape(1).astype(jnp.int32),
        [heads_out],
        [((count, size, column), BF16)],
    )


def upstream_members(base, odd, pieces, rows):
    count = len(pieces)
    size, column = pieces[0].shape
    per_head = HD // size

    def kernel(scalar_ref, *refs):
        out_ref, parts_ref = refs[count:]
        put_in_order(parts_ref, scalar_ref, refs[:count], rows, lambda: None)
        for head in range(count // per_head):
            parts = [parts_ref[head * per_head + i] for i in range(per_head)]
            out_ref[head * column : (head + 1) * column, :] = (
                jnp.concatenate(parts, axis=0).astype(F32).T.astype(BF16)
            )

    return small_call(
        kernel,
        [((count // per_head * column, HD), BF16)],
        jnp.stack([base, odd]).astype(jnp.int32),
        pieces,
        [((count, size, column), BF16)],
    )[0]


def rope_back_kernel(query_rows, key_rows, count, scalar_ref, *refs):
    raw_ref, dq_ref, cos_ref, sin_ref, gain_ref, dk_ref, dv_ref = refs[:7]
    more = refs[7 : -2 - count]
    outs, gain_out, parts_ref = refs[-2 - count : -2], refs[-2], refs[-1]
    column = cos_ref.shape[1]
    cosine, sine = cos_ref[...], sin_ref[...]

    def back(parts, gain, upstream):
        heads = jnp.concatenate(parts, axis=0).astype(F32)
        scale = lax.rsqrt(jnp.mean(heads * heads, axis=0, keepdims=True) + EPSILON)
        low, high = upstream[:HALF], upstream[HALF:]
        turned = jnp.concatenate([low * cosine + high * sine, high * cosine - low * sine], axis=0)
        gain_grad = jnp.sum(turned * heads * scale, axis=1, keepdims=True)
        scaled = turned * gain
        mean = jnp.mean(scaled * heads, axis=0, keepdims=True)
        return (scale * scaled - heads * (scale * scale * scale * mean)).astype(BF16), gain_grad

    per_head = HD // query_rows
    total = jnp.zeros((HD, 1), F32)
    for head in range(count // per_head):
        at = [head * per_head + i for i in range(per_head)]
        grad, gain_grad = back(
            [raw_ref[i, :query_rows, :] for i in at],
            gain_ref[:, 0:1],
            dq_ref[head * column : (head + 1) * column, :].T,
        )
        total = total + gain_grad
        for place, i in enumerate(at):
            parts_ref[i, :query_rows, :] = grad[place * query_rows : (place + 1) * query_rows]
    gain_out[:, 0:1] = total
    key_grad, value_grad = dk_ref[...], dv_ref[...]
    for ref in more:
        key_grad = key_grad + ref[:, :HD].astype(F32)
        value_grad = value_grad + ref[:, HD:].astype(F32)
    grad, gain_grad = back(
        [raw_ref[i, query_rows : query_rows + key_rows, :] for i in range(count)],
        gain_ref[:, 1:2],
        key_grad.T,
    )
    gain_out[:, 1:2] = gain_grad
    value_grad = value_grad.T.astype(BF16)
    for i in range(count):
        cut = slice(i * key_rows, (i + 1) * key_rows)
        parts_ref[i, query_rows : query_rows + key_rows, :] = grad[cut]
        parts_ref[i, query_rows + key_rows :, :] = value_grad[cut]
    for flip, out_ref in enumerate(outs):
        out_ref[...] = parts_ref[scalar_ref[0] ^ flip]


def rope_back_members(base, raw, dq, cosine, sine, gains, dk, dv, more, query_rows, key_rows):
    count, size, column = raw.shape
    return small_call(
        functools.partial(rope_back_kernel, query_rows, key_rows, count),
        [((size, column), BF16)] * count + [((HD, 2), F32)],
        base.reshape(1).astype(jnp.int32),
        [raw, dq, cosine, sine, gains, dk, dv] + list(more),
        [((count, size, column), BF16)],
    )


def attend_kernel(first, last, *refs):
    refs = list(refs)
    q_ref, k_ref, v_ref, qpos_ref, qlow_ref, kpos_ref = refs[:6]
    outs = refs[6:] if first else refs[7:]
    kpos = kpos_ref[...]
    scores = col_inner(q_ref[...], k_ref[...])
    rows = q_ref.shape[0]
    qpos = jnp.broadcast_to(qpos_ref[...], (8, rows)).T[:, :1]
    qlow = jnp.broadcast_to(qlow_ref[...], (8, rows)).T[:, :1]
    allowed = (kpos <= qpos) & (kpos >= qlow)
    lifted = jnp.where(allowed, jnp.exp2(scores * EXP2_SCALE), 0.0).astype(BF16)
    values = jnp.concatenate([v_ref[...], jnp.ones(v_ref.shape, BF16)], axis=1)
    total = dot(lifted, values)
    if not first:
        total = total + refs[6][...]
    if last:
        weight = total[:, HD:]
        outs[0][...] = total[:, :HD] / weight
        outs[1][...] = jnp.log2(weight).T[:8, :]
    else:
        outs[0][...] = total


def attend(query, keys, values, qpos, qlow, kpos, total, last):
    rows, tokens = query.shape[0], keys.shape[0]
    value_at = values.shape[1] // HD - 1
    own = qpos.shape[1]
    block = 256
    wrap = own // block
    first = total is None
    cost = pl.CostEstimate(
        flops=20 * rows * tokens * HD, bytes_accessed=4 * tokens * HD, transcendentals=rows * tokens
    )
    whole = lambda i: (0, 0)
    return pl.pallas_call(
        functools.partial(attend_kernel, first, last),
        grid=(rows // block,),
        in_specs=[
            pl.BlockSpec((block, HD), lambda i: (i, 0)),
            pl.BlockSpec((tokens, HD), whole),
            pl.BlockSpec((tokens, HD), lambda i: (0, value_at)),
            pl.BlockSpec((1, block), lambda i: (0, i % wrap)),
            pl.BlockSpec((1, block), lambda i: (0, i % wrap)),
            pl.BlockSpec((1, tokens), whole),
        ]
        + ([] if first else [pl.BlockSpec((block, 2 * HD), lambda i: (i, 0))]),
        out_specs=[
            pl.BlockSpec((block, HD), lambda i: (i, 0)),
            pl.BlockSpec((8, block), lambda i: (0, i)),
        ]
        if last
        else pl.BlockSpec((block, 2 * HD), lambda i: (i, 0)),
        out_shape=[
            jax.ShapeDtypeStruct((rows, HD), F32),
            jax.ShapeDtypeStruct((8, rows), F32),
        ]
        if last
        else jax.ShapeDtypeStruct((rows, 2 * HD), F32),
        compiler_params=pltpu.CompilerParams(vmem_limit_bytes=VMEM_LIMIT),
        cost_estimate=cost,
    )(query, keys, values, qpos, qlow, kpos, *([] if first else [total]))


def attend_back_kernel(
    chunk, own, first, q_ref, g_ref, log_ref, qpos_ref, qlow_ref, k_ref, v_ref, kpos_ref,
    in_ref, extra_ref, dq_ref, dk_ref, dv_ref, *new_ref,
):
    rows = q_ref.shape[0]
    delta_ref = new_ref[0] if first else extra_ref

    @pl.when(pl.program_id(0) == 0)
    def _():
        if first:
            dq_ref[...] = jnp.zeros_like(dq_ref)
            for i in range(rows // chunk):
                at = pl.ds(i * chunk, chunk)
                product = g_ref[at, :].astype(F32) * in_ref[at, :]
                sums = jnp.sum(product.T, axis=0, keepdims=True)
                delta_ref[:, at] = jnp.broadcast_to(sums, (8, chunk))
        else:
            dq_ref[...] = in_ref[...]

    keys = k_ref[...]
    values = v_ref[...]
    kpos = jnp.broadcast_to(kpos_ref[...], (8, keys.shape[0])).T[:, :1]
    key_sum = jnp.zeros(keys.shape, F32)
    value_sum = jnp.zeros(keys.shape, F32)
    for i in range(rows // chunk):
        at = pl.ds(i * chunk, chunk)
        place = pl.ds((i * chunk) % own, chunk)
        query = q_ref[at, :]
        upstream = g_ref[at, :]
        scores = col_inner(keys, query)
        allowed = (kpos <= qpos_ref[:, place]) & (kpos >= qlow_ref[:, place])
        probs = jnp.where(allowed, jnp.exp2(scores * EXP2_SCALE - log_ref[0:1, at]), 0.0)
        prob_grad = col_inner(values, upstream)
        score_grad = (probs * (prob_grad - delta_ref[0:1, at])).astype(BF16)
        value_sum = value_sum + dot(probs.astype(BF16), upstream)
        key_sum = key_sum + dot(score_grad, query)
        dq_ref[at, :] += row_outer(score_grad, keys) * SCORE_SCALE
    dk_ref[...] = key_sum * SCORE_SCALE
    dv_ref[...] = value_sum


def attend_back(query, upstream, logs, qpos, qlow, keys, values, kpos, before, out):
    rows, tokens = query.shape[0], keys.shape[0]
    value_at = values.shape[1] // HD - 1
    own = qpos.shape[1]
    block = 512
    first = before is None
    cost = pl.CostEstimate(
        flops=32 * rows * tokens * HD, bytes_accessed=8 * tokens * HD, transcendentals=rows * tokens
    )
    whole = lambda i: (0, 0)
    taken = (out, logs) if first else before
    return pl.pallas_call(
        functools.partial(attend_back_kernel, 512, own, first),
        grid=(tokens // block,),
        in_specs=[
            pl.BlockSpec((rows, HD), whole),
            pl.BlockSpec((rows, HD), whole),
            pl.BlockSpec((8, rows), whole),
            pl.BlockSpec((1, own), whole),
            pl.BlockSpec((1, own), whole),
            pl.BlockSpec((block, HD), lambda i: (i, 0)),
            pl.BlockSpec((block, HD), lambda i: (i, value_at)),
            pl.BlockSpec((1, block), lambda i: (0, i)),
            pl.BlockSpec((rows, HD), whole),
            pl.BlockSpec((8, rows), whole),
        ],
        out_specs=[
            pl.BlockSpec((rows, HD), whole),
            pl.BlockSpec((block, HD), lambda i: (i, 0)),
            pl.BlockSpec((block, HD), lambda i: (i, 0)),
        ]
        + ([pl.BlockSpec((8, rows), whole)] if first else []),
        out_shape=[
            jax.ShapeDtypeStruct((rows, HD), F32),
            jax.ShapeDtypeStruct((tokens, HD), F32),
            jax.ShapeDtypeStruct((tokens, HD), F32),
        ]
        + ([jax.ShapeDtypeStruct((8, rows), F32)] if first else []),
        compiler_params=pltpu.CompilerParams(vmem_limit_bytes=VMEM_LIMIT),
        cost_estimate=cost,
    )(query, upstream, logs, qpos, qlow, keys, values, kpos, *taken)


def local(
    inputs,
    dealing,
    lengths,
    input_gain,
    w_query,
    w_key,
    w_value,
    query_gain,
    key_gain,
    w_out,
    hidden_gain,
    w_gate,
    w_up,
    w_down,
    cotangent,
):
    heads, blks = lax.axis_size("head"), lax.axis_size("blk")
    head, blk = lax.axis_index("head"), lax.axis_index("blk")
    shards = heads * blks
    chips = blks // 2
    chip, core = blk // 2, blk % 2
    shard = head * blks + blk
    rows, width = inputs.shape
    column = rows * blks
    pair = 2 * rows
    per_device = QH // blks
    query_rows, key_rows = w_query.shape[1], w_key.shape[1]
    qkv_rows = query_rows + 2 * key_rows
    in_pair = shards // KVH == heads and blks == 2 * heads

    gains = jnp.zeros((2 * width + 2 * HD,), F32)
    hidden_part = jnp.where(head == 0, hidden_gain.astype(F32), 0.0)
    for at, part in (
        (shard * input_gain.shape[0], input_gain),
        (width + blk * hidden_gain.shape[0], hidden_part),
        (2 * width + shard * query_gain.shape[0], query_gain),
        (2 * width + HD + shard * key_gain.shape[0], key_gain),
    ):
        gains = lax.dynamic_update_slice(gains, part.astype(F32), (at,))
    wire = Wire(inputs)

    index = jnp.stack(
        [
            (((chip - step) % chips) * 2 + (core ^ flip)) * heads + (head ^ place)
            for place in range(heads)
            for step in range(chips)
            for flip in range(2)
        ]
    )
    key_places, query_starts, cosine, sine = tables(
        index, lengths, dealing.reshape(blks * heads, rows), column, heads
    )
    query_places = key_places[:1]

    qkv_job = Job(
        plane_gather(jnp.concatenate([w_query.T, w_key.T, w_value.T], axis=0), False)
    )
    gain_job = Job(sum_everywhere(gains.reshape(-1, 128)))
    token_blocks = wire.drive(
        column_gather(inputs), riders=[qkv_job], hooks=[lambda: [gain_job]]
    )
    qkv_weights, gains = qkv_job.result, gain_job.result
    token_blocks = [part for parts in token_blocks for part in parts]
    gains = gains.reshape(-1)
    input_norm = gains[:width]
    hidden_norm = gains[width : 2 * width]
    query_norm = gains[2 * width : 2 * width + HD]
    key_norm = gains[2 * width + HD :]
    qkv_weights = jnp.concatenate(qkv_weights, axis=0)
    feed_rows, out_rows = w_down.shape[0], w_out.shape[0]
    out_weights = lax.all_gather(wire.tie(w_out)[0], "head", axis=0, tiled=True)
    column_values = jnp.concatenate(token_blocks, axis=0).astype(F32)
    normed_column = (column_values * rms_scale(column_values) * input_norm).astype(BF16)
    raw = col_inner(qkv_weights, normed_column).astype(BF16)
    norms = jnp.stack([query_norm, key_norm], axis=1)

    def reorder(value, index):
        cut = value.reshape(value.shape[:-1] + (blks, rows))
        return jnp.take(cut, index, axis=-2).reshape(value.shape)

    places = jnp.arange(blks)
    to_ring = ((chip - places // 2) % chips) * 2 + ((places % 2) ^ core)

    def gather_members(value):
        return reorder(lax.all_gather(reorder(value, to_ring), "blk", axis=0), to_ring)

    def exchange(pieces, behind=False):
        return [pieces[0]] + wire.phase(
            [(pieces[flip], member_move(flip)) for flip in range(1, heads)], behind
        )

    member = blk % heads
    odd = chip % 2
    if in_pair:
        pieces = exchange(split_blocks(head ^ member, [raw], heads))
        raw, query, key_value = rope_members(
            member, odd, pieces, cosine, sine, norms, rows, query_rows, key_rows
        )
    else:
        raw = raw.reshape(heads, qkv_rows, column)
        by_head = jnp.stack([pick(raw, head ^ place) for place in range(heads)])
        every = jnp.swapaxes(gather_members(by_head), 0, 1)
        every = every.reshape(shards, qkv_rows, column)
        query_all = every[:, :query_rows].reshape(QH, HD, column)
        key_all = every[:, query_rows : query_rows + key_rows].reshape(KVH, HD, column)
        value_all = every[:, query_rows + key_rows :].reshape(KVH, HD, column)
        query_raw = lax.dynamic_slice_in_dim(query_all, blk * per_device, per_device, 0)
        key_raw = pick(key_all, blk * KVH // blks)
        value_raw = pick(value_all, blk * KVH // blks)

        query = rope_forward(query_raw, query_norm, cosine, sine).astype(BF16)
        keys = rope_forward(key_raw, key_norm, cosine, sine).astype(BF16)
        query = jnp.swapaxes(query, 1, 2).reshape(per_device * column, HD)
        key_value = jnp.concatenate([keys.T, value_raw.T], axis=1)
    own_cotangent = lax.dynamic_slice_in_dim(cotangent, head * rows, rows, 0)
    cotangent_job = wire.add(column_gather(own_cotangent))

    pairs = {0: key_value}
    key_pieces, value_pieces = dict(pairs), dict(pairs)
    total = None

    def add_column(place, total):
        return attend(
            query,
            key_pieces[place],
            value_pieces[place],
            query_places,
            query_starts,
            key_places[place : place + 1],
            total,
            place == heads - 1,
        )

    ready = [0]
    for forward, backward in zip(plane_steps(False), plane_steps(True)):
        if forward == backward:
            items = [(pairs[source], head_move(bit)) for place, source, bit in forward]
        else:
            items = [
                (key_pieces[source][:, :HD], head_move(bit)) for place, source, bit in forward
            ] + [(value_pieces[source][:, -HD:], head_move(bit)) for place, source, bit in backward]
        got = wire.phase(items, behind=True)
        for place in ready:
            total = add_column(place, total)
        if ready == [0]:
            late = jnp.concatenate([w_gate.T, w_up.T, w_down], axis=0)
            total, late = wire.tie(total, late)
        else:
            total = wire.tie(total)[0]
        ready = [place for place, source, bit in forward]
        for index, place in enumerate(ready):
            key_pieces[place] = got[index]
            if forward == backward:
                value_pieces[place] = pairs[place] = got[index]
            else:
                value_pieces[backward[index][0]] = got[len(forward) + index]
    wire.phase([], behind=True)
    for place in ready:
        total = add_column(place, total)
    heads_out, logs = total

    if in_pair:
        pieces = exchange(mixed_members(member, heads_out, heads, column))
        mixed = join_members(member, odd, pieces, rows).reshape(heads * out_rows, column)
    else:
        mixed_heads = jnp.swapaxes(heads_out.astype(BF16).reshape(per_device, column, HD), 1, 2)
        every = gather_members(mixed_heads)
        every = every.reshape(heads, blks, out_rows, column)
        mixed = lax.dynamic_index_in_dim(every, blk, 1).reshape(heads * out_rows, column)
    wire.jobs.remove(cotangent_job)
    branch = wire.drive(
        column_scatter(
            lambda step: row_outer(mixed[:, step * pair : (step + 1) * pair], out_weights)
        ),
        riders=[cotangent_job],
    )
    token_values = inputs.astype(F32)
    middle = token_values + branch
    scale_two = rms_scale(middle)
    hidden_in = (middle * scale_two * hidden_norm).astype(BF16)

    late = lax.all_gather(late, "head", axis=0)
    gate_weights, up_weights, down_weights = (
        late[:, i * feed_rows : (i + 1) * feed_rows].reshape(-1, width) for i in range(3)
    )
    hidden_parts = []
    feed_halves = []
    feed_weights = [gate_weights, up_weights, down_weights]
    half_chips = chips // 2

    def feed_half(index):
        start = index * half_chips
        steps = range(start, start + half_chips)
        tokens, upstream = (
            jnp.concatenate([part for step in steps for part in parts[step]], axis=0)
            for parts in (hidden_parts, cotangent_job.result)
        )
        gate_weights, up_weights, down_weights = feed_weights
        act_grad = col_inner(upstream, down_weights)
        gate = col_inner(tokens, gate_weights)
        up_proj = col_inner(tokens, up_weights)
        sigmoid_gate = jax.nn.sigmoid(gate)
        silu_gate = gate * sigmoid_gate
        activated = (silu_gate * up_proj).astype(BF16)
        gate_grad = (
            act_grad * up_proj * sigmoid_gate * (1.0 + gate * (1.0 - sigmoid_gate))
        ).astype(BF16)
        up_grad = (act_grad * silu_gate).astype(BF16)
        back = dot(gate_grad, gate_weights) + dot(up_grad, up_weights)
        feed_halves.append((tokens, upstream, activated, gate_grad, up_grad, back))

    def feed_hook(step):
        def hook():
            if step == 0:
                feed_weights[:] = wire.tie(*feed_weights)
            if step == half_chips:
                feed_half(0)
                feed_halves[0] = tuple(wire.tie(*feed_halves[0]))

        return hook

    wire.drive(
        column_gather(hidden_in, hidden_parts), hooks=[feed_hook(step) for step in range(chips)]
    )
    feed_half(1)
    gate_weights, up_weights, down_weights = feed_weights

    def half_rows(index, step):
        at = (step % half_chips) * pair
        return feed_halves[step // half_chips][index][at : at + pair]

    grad_down, grad_gate, grad_up = (
        sum(row_outer(half[left], half[right]) for half in feed_halves).astype(BF16)
        for left, right in ((2, 1), (3, 0), (4, 0))
    )
    feed_grads = [grad_down, grad_gate, grad_up]

    def keep_grads(*indices):
        def hook():
            for index in indices:
                feed_grads[index] = wire.tie(feed_grads[index])[0]

        return hook

    hidden_grad = wire.drive(
        column_scatter(lambda step: half_rows(5, step), apart=True),
        hooks=[lambda: None, lambda: None, lambda: None, keep_grads(0), keep_grads(1)],
    )
    hidden_gain_grad = jnp.sum(hidden_grad * middle * scale_two, axis=0)
    middle_grad = own_cotangent.astype(F32) + norm_back(hidden_grad, middle, scale_two, hidden_norm)
    branch_grad = middle_grad.astype(BF16)
    down_parts = {}

    def keep_all():
        feed_grads[:] = [
            jnp.concatenate(
                [grad.reshape(heads, feed_rows, width) for grad in feed_grads], axis=1
            )
        ]
        for step in range(1, chips):
            down_parts[step] = dot(half_rows(2, step), down_weights)
        feed_grads[0], *parts = wire.tie(feed_grads[0], *down_parts.values())
        down_parts.update(zip(down_parts, parts))

    branch_blocks = join_blocks(
        wire.drive(column_gather(branch_grad), hooks=[keep_grads(2), keep_all])
    )
    down_parts[0] = dot(half_rows(2, 0), down_weights)
    feed_grads = lax.psum_scatter(feed_grads[0], "head", scatter_dimension=0).astype(F32)
    down_job = wire.add(column_scatter(lambda step: down_parts[step]))
    mixed_grads = [col_inner(out_weights, block).astype(BF16) for block in branch_blocks]
    grad_out = dot(mixed, jnp.concatenate(branch_blocks, axis=0)).reshape(heads, out_rows, width)
    if in_pair:
        pieces = exchange(split_blocks(member, mixed_grads, heads), True)
        upstream = upstream_members(member, odd, pieces, rows)
    else:
        mixed_grad = jnp.concatenate(mixed_grads, axis=1).reshape(heads, out_rows, column)
        every = gather_members(mixed_grad)
        every = jnp.swapaxes(every, 0, 1).reshape(blks, per_device, HD, column)
        upstream = jnp.swapaxes(pick(every, blk), 1, 2).reshape(per_device * column, HD)

    key_grads, value_grads = {}, {}
    carry = None
    wire.phase([], behind=True)
    for forward, backward in zip(plane_steps(False)[::-1] + [[]], plane_steps(True)[::-1] + [[]]):
        for place in [step[0] for step in forward] if forward else [0]:
            results = attend_back(
                query,
                upstream,
                logs,
                query_places,
                query_starts,
                key_pieces[place],
                value_pieces[place],
                key_places[place : place + 1],
                carry,
                heads_out,
            )
            key_grads[place] = key_grads.get(place, 0.0) + results[1]
            value_grads[place] = value_grads.get(place, 0.0) + results[2]
            carry = (results[0], carry[1] if carry else results[3])
        if not forward:
            break
        if forward == backward:
            items = [
                (
                    jnp.concatenate([key_grads[place], value_grads[place]], axis=1).astype(BF16),
                    head_move(bit),
                )
                for place, source, bit in forward
            ]
        else:
            items = [
                (key_grads[place].astype(BF16), head_move(bit)) for place, source, bit in forward
            ] + [
                (value_grads[place].astype(BF16), head_move(bit))
                for place, source, bit in backward
            ]
        tied = lax.optimization_barrier(tuple(value for value, move in items) + carry)
        items = [(value, move) for value, (ignored, move) in zip(tied, items)]
        carry = tied[len(items) :]
        got = wire.phase(items, behind=True)
        last_parts = got
        if forward[0][1] == 0:
            continue
        for index, (place, source, bit) in enumerate(forward):
            part = got[index][:, :HD].astype(F32)
            key_grads[source] = key_grads.get(source, 0.0) + part
        for index, (place, source, bit) in enumerate(backward):
            part = got[index if forward == backward else len(forward) + index]
            value_grads[source] = value_grads.get(source, 0.0) + part[:, -HD:].astype(F32)
    query_grad = carry[0]

    if in_pair:
        *pieces, gain_grads = rope_back_members(
            member, raw, query_grad, cosine, sine, norms, key_grads[0], value_grads[0], last_parts,
            query_rows, key_rows,
        )
        pieces = exchange(pieces, True)
        raw_grad = join_members(head ^ member, odd, pieces, rows).reshape(-1, column)
    else:
        key_grad = key_grads[0] + sum(part[:, :HD].astype(F32) for part in last_parts)
        value_grad = value_grads[0] + sum(part[:, HD:].astype(F32) for part in last_parts)
        query_grad = jnp.swapaxes(query_grad.reshape(per_device, column, HD), 1, 2)
        query_raw_grad, query_gain_grad = rope_backward(
            query_raw, query_norm, cosine, sine, query_grad
        )
        key_raw_grad, key_gain_grad = rope_backward(key_raw, key_norm, cosine, sine, key_grad.T)
        query_raw_grad = query_raw_grad.astype(BF16)
        key_raw_grad = key_raw_grad.astype(BF16)
        value_raw_grad = value_grad.T.astype(BF16)
        gain_grads = jnp.stack([jnp.sum(query_gain_grad, axis=0), key_gain_grad], axis=1)

        def spread(part, count, index):
            empty = jnp.zeros((count,) + part.shape[1:], BF16)
            return lax.dynamic_update_slice_in_dim(empty, part, index, 0)

        every = jnp.concatenate(
            [
                spread(query_raw_grad, QH, blk * per_device).reshape(shards, query_rows, column),
                spread(key_raw_grad[None], KVH, blk * KVH // blks).reshape(
                    shards, key_rows, column
                ),
                spread(value_raw_grad[None], KVH, blk * KVH // blks).reshape(
                    shards, key_rows, column
                ),
            ],
            axis=1,
        ).reshape(heads, blks, qkv_rows, column)
        every = reorder(jnp.swapaxes(every, 0, 1), to_ring)
        by_head = reorder(lax.psum_scatter(every, "blk", scatter_dimension=0), to_ring)
        raw_grad = jnp.concatenate(
            [pick(by_head, head ^ place) for place in range(heads)], axis=0
        )

    while wire.jobs:
        wire.phase([], behind=True)
    done = [feed_grads, (middle + down_job.result).astype(BF16)]
    tail = []

    def start_tail():
        qkv_grad = dot(wire.tie(raw_grad)[0], normed_column)
        input_gain_grad = jnp.sum(qkv_grad * qkv_weights.astype(F32), axis=0) / input_norm
        sums = jnp.concatenate(
            [input_gain_grad, hidden_gain_grad, gain_grads[:, 0], gain_grads[:, 1]]
        )
        qkv_grad = qkv_grad.reshape(heads, qkv_rows, width)
        tail.append(Job(sum_everywhere(sums.reshape(-1, 128))))
        parts = [
            jnp.concatenate([qkv_grad[place], pick(grad_out, head ^ place)], axis=0)
            for place in range(heads)
        ]
        tail.append(Job(plane_scatter(parts, False)))

    def keep_done():
        done[:] = wire.tie(*done)

    normed_grad = wire.drive(
        column_scatter(
            lambda step: row_outer(raw_grad[:, step * pair : (step + 1) * pair], qkv_weights)
        ),
        hooks=[start_tail, lambda: tail, keep_done],
    )
    sums, qkv_grad = tail[0].result.reshape(-1), tail[1].result
    feed_grads, layer_out = done
    grad_out = tail[1].result[qkv_rows:]
    grad_gate, grad_up, grad_down = (
        feed_grads[i * feed_rows : (i + 1) * feed_rows] for i in (1, 2, 0)
    )
    token_values = wire.token.astype(F32)
    grad_input = middle_grad + norm_back(
        normed_grad, token_values, rms_scale(token_values), input_norm
    )

    def own_part(at, size):
        return lax.dynamic_slice_in_dim(sums, at, size)

    return (
        layer_out,
        grad_input,
        own_part(shard * input_gain.shape[0], input_gain.shape[0]),
        qkv_grad[:query_rows].T,
        qkv_grad[query_rows : query_rows + key_rows].T,
        qkv_grad[query_rows + key_rows : qkv_rows].T,
        own_part(2 * width + shard * query_gain.shape[0], query_gain.shape[0]),
        own_part(2 * width + HD + shard * key_gain.shape[0], key_gain.shape[0]),
        grad_out,
        own_part(width + blk * hidden_gain.shape[0], hidden_gain.shape[0]),
        grad_gate.T,
        grad_up.T,
        grad_down,
    )


def solution(mesh):
    return jax.shard_map(
        local,
        mesh=mesh,
        in_specs=(
            P(("blk", "head"), None),
            P(),
            P(),
            P(("head", "blk")),
            P(None, ("head", "blk")),
            P(None, ("head", "blk")),
            P(None, ("head", "blk")),
            P(("head", "blk")),
            P(("head", "blk")),
            P(("head", "blk"), None),
            P("blk"),
            P(None, ("head", "blk")),
            P(None, ("head", "blk")),
            P(("head", "blk"), None),
            P("blk", None),
        ),
        out_specs=(
            P(("blk", "head"), None),
            P(("blk", "head"), None),
            P(("head", "blk")),
            P(None, ("head", "blk")),
            P(None, ("head", "blk")),
            P(None, ("head", "blk")),
            P(("head", "blk")),
            P(("head", "blk")),
            P(("head", "blk"), None),
            P("blk"),
            P(None, ("head", "blk")),
            P(None, ("head", "blk")),
            P(("head", "blk"), None),
        ),
        check_vma=False,
    )
```

```python
import functools
import math

import jax
import jax.numpy as jnp
import numpy as np
from jax import lax
from jax.experimental import pallas as pl
from jax.experimental.pallas import tpu as pltpu
from jax.sharding import PartitionSpec as P

QH = 16
KVH = 8
HD = 128
HALF = HD // 2
EPSILON = 1e-06
ROPE_BASE = 1000000.0
SCORE_SCALE = HD ** (-0.5)
EXP2_SCALE = SCORE_SCALE * math.log2(math.e)
CONTRACT_ROWS = (((0,), (0,)), ((), ()))
CONTRACT_COLS = (((1,), (1,)), ((), ()))
BF16 = jnp.bfloat16
F32 = jnp.float32
MIB = 1024 * 1024


def dot(left, right):
    return jnp.dot(left, right, preferred_element_type=F32)


def row_outer(left, right):
    return lax.dot_general(left, right, CONTRACT_ROWS, preferred_element_type=F32)


def col_inner(left, right):
    return lax.dot_general(left, right, CONTRACT_COLS, preferred_element_type=F32)


def rms_scale(values):
    return lax.rsqrt(jnp.mean(values * values, axis=-1, keepdims=True) + EPSILON)


def norm_back(upstream, source, scale_rows, gain):
    scaled = upstream * gain
    return scale_rows * scaled - source * scale_rows**3 * jnp.mean(
        scaled * source, axis=-1, keepdims=True
    )


def head_bits():
    count = lax.axis_size("head")
    return [1 << i for i in range(count.bit_length() - 1)]


def head_move(bit):
    count = lax.axis_size("head")
    return ("head", [(i, i ^ bit) for i in range(count)], bit)


def blk_move(steps, flip, link):
    count = lax.axis_size("blk")
    return ("blk", [(i, ((i + 2 * steps) % count) ^ flip) for i in range(count)], link)


def swap_move():
    return blk_move(0, 1, None)


def ring_move(steps):
    return blk_move(steps, 0, "z")


def member_move(flip):
    count = lax.axis_size("blk")
    return ("blk", [(i, i ^ flip) for i in range(count)], "z" if flip > 1 else None)


class Job:
    def __init__(self, steps):
        self.steps = steps
        self.wanted = None
        self.result = None
        self.advance(None)

    def advance(self, got):
        try:
            self.wanted = self.steps.send(got)
        except StopIteration as end:
            self.wanted = None
            self.result = end.value


class Wire:
    def __init__(self, token):
        self.token = token
        self.jobs = []

    def add(self, steps):
        job = Job(steps)
        self.jobs.append(job)
        return job

    def tie(self, *arrays):
        *arrays, self.token = lax.optimization_barrier(arrays + (self.token,))
        return arrays

    def phase(self, items, behind=False, riders=(), along=()):
        items = list(items)
        count = len(items)
        taken = []
        for job in list(riders) + (self.jobs if behind else []):
            if job.wanted is not None:
                taken.append((job, len(items), len(items) + len(job.wanted)))
                items.extend(job.wanted)
        if not items:
            for job, start, end in taken:
                job.advance([])
            return []
        values = self.tie(*[value for value, move in items])
        outs = [lax.ppermute(value, move[0], move[1]) for value, (same, move) in zip(values, items)]
        outs = self.tie(*outs, *along)
        self.along = outs[len(items) :]
        for job, start, end in taken:
            job.advance(outs[start:end])
        self.jobs = [job for job in self.jobs if job.wanted is not None]
        return outs[:count]

    def drive(self, steps, hooks=(), riders=(), behind=None, along=()):
        job = Job(steps)
        riders = list(riders)
        hooks = list(hooks)
        count = 0
        while job.wanted is not None or any(rider.wanted is not None for rider in riders):
            got = self.phase(
                job.wanted or [],
                riders=riders,
                behind=behind is not None and count >= behind,
                along=() if count else along,
            )
            if job.wanted is not None:
                job.advance(got)
            if hooks:
                riders.extend(hooks.pop(0)() or [])
            count += 1
        return job.result


def column_gather(value, blocks=None):
    chips = lax.axis_size("blk") // 2
    near = chips // 2
    blocks = {} if blocks is None else blocks
    fresh = {0: value}
    up = down = value
    for hop in range(1, near + 2):
        items = [(part, swap_move()) for part in fresh.values()]
        if hop <= near:
            items.append((up, ring_move(1)))
        if hop <= chips - 1 - near:
            items.append((down, ring_move(-1)))
        got = yield items
        for (step, part), other in zip(fresh.items(), got):
            blocks[step] = [part, other]
        got = got[len(fresh) :]
        fresh = {}
        if got:
            up = fresh[hop] = got[0]
        if len(got) > 1:
            down = fresh[chips - hop] = got[1]
    return [blocks[step] for step in range(chips)]


def ring_gather(value):
    chips = lax.axis_size("blk") // 2
    blocks = []
    for step in range(chips):
        items = [(value, swap_move())]
        if step < chips - 1:
            items.append((value, ring_move(1)))
        got = yield items
        blocks.append([value, got[0]])
        value = got[-1]
    return blocks


def ring_scatter(part_of):
    chips = lax.axis_size("blk") // 2
    order = list(range(1, chips)) + [0]

    def halves(step):
        part = part_of(step)
        rows = part.shape[0] // 2
        return part[:rows], part[rows:]

    own, other = halves(order[0])
    got = yield [(other.astype(BF16), swap_move())]
    total = own.astype(F32) + got[0].astype(F32)
    for step in order[1:]:
        own, other = halves(step)
        got = yield [(total.astype(BF16), ring_move(1)), (other.astype(BF16), swap_move())]
        total = own.astype(F32) + got[1].astype(F32) + got[0].astype(F32)
    return total


def join_blocks(blocks):
    return [jnp.concatenate(block, axis=0) for block in blocks]


def column_scatter(part_of, apart=False):
    chips = lax.axis_size("blk") // 2
    near = chips // 2
    totals = {}

    def swaps(steps):
        parts = {step: part_of(step) for step in steps}
        half = parts[steps[0]].shape[0] // 2
        items = [(parts[step][half:].astype(BF16), swap_move()) for step in steps]
        return items, {step: part[:half] for step, part in parts.items()}

    def add(own, got):
        for (step, part), other in zip(own.items(), got):
            totals[step] = part.astype(F32) + other.astype(F32) + totals.get(step, 0.0)

    items, own = swaps([near])
    add(own, (yield items))
    for hop in range(near, 0, -1):
        both = hop <= chips - 1 - near
        moves = [(totals[hop].astype(BF16), ring_move(-1))]
        if both:
            moves.append((totals[chips - hop].astype(BF16), ring_move(1)))
        steps = sorted({hop - 1, (chips - hop + 1) % chips})
        if apart:
            got = yield moves
            items, own = swaps(steps)
            add(own, (yield items))
            apart = False
        else:
            items, own = swaps(steps)
            got = yield moves + items
            add(own, got[len(moves) :])
        totals[hop - 1] = totals[hop - 1] + got[0].astype(F32)
        if both:
            step = (chips - hop + 1) % chips
            totals[step] = totals[step] + got[1].astype(F32)
    return totals[0]


def plane_steps(backwards):
    bits = head_bits()
    order = bits[::-1] if backwards else bits
    steps = []
    for weight in range(1, len(bits) + 1):
        step = []
        for place in range(1 << len(bits)):
            if bin(place).count("1") == weight:
                last = [bit for bit in order if place & bit][-1]
                step.append((place, place ^ last, last))
        steps.append(step)
    return steps


def plane_gather(value, backwards):
    pieces = {0: value}
    for step in plane_steps(backwards):
        got = yield [(pieces[source], head_move(bit)) for place, source, bit in step]
        for (place, source, bit), piece in zip(step, got):
            pieces[place] = piece
    return [pieces[i] for i in range(len(pieces))]


def plane_scatter(parts, backwards, pause=False):
    pieces = list(parts)
    for index, step in enumerate(plane_steps(backwards)[::-1]):
        if pause and index == 1:
            yield []
        got = yield [(pieces[place].astype(BF16), head_move(bit)) for place, source, bit in step]
        for (place, source, bit), piece in zip(step, got):
            pieces[source] = pieces[source] + piece.astype(F32)
    return pieces[0]


def sum_everywhere(value):
    chips = lax.axis_size("blk") // 2
    for moves in (
        *([head_move(bit)] for bit in head_bits()),
        [swap_move()],
        [blk_move(steps, 0, None) for steps in range(1, chips)],
    ):
        got = yield [(value, move) for move in moves]
        for part in got:
            value = value + part
    return value


def pick(stack, index):
    return lax.dynamic_index_in_dim(stack, index, 0, keepdims=False)


def token_starts(anchors, lengths):
    ends = jnp.cumsum(lengths)
    seq_starts = ends - lengths
    inside = seq_starts[None, :] <= anchors[:, None]
    return jnp.max(jnp.where(inside, seq_starts[None, :], 0), axis=1)


def rope_tables(places):
    ladder = jnp.arange(HALF, dtype=F32)
    rates = jnp.exp(ladder * (-2.0 * math.log(ROPE_BASE) / HD))
    angles = rates[:, None] * places.astype(F32)[None, :]
    return (jnp.cos(angles), jnp.sin(angles))


def rope_forward(raw, gain, cosine, sine):
    heads = raw.astype(F32)
    scale = lax.rsqrt(jnp.mean(heads * heads, axis=-2, keepdims=True) + EPSILON)
    normed = heads * scale * gain[:, None]
    low, high = normed[..., :HALF, :], normed[..., HALF:, :]
    return jnp.concatenate([low * cosine - high * sine, high * cosine + low * sine], axis=-2)


def rope_backward(raw, gain, cosine, sine, upstream):
    heads = raw.astype(F32)
    scale = lax.rsqrt(jnp.mean(heads * heads, axis=-2, keepdims=True) + EPSILON)
    low, high = upstream[..., :HALF, :], upstream[..., HALF:, :]
    turned = jnp.concatenate([low * cosine + high * sine, high * cosine - low * sine], axis=-2)
    gain_grad = jnp.sum(turned * heads * scale, axis=-1)
    scaled = turned * gain[:, None]
    back = scale * scaled - heads * scale**3 * jnp.mean(scaled * heads, axis=-2, keepdims=True)
    return back, gain_grad


def small_call(kernel, outs, scalars, arrays, scratch=()):
    vmem = pl.BlockSpec(memory_space=pltpu.VMEM)
    return pl.pallas_call(
        kernel,
        in_specs=[pl.BlockSpec(memory_space=pltpu.SMEM)] + [vmem] * len(arrays),
        out_specs=[vmem] * len(outs),
        out_shape=[jax.ShapeDtypeStruct(shape, dtype) for shape, dtype in outs],
        scratch_shapes=[pltpu.VMEM(shape, dtype) for shape, dtype in scratch],
        compiler_params=pltpu.CompilerParams(vmem_limit_bytes=10 * MIB),
        cost_estimate=pl.CostEstimate(
            flops=0,
            bytes_accessed=3 * sum(array.size * array.dtype.itemsize for array in arrays),
            transcendentals=0,
        ),
    )(scalars, *arrays)


def table_kernel(blocks, sequences, index_ref, deal_ref, rate_ref, key_ref, start_ref, cos_ref, sin_ref):
    heads, column = key_ref.shape
    rows = column // blocks
    for place in range(heads):
        for block in range(blocks):
            row = deal_ref[pl.ds(index_ref[place * blocks + block], 1), :]
            key_ref[place : place + 1, block * rows : (block + 1) * rows] = row
    own = key_ref[0:1, :]
    starts = jnp.zeros_like(own)
    first = jnp.int32(0)
    for sequence in range(sequences - 1):
        first = first + index_ref[heads * blocks + sequence]
        starts = jnp.where(own >= first, first, starts)
    start_ref[...] = starts
    angles = rate_ref[:, :1] * (own - starts).astype(F32)
    cos_ref[...] = jnp.cos(angles)
    sin_ref[...] = jnp.sin(angles)


def tables(index, lengths, deals, column, heads):
    rates = np.exp(
        np.arange(HALF, dtype=np.float32) * np.float32(-2.0 * math.log(ROPE_BASE) / HD)
    ).astype(np.float32)
    return small_call(
        functools.partial(table_kernel, column // deals.shape[1], lengths.shape[0]),
        [
            ((heads, column), jnp.int32),
            ((1, column), jnp.int32),
            ((HALF, column), F32),
            ((HALF, column), F32),
        ],
        jnp.concatenate([index, lengths]),
        [deals, jnp.asarray(np.broadcast_to(rates[:, None], (HALF, 128)))],
    )


def put_in_order(out_ref, scalar_ref, pieces, rows, finish):
    base = scalar_ref[0]
    for flip, piece in enumerate(pieces):
        value = piece[...]
        column = value.shape[1]
        if flip & 1:
            cuts = [value[:, i * rows : (i + 1) * rows] for i in range(column // rows)]
            value = jnp.concatenate([cuts[i ^ 1] for i in range(column // rows)], axis=1)
        at = pl.ds(base ^ flip, 1)
        if flip & 2:
            pair = 2 * rows

            @pl.when(scalar_ref[1] == 0)
            def _(at=at, value=value, pair=pair):
                out_ref[at] = jnp.concatenate([value[:, pair:], value[:, :pair]], axis=1)[None]

            @pl.when(scalar_ref[1] != 0)
            def _(at=at, value=value, pair=pair):
                out_ref[at] = jnp.concatenate([value[:, -pair:], value[:, :-pair]], axis=1)[None]

        else:
            out_ref[at] = value[None]
    finish()


def join_members(base, odd, pieces, rows):
    count = len(pieces)

    def kernel(scalar_ref, *refs):
        put_in_order(refs[count], scalar_ref, refs[:count], rows, lambda: None)

    return small_call(
        kernel,
        [((count,) + pieces[0].shape, BF16)],
        jnp.stack([base, odd]).astype(jnp.int32),
        pieces,
    )[0]


def split_blocks(base, blocks, count):
    size = blocks[0].shape[0] // count
    width = blocks[0].shape[1]

    def kernel(scalar_ref, *refs):
        for flip in range(count):
            start = pl.multiple_of((scalar_ref[0] ^ flip) * size, size)
            for index in range(len(blocks)):
                refs[len(blocks) + flip][:, index * width : (index + 1) * width] = refs[index][
                    pl.ds(start, size), :
                ]

    return small_call(
        kernel,
        [((size, width * len(blocks)), BF16)] * count,
        base.reshape(1).astype(jnp.int32),
        blocks,
    )


def rope_kernel(rows, query_rows, key_rows, scalar_ref, *refs):
    pieces = refs[:-6]
    cos_ref, sin_ref, gain_ref, raw_ref, query_ref, pair_ref = refs[-6:]
    count, column = len(pieces), cos_ref.shape[1]
    put_in_order(raw_ref, scalar_ref, pieces, rows, lambda: None)
    cosine, sine = cos_ref[...], sin_ref[...]

    def rotate(parts, gain):
        heads = jnp.concatenate(parts, axis=0).astype(F32)
        scale = lax.rsqrt(jnp.mean(heads * heads, axis=0, keepdims=True) + EPSILON)
        normed = heads * scale * gain
        low, high = normed[:HALF], normed[HALF:]
        turned = jnp.concatenate([low * cosine - high * sine, high * cosine + low * sine], axis=0)
        return turned.T.astype(BF16)

    per_head = HD // query_rows
    for head in range(count // per_head):
        parts = [raw_ref[head * per_head + i, :query_rows, :] for i in range(per_head)]
        query_ref[head * column : (head + 1) * column, :] = rotate(parts, gain_ref[:, 0:1])
    parts = [raw_ref[i, query_rows : query_rows + key_rows, :] for i in range(count)]
    pair_ref[:, :HD] = rotate(parts, gain_ref[:, 1:2])
    parts = [raw_ref[i, query_rows + key_rows :, :] for i in range(count)]
    pair_ref[:, HD:] = jnp.concatenate(parts, axis=0).astype(F32).T.astype(BF16)


def rope_members(base, odd, pieces, cosine, sine, gains, rows, query_rows, key_rows):
    count, column = len(pieces), cosine.shape[1]
    return small_call(
        functools.partial(rope_kernel, rows, query_rows, key_rows),
        [
            ((count,) + pieces[0].shape, BF16),
            ((count * query_rows // HD * column, HD), BF16),
            ((column, 2 * HD), BF16),
        ],
        jnp.stack([base, odd]).astype(jnp.int32),
        list(pieces) + [cosine, sine, gains],
    )


def mixed_kernel(scalar_ref, in_ref, *refs):
    outs, parts_ref = refs[:-1], refs[-1]
    count, size, column = parts_ref.shape
    for head in range(in_ref.shape[0] // column):
        part = in_ref[head * column : (head + 1) * column, :].T.astype(BF16)
        per_head = HD // size
        for i in range(per_head):
            parts_ref[head * per_head + i] = part[i * size : (i + 1) * size]
    for flip, out_ref in enumerate(outs):
        out_ref[...] = parts_ref[scalar_ref[0] ^ flip]


def mixed_members(base, heads_out, count, column):
    size = heads_out.shape[0] // column * HD // count
    return small_call(
        mixed_kernel,
        [((size, column), BF16)] * count,
        base.reshape(1).astype(jnp.int32),
        [heads_out],
        [((count, size, column), BF16)],
    )


def upstream_members(base, odd, pieces, rows):
    count = len(pieces)
    size, column = pieces[0].shape
    per_head = HD // size

    def kernel(scalar_ref, *refs):
        out_ref, parts_ref = refs[count:]
        put_in_order(parts_ref, scalar_ref, refs[:count], rows, lambda: None)
        for head in range(count // per_head):
            parts = [parts_ref[head * per_head + i] for i in range(per_head)]
            out_ref[head * column : (head + 1) * column, :] = (
                jnp.concatenate(parts, axis=0).astype(F32).T.astype(BF16)
            )

    return small_call(
        kernel,
        [((count // per_head * column, HD), BF16)],
        jnp.stack([base, odd]).astype(jnp.int32),
        pieces,
        [((count, size, column), BF16)],
    )[0]


def light():
    return pl.CostEstimate(flops=1, bytes_accessed=1, transcendentals=0)


def weight_grad_kernel(count, groups, *refs):
    pieces, lefts = refs[:count], refs[count : count + groups]
    out_ref, right_ref = refs[-2:]
    rows = pieces[0].shape[0]

    @pl.when(pl.program_id(0) == 0)
    def _():
        for index in range(count):
            right_ref[index * rows : (index + 1) * rows, :] = pieces[index][...]

    size = out_ref.shape[1]
    for head in range(lefts[0].shape[1] // size):

        @pl.when(pl.program_id(0) == head)
        def _(head=head):
            cut = slice(head * size, (head + 1) * size)
            left = jnp.concatenate([ref[:, cut] for ref in lefts], axis=0)
            out_ref[0] = row_outer(left, right_ref[...]).astype(BF16)


def weight_grads(lefts, pieces, heads, kind, into):
    size = lefts[0].shape[1] // heads
    piece, width = pieces[0].shape
    count = len(pieces)
    specs = [pl.BlockSpec((piece, width), lambda i: (0, 0))] * count
    specs += [pl.BlockSpec(left.shape, lambda i: (0, 0)) for left in lefts]
    operands = list(pieces) + list(lefts)
    aliases = {}
    if into is not None:
        specs.append(pl.BlockSpec(memory_space=pl.ANY))
        aliases = {len(operands): 0}
        operands.append(into)
    return pl.pallas_call(
        functools.partial(weight_grad_kernel, count, len(lefts)),
        grid=(heads,),
        in_specs=specs,
        out_specs=pl.BlockSpec((1, size, width), lambda i: (i, kind, 0)),
        out_shape=jax.ShapeDtypeStruct((heads, 3 * size, width), BF16),
        scratch_shapes=[pltpu.VMEM((count * piece, width), BF16)],
        input_output_aliases=aliases,
        compiler_params=pltpu.CompilerParams(vmem_limit_bytes=20 * MIB),
        cost_estimate=light(),
    )(*operands)


def rope_back_kernel(query_rows, key_rows, count, scalar_ref, *refs):
    raw_ref, dq_ref, cos_ref, sin_ref, gain_ref, dk_ref, dv_ref = refs[:7]
    more = refs[7 : -2 - count]
    outs, gain_out, parts_ref = refs[-2 - count : -2], refs[-2], refs[-1]
    column = cos_ref.shape[1]
    cosine, sine = cos_ref[...], sin_ref[...]

    def back(parts, gain, upstream):
        heads = jnp.concatenate(parts, axis=0).astype(F32)
        scale = lax.rsqrt(jnp.mean(heads * heads, axis=0, keepdims=True) + EPSILON)
        low, high = upstream[:HALF], upstream[HALF:]
        turned = jnp.concatenate([low * cosine + high * sine, high * cosine - low * sine], axis=0)
        gain_grad = jnp.sum(turned * heads * scale, axis=1, keepdims=True)
        scaled = turned * gain
        mean = jnp.mean(scaled * heads, axis=0, keepdims=True)
        return (scale * scaled - heads * (scale * scale * scale * mean)).astype(BF16), gain_grad

    per_head = HD // query_rows
    total = jnp.zeros((HD, 1), F32)
    for head in range(count // per_head):
        at = [head * per_head + i for i in range(per_head)]
        grad, gain_grad = back(
            [raw_ref[i, :query_rows, :] for i in at],
            gain_ref[:, 0:1],
            dq_ref[head * column : (head + 1) * column, :].T,
        )
        total = total + gain_grad
        for place, i in enumerate(at):
            parts_ref[i, :query_rows, :] = grad[place * query_rows : (place + 1) * query_rows]
    gain_out[:, 0:1] = total
    key_grad, value_grad = dk_ref[...], dv_ref[...]
    for ref in more:
        key_grad = key_grad + ref[:, :HD].astype(F32)
        value_grad = value_grad + ref[:, HD:].astype(F32)
    grad, gain_grad = back(
        [raw_ref[i, query_rows : query_rows + key_rows, :] for i in range(count)],
        gain_ref[:, 1:2],
        key_grad.T,
    )
    gain_out[:, 1:2] = gain_grad
    value_grad = value_grad.T.astype(BF16)
    for i in range(count):
        cut = slice(i * key_rows, (i + 1) * key_rows)
        parts_ref[i, query_rows : query_rows + key_rows, :] = grad[cut]
        parts_ref[i, query_rows + key_rows :, :] = value_grad[cut]
    for flip, out_ref in enumerate(outs):
        out_ref[...] = parts_ref[scalar_ref[0] ^ flip]


def rope_back_members(base, raw, dq, cosine, sine, gains, dk, dv, more, query_rows, key_rows):
    count, size, column = raw.shape
    return small_call(
        functools.partial(rope_back_kernel, query_rows, key_rows, count),
        [((size, column), BF16)] * count + [((HD, 2), F32)],
        base.reshape(1).astype(jnp.int32),
        [raw, dq, cosine, sine, gains, dk, dv] + list(more),
        [((count, size, column), BF16)],
    )


def attend_kernel(first, last, *refs):
    refs = list(refs)
    q_ref, k_ref, v_ref, qpos_ref, qlow_ref, kpos_ref = refs[:6]
    outs = refs[6:] if first else refs[7:]
    kpos = kpos_ref[...]
    scores = col_inner(q_ref[...], k_ref[...])
    rows = q_ref.shape[0]
    qpos = jnp.broadcast_to(qpos_ref[...], (8, rows)).T[:, :1]
    qlow = jnp.broadcast_to(qlow_ref[...], (8, rows)).T[:, :1]
    allowed = (kpos <= qpos) & (kpos >= qlow)
    lifted = jnp.where(allowed, jnp.exp2(scores * EXP2_SCALE), 0.0).astype(BF16)
    values = jnp.concatenate([v_ref[...], jnp.ones(v_ref.shape, BF16)], axis=1)
    total = dot(lifted, values)
    if not first:
        total = total + refs[6][...]
    if last:
        weight = total[:, HD:]
        outs[0][...] = total[:, :HD] / weight
        outs[1][...] = jnp.log2(weight).T[:8, :]
    else:
        outs[0][...] = total


def attend(query, keys, values, qpos, qlow, kpos, total, last):
    rows, tokens = query.shape[0], keys.shape[0]
    value_at = values.shape[1] // HD - 1
    own = qpos.shape[1]
    block = 256
    wrap = own // block
    first = total is None
    cost = pl.CostEstimate(
        flops=20 * rows * tokens * HD, bytes_accessed=4 * tokens * HD, transcendentals=rows * tokens
    )
    whole = lambda i: (0, 0)
    return pl.pallas_call(
        functools.partial(attend_kernel, first, last),
        grid=(rows // block,),
        in_specs=[
            pl.BlockSpec((block, HD), lambda i: (i, 0)),
            pl.BlockSpec((tokens, HD), whole),
            pl.BlockSpec((tokens, HD), lambda i: (0, value_at)),
            pl.BlockSpec((1, block), lambda i: (0, i % wrap)),
            pl.BlockSpec((1, block), lambda i: (0, i % wrap)),
            pl.BlockSpec((1, tokens), whole),
        ]
        + ([] if first else [pl.BlockSpec((block, 2 * HD), lambda i: (i, 0))]),
        out_specs=[
            pl.BlockSpec((block, HD), lambda i: (i, 0)),
            pl.BlockSpec((8, block), lambda i: (0, i)),
        ]
        if last
        else pl.BlockSpec((block, 2 * HD), lambda i: (i, 0)),
        out_shape=[
            jax.ShapeDtypeStruct((rows, HD), F32),
            jax.ShapeDtypeStruct((8, rows), F32),
        ]
        if last
        else jax.ShapeDtypeStruct((rows, 2 * HD), F32),
        compiler_params=pltpu.CompilerParams(vmem_limit_bytes=14 * MIB),
        cost_estimate=cost,
    )(query, keys, values, qpos, qlow, kpos, *([] if first else [total]))


def attend_back_kernel(
    chunk, own, first, q_ref, g_ref, log_ref, qpos_ref, qlow_ref, k_ref, v_ref, kpos_ref,
    in_ref, extra_ref, dq_ref, dk_ref, dv_ref, *new_ref,
):
    rows = q_ref.shape[0]
    delta_ref = new_ref[0] if first else extra_ref

    @pl.when(pl.program_id(0) == 0)
    def _():
        if first:
            dq_ref[...] = jnp.zeros_like(dq_ref)
            for i in range(rows // chunk):
                at = pl.ds(i * chunk, chunk)
                product = g_ref[at, :].astype(F32) * in_ref[at, :]
                sums = jnp.sum(product.T, axis=0, keepdims=True)
                delta_ref[:, at] = jnp.broadcast_to(sums, (8, chunk))
        else:
            dq_ref[...] = in_ref[...]

    keys = k_ref[...]
    values = v_ref[...]
    kpos = jnp.broadcast_to(kpos_ref[...], (8, keys.shape[0])).T[:, :1]
    key_sum = jnp.zeros(keys.shape, F32)
    value_sum = jnp.zeros(keys.shape, F32)
    for i in range(rows // chunk):
        at = pl.ds(i * chunk, chunk)
        place = pl.ds((i * chunk) % own, chunk)
        query = q_ref[at, :]
        upstream = g_ref[at, :]
        scores = col_inner(keys, query)
        allowed = (kpos <= qpos_ref[:, place]) & (kpos >= qlow_ref[:, place])
        probs = jnp.where(allowed, jnp.exp2(scores * EXP2_SCALE - log_ref[0:1, at]), 0.0)
        prob_grad = col_inner(values, upstream)
        score_grad = (probs * (prob_grad - delta_ref[0:1, at])).astype(BF16)
        value_sum = value_sum + dot(probs.astype(BF16), upstream)
        key_sum = key_sum + dot(score_grad, query)
        dq_ref[at, :] += row_outer(score_grad, keys) * SCORE_SCALE
    dk_ref[...] = key_sum * SCORE_SCALE
    dv_ref[...] = value_sum


def attend_back(query, upstream, logs, qpos, qlow, keys, values, kpos, before, out):
    rows, tokens = query.shape[0], keys.shape[0]
    value_at = values.shape[1] // HD - 1
    own = qpos.shape[1]
    block = 512
    first = before is None
    cost = pl.CostEstimate(
        flops=32 * rows * tokens * HD, bytes_accessed=8 * tokens * HD, transcendentals=rows * tokens
    )
    whole = lambda i: (0, 0)
    taken = (out, logs) if first else before
    return pl.pallas_call(
        functools.partial(attend_back_kernel, 512, own, first),
        grid=(tokens // block,),
        in_specs=[
            pl.BlockSpec((rows, HD), whole),
            pl.BlockSpec((rows, HD), whole),
            pl.BlockSpec((8, rows), whole),
            pl.BlockSpec((1, own), whole),
            pl.BlockSpec((1, own), whole),
            pl.BlockSpec((block, HD), lambda i: (i, 0)),
            pl.BlockSpec((block, HD), lambda i: (i, value_at)),
            pl.BlockSpec((1, block), lambda i: (0, i)),
            pl.BlockSpec((rows, HD), whole),
            pl.BlockSpec((8, rows), whole),
        ],
        out_specs=[
            pl.BlockSpec((rows, HD), whole),
            pl.BlockSpec((block, HD), lambda i: (i, 0)),
            pl.BlockSpec((block, HD), lambda i: (i, 0)),
        ]
        + ([pl.BlockSpec((8, rows), whole)] if first else []),
        out_shape=[
            jax.ShapeDtypeStruct((rows, HD), F32),
            jax.ShapeDtypeStruct((tokens, HD), F32),
            jax.ShapeDtypeStruct((tokens, HD), F32),
        ]
        + ([jax.ShapeDtypeStruct((8, rows), F32)] if first else []),
        compiler_params=pltpu.CompilerParams(vmem_limit_bytes=18 * MIB),
        cost_estimate=cost,
    )(query, upstream, logs, qpos, qlow, keys, values, kpos, *taken)


def local(
    inputs,
    dealing,
    lengths,
    input_gain,
    w_query,
    w_key,
    w_value,
    query_gain,
    key_gain,
    w_out,
    hidden_gain,
    w_gate,
    w_up,
    w_down,
    cotangent,
):
    heads, blks = lax.axis_size("head"), lax.axis_size("blk")
    head, blk = lax.axis_index("head"), lax.axis_index("blk")
    shards = heads * blks
    chips = blks // 2
    chip, core = blk // 2, blk % 2
    shard = head * blks + blk
    rows, width = inputs.shape
    column = rows * blks
    pair = 2 * rows
    per_device = QH // blks
    query_rows, key_rows = w_query.shape[1], w_key.shape[1]
    qkv_rows = query_rows + 2 * key_rows
    in_pair = shards // KVH == heads and blks == 2 * heads

    gains = jnp.zeros((2 * width + 2 * HD,), F32)
    hidden_part = jnp.where(head == 0, hidden_gain.astype(F32), 0.0)
    for at, part in (
        (shard * input_gain.shape[0], input_gain),
        (width + blk * hidden_gain.shape[0], hidden_part),
        (2 * width + shard * query_gain.shape[0], query_gain),
        (2 * width + HD + shard * key_gain.shape[0], key_gain),
    ):
        gains = lax.dynamic_update_slice(gains, part.astype(F32), (at,))
    wire = Wire(inputs)

    index = jnp.stack(
        [
            (((chip - step) % chips) * 2 + (core ^ flip)) * heads + (head ^ place)
            for place in range(heads)
            for step in range(chips)
            for flip in range(2)
        ]
    )
    key_places, query_starts, cosine, sine = tables(
        index, lengths, dealing.reshape(blks * heads, rows), column, heads
    )
    query_places = key_places[:1]

    qkv_job = Job(
        plane_gather(jnp.concatenate([w_query.T, w_key.T, w_value.T], axis=0), False)
    )
    gain_job = Job(sum_everywhere(gains.reshape(-1, 128)))
    own_cotangent = lax.dynamic_slice_in_dim(cotangent, head * rows, rows, 0)
    cotangent_job = wire.add(ring_gather(own_cotangent))
    token_blocks = wire.drive(
        column_gather(inputs), riders=[qkv_job], hooks=[lambda: [gain_job]]
    )
    qkv_weights, gains = qkv_job.result, gain_job.result
    token_blocks = [part for parts in token_blocks for part in parts]
    gains = gains.reshape(-1)
    input_norm = gains[:width]
    hidden_norm = gains[width : 2 * width]
    query_norm = gains[2 * width : 2 * width + HD]
    key_norm = gains[2 * width + HD :]
    qkv_weights = jnp.concatenate(qkv_weights, axis=0)
    feed_rows, out_rows = w_down.shape[0], w_out.shape[0]
    out_weights = lax.all_gather(wire.tie(w_out)[0], "head", axis=0, tiled=True)
    column_values = jnp.concatenate(token_blocks, axis=0).astype(F32)
    normed_column = (column_values * rms_scale(column_values) * input_norm).astype(BF16)
    raw = col_inner(qkv_weights, normed_column).astype(BF16)
    wire.phase([], behind=True, along=[raw])
    raw = wire.along[0]
    norms = jnp.stack([query_norm, key_norm], axis=1)

    def reorder(value, index):
        cut = value.reshape(value.shape[:-1] + (blks, rows))
        return jnp.take(cut, index, axis=-2).reshape(value.shape)

    places = jnp.arange(blks)
    to_ring = ((chip - places // 2) % chips) * 2 + ((places % 2) ^ core)

    def gather_members(value):
        return reorder(lax.all_gather(reorder(value, to_ring), "blk", axis=0), to_ring)

    def exchange(pieces, behind=False):
        return [pieces[0]] + wire.phase(
            [(pieces[flip], member_move(flip)) for flip in range(1, heads)], behind
        )

    member = blk % heads
    odd = chip % 2
    if in_pair:
        pieces = exchange(split_blocks(head ^ member, [raw], heads))
        raw, query, key_value = rope_members(
            member, odd, pieces, cosine, sine, norms, rows, query_rows, key_rows
        )
    else:
        raw = raw.reshape(heads, qkv_rows, column)
        by_head = jnp.stack([pick(raw, head ^ place) for place in range(heads)])
        every = jnp.swapaxes(gather_members(by_head), 0, 1)
        every = every.reshape(shards, qkv_rows, column)
        query_all = every[:, :query_rows].reshape(QH, HD, column)
        key_all = every[:, query_rows : query_rows + key_rows].reshape(KVH, HD, column)
        value_all = every[:, query_rows + key_rows :].reshape(KVH, HD, column)
        query_raw = lax.dynamic_slice_in_dim(query_all, blk * per_device, per_device, 0)
        key_raw = pick(key_all, blk * KVH // blks)
        value_raw = pick(value_all, blk * KVH // blks)

        query = rope_forward(query_raw, query_norm, cosine, sine).astype(BF16)
        keys = rope_forward(key_raw, key_norm, cosine, sine).astype(BF16)
        query = jnp.swapaxes(query, 1, 2).reshape(per_device * column, HD)
        key_value = jnp.concatenate([keys.T, value_raw.T], axis=1)

    pairs = {0: key_value}
    key_pieces, value_pieces = dict(pairs), dict(pairs)
    total = None

    def add_column(place, total):
        return attend(
            query,
            key_pieces[place],
            value_pieces[place],
            query_places,
            query_starts,
            key_places[place : place + 1],
            total,
            place == heads - 1,
        )

    ready = [0]
    for forward, backward in zip(plane_steps(False), plane_steps(True)):
        if forward == backward:
            items = [(pairs[source], head_move(bit)) for place, source, bit in forward]
        else:
            items = [
                (key_pieces[source][:, :HD], head_move(bit)) for place, source, bit in forward
            ] + [(value_pieces[source][:, -HD:], head_move(bit)) for place, source, bit in backward]
        for place in ready:
            total = add_column(place, total)
        got = wire.phase(items, behind=True, along=[total])
        total = wire.along[0]
        if ready == [0]:
            late = wire.tie(jnp.concatenate([w_gate.T, w_up.T, w_down], axis=0))[0]
        ready = [place for place, source, bit in forward]
        for index, place in enumerate(ready):
            key_pieces[place] = got[index]
            if forward == backward:
                value_pieces[place] = pairs[place] = got[index]
            else:
                value_pieces[backward[index][0]] = got[len(forward) + index]
    for place in ready:
        total = add_column(place, total)
    heads_out, logs = total

    if in_pair:
        pieces = exchange(mixed_members(member, heads_out, heads, column), True)
        mixed = join_members(member, odd, pieces, rows).reshape(heads * out_rows, column)
    else:
        mixed_heads = jnp.swapaxes(heads_out.astype(BF16).reshape(per_device, column, HD), 1, 2)
        every = gather_members(mixed_heads)
        every = every.reshape(heads, blks, out_rows, column)
        mixed = lax.dynamic_index_in_dim(every, blk, 1).reshape(heads * out_rows, column)
    branch_parts = row_outer(mixed, out_weights)
    branch = wire.drive(
        column_scatter(lambda step: branch_parts[step * pair : (step + 1) * pair])
    )
    while wire.jobs:
        wire.phase([], behind=True)
    token_values = inputs.astype(F32)
    middle = token_values + branch
    scale_two = rms_scale(middle)
    hidden_in = (middle * scale_two * hidden_norm).astype(BF16)

    late = lax.all_gather(late, "head", axis=0)
    hidden_parts = {}
    feed_groups = []
    near = chips // 2
    groups = [sorted({hop, (chips - hop) % chips}) for hop in range(near + 1)]

    def group_pieces(index, parts):
        return [part for step in groups[index] for part in parts[step]]

    feed_weights = []

    def feed_group(index):
        tokens = jnp.concatenate(group_pieces(index, hidden_parts), axis=0)
        upstream = jnp.concatenate(group_pieces(index, cotangent_job.result), axis=0)
        gate_weights, up_weights, down_weights = feed_weights
        act_grad = col_inner(upstream, down_weights)
        gate = col_inner(tokens, gate_weights)
        up_proj = col_inner(tokens, up_weights)
        sigmoid_gate = jax.nn.sigmoid(gate)
        silu_gate = gate * sigmoid_gate
        activated = (silu_gate * up_proj).astype(BF16)
        gate_grad = (
            act_grad * up_proj * sigmoid_gate * (1.0 + gate * (1.0 - sigmoid_gate))
        ).astype(BF16)
        up_grad = (act_grad * silu_gate).astype(BF16)
        back = dot(gate_grad, gate_weights) + dot(up_grad, up_weights)
        down = dot(activated, down_weights)
        feed_groups.append((activated, gate_grad, up_grad, back, down))

    def start_feed():
        feed_weights.extend(wire.along)

    def keep_first():
        feed_group(0)
        feed_groups[0] = wire.tie(*feed_groups[0])

    wire.drive(
        column_gather(hidden_in, hidden_parts),
        hooks=[start_feed, keep_first],
        along=[
            late[:, i * feed_rows : (i + 1) * feed_rows].reshape(-1, width) for i in range(3)
        ],
    )
    for index in range(1, near + 1):
        feed_group(index)

    def group_rows(index, step):
        group = min(step, chips - step)
        at = groups[group].index(step) * pair
        return feed_groups[group][index][at : at + pair]

    hidden_pieces = sum((group_pieces(index, hidden_parts) for index in range(near + 1)), [])
    upstream_pieces = sum(
        (group_pieces(index, cotangent_job.result) for index in range(near + 1)), []
    )
    down_grads = weight_grads([group[0] for group in feed_groups], upstream_pieces, heads, 2, None)
    gate_grads = weight_grads([group[1] for group in feed_groups], hidden_pieces, heads, 0, down_grads)
    feed_grads = [gate_grads]

    def keep_grads():
        downs = [group[4].astype(BF16) for group in feed_groups]
        feed_grads[0], *downs = wire.tie(feed_grads[0], *downs)
        for index, down in enumerate(downs):
            feed_groups[index] = tuple(feed_groups[index][:4]) + (down,)

    def keep_last():
        feed_grads[0] = wire.tie(
            weight_grads([group[2] for group in feed_groups], hidden_pieces, heads, 1, feed_grads[0])
        )[0]

    hidden_grad = wire.drive(
        column_scatter(lambda step: group_rows(3, step), apart=True),
        hooks=[lambda: None] * (near + 1) + [keep_grads],
    )
    hidden_gain_grad = jnp.sum(hidden_grad * middle * scale_two, axis=0)
    middle_grad = own_cotangent.astype(F32) + norm_back(hidden_grad, middle, scale_two, hidden_norm)
    branch_grad = middle_grad.astype(BF16)
    branch_blocks = join_blocks(wire.drive(column_gather(branch_grad), hooks=[keep_last]))
    down_job = wire.add(column_scatter(lambda step: group_rows(4, step)))
    feed_grads = lax.psum_scatter(feed_grads[0], "head", scatter_dimension=0).astype(F32)
    mixed_grads = [col_inner(out_weights, block).astype(BF16) for block in branch_blocks]
    grad_out = dot(mixed, jnp.concatenate(branch_blocks, axis=0)).reshape(heads, out_rows, width)
    out_parts = [pick(grad_out, head ^ place) for place in range(heads)]
    if in_pair:
        pieces = exchange(split_blocks(member, mixed_grads, heads), True)
        upstream = upstream_members(member, odd, pieces, rows)
    else:
        mixed_grad = jnp.concatenate(mixed_grads, axis=1).reshape(heads, out_rows, column)
        every = gather_members(mixed_grad)
        every = jnp.swapaxes(every, 0, 1).reshape(blks, per_device, HD, column)
        upstream = jnp.swapaxes(pick(every, blk), 1, 2).reshape(per_device * column, HD)

    key_grads, value_grads = {}, {}
    carry = None
    for forward, backward in zip(plane_steps(False)[::-1] + [[]], plane_steps(True)[::-1] + [[]]):
        for place in [step[0] for step in forward] if forward else [0]:
            results = attend_back(
                query,
                upstream,
                logs,
                query_places,
                query_starts,
                key_pieces[place],
                value_pieces[place],
                key_places[place : place + 1],
                carry,
                heads_out,
            )
            key_grads[place] = key_grads.get(place, 0.0) + results[1]
            value_grads[place] = value_grads.get(place, 0.0) + results[2]
            carry = (results[0], carry[1] if carry else results[3])
        if not forward:
            break
        if forward == backward:
            items = [
                (
                    jnp.concatenate([key_grads[place], value_grads[place]], axis=1).astype(BF16),
                    head_move(bit),
                )
                for place, source, bit in forward
            ]
        else:
            items = [
                (key_grads[place].astype(BF16), head_move(bit)) for place, source, bit in forward
            ] + [
                (value_grads[place].astype(BF16), head_move(bit))
                for place, source, bit in backward
            ]
        tied = lax.optimization_barrier(tuple(value for value, move in items) + carry)
        items = [(value, move) for value, (ignored, move) in zip(tied, items)]
        carry = tied[len(items) :]
        got = wire.phase(items, behind=True)
        last_parts = got
        if forward[0][1] == 0:
            continue
        for index, (place, source, bit) in enumerate(forward):
            part = got[index][:, :HD].astype(F32)
            key_grads[source] = key_grads.get(source, 0.0) + part
        for index, (place, source, bit) in enumerate(backward):
            part = got[index if forward == backward else len(forward) + index]
            value_grads[source] = value_grads.get(source, 0.0) + part[:, -HD:].astype(F32)
    query_grad = carry[0]

    if in_pair:
        *pieces, gain_grads = rope_back_members(
            member, raw, query_grad, cosine, sine, norms, key_grads[0], value_grads[0], last_parts,
            query_rows, key_rows,
        )
        pieces = exchange(pieces, True)
        raw_grad = join_members(head ^ member, odd, pieces, rows).reshape(-1, column)
    else:
        key_grad = key_grads[0] + sum(part[:, :HD].astype(F32) for part in last_parts)
        value_grad = value_grads[0] + sum(part[:, HD:].astype(F32) for part in last_parts)
        query_grad = jnp.swapaxes(query_grad.reshape(per_device, column, HD), 1, 2)
        query_raw_grad, query_gain_grad = rope_backward(
            query_raw, query_norm, cosine, sine, query_grad
        )
        key_raw_grad, key_gain_grad = rope_backward(key_raw, key_norm, cosine, sine, key_grad.T)
        query_raw_grad = query_raw_grad.astype(BF16)
        key_raw_grad = key_raw_grad.astype(BF16)
        value_raw_grad = value_grad.T.astype(BF16)
        gain_grads = jnp.stack([jnp.sum(query_gain_grad, axis=0), key_gain_grad], axis=1)

        def spread(part, count, index):
            empty = jnp.zeros((count,) + part.shape[1:], BF16)
            return lax.dynamic_update_slice_in_dim(empty, part, index, 0)

        every = jnp.concatenate(
            [
                spread(query_raw_grad, QH, blk * per_device).reshape(shards, query_rows, column),
                spread(key_raw_grad[None], KVH, blk * KVH // blks).reshape(
                    shards, key_rows, column
                ),
                spread(value_raw_grad[None], KVH, blk * KVH // blks).reshape(
                    shards, key_rows, column
                ),
            ],
            axis=1,
        ).reshape(heads, blks, qkv_rows, column)
        every = reorder(jnp.swapaxes(every, 0, 1), to_ring)
        by_head = reorder(lax.psum_scatter(every, "blk", scatter_dimension=0), to_ring)
        raw_grad = jnp.concatenate(
            [pick(by_head, head ^ place) for place in range(heads)], axis=0
        )

    while down_job.wanted is not None:
        wire.phase([], behind=True)
    done = [feed_grads, (middle + down_job.result).astype(BF16)]

    qkv_grad = dot(raw_grad, normed_column)
    input_gain_grad = jnp.sum(qkv_grad * qkv_weights.astype(F32), axis=0) / input_norm
    sums = jnp.concatenate([input_gain_grad, hidden_gain_grad, gain_grads[:, 0], gain_grads[:, 1]])
    qkv_grad = qkv_grad.reshape(heads, qkv_rows, width)
    out_job = Job(plane_scatter(out_parts, True, pause=True))
    tail = [
        Job(sum_everywhere(sums.reshape(-1, 128))),
        Job(plane_scatter(list(qkv_grad), False)),
        out_job,
    ]

    def keep_done():
        done[:] = wire.tie(*done)

    normed_grad = wire.drive(
        ring_scatter(
            lambda step: row_outer(raw_grad[:, step * pair : (step + 1) * pair], qkv_weights)
        ),
        hooks=[lambda: tail] + [lambda: None] * (chips - 3) + [keep_done],
    )
    sums, grad_tail, grad_out = tail[0].result.reshape(-1), tail[1].result, out_job.result
    feed_grads, layer_out = done
    grad_gate, grad_up, grad_down = (
        feed_grads[i * feed_rows : (i + 1) * feed_rows] for i in range(3)
    )
    token_values = wire.token.astype(F32)
    grad_input = middle_grad + norm_back(
        normed_grad, token_values, rms_scale(token_values), input_norm
    )

    def own_part(at, size):
        return lax.dynamic_slice_in_dim(sums, at, size)

    return (
        layer_out,
        grad_input,
        own_part(shard * input_gain.shape[0], input_gain.shape[0]),
        grad_tail[:query_rows].T,
        grad_tail[query_rows : query_rows + key_rows].T,
        grad_tail[query_rows + key_rows :].T,
        own_part(2 * width + shard * query_gain.shape[0], query_gain.shape[0]),
        own_part(2 * width + HD + shard * key_gain.shape[0], key_gain.shape[0]),
        grad_out,
        own_part(width + blk * hidden_gain.shape[0], hidden_gain.shape[0]),
        grad_gate.T,
        grad_up.T,
        grad_down,
    )


def solution(mesh):
    return jax.shard_map(
        local,
        mesh=mesh,
        in_specs=(
            P(("blk", "head"), None),
            P(),
            P(),
            P(("head", "blk")),
            P(None, ("head", "blk")),
            P(None, ("head", "blk")),
            P(None, ("head", "blk")),
            P(("head", "blk")),
            P(("head", "blk")),
            P(("head", "blk"), None),
            P("blk"),
            P(None, ("head", "blk")),
            P(None, ("head", "blk")),
            P(("head", "blk"), None),
            P("blk", None),
        ),
        out_specs=(
            P(("blk", "head"), None),
            P(("blk", "head"), None),
            P(("head", "blk")),
            P(None, ("head", "blk")),
            P(None, ("head", "blk")),
            P(None, ("head", "blk")),
            P(("head", "blk")),
            P(("head", "blk")),
            P(("head", "blk"), None),
            P("blk"),
            P(None, ("head", "blk")),
            P(None, ("head", "blk")),
            P(("head", "blk"), None),
        ),
        check_vma=False,
    )
```

```python
import functools
import math

import jax
import jax.numpy as jnp
import numpy as np
from jax import lax
from jax.experimental import pallas as pl
from jax.experimental.pallas import tpu as pltpu
from jax.sharding import PartitionSpec as P

QH = 16
KVH = 8
HD = 128
HALF = HD // 2
EPSILON = 1e-06
ROPE_BASE = 1000000.0
SCORE_SCALE = HD ** (-0.5)
EXP2_SCALE = SCORE_SCALE * math.log2(math.e)
CONTRACT_ROWS = (((0,), (0,)), ((), ()))
CONTRACT_COLS = (((1,), (1,)), ((), ()))
BF16 = jnp.bfloat16
F32 = jnp.float32
MIB = 1024 * 1024


def dot(left, right):
    return jnp.dot(left, right, preferred_element_type=F32)


def row_outer(left, right):
    return lax.dot_general(left, right, CONTRACT_ROWS, preferred_element_type=F32)


def col_inner(left, right):
    return lax.dot_general(left, right, CONTRACT_COLS, preferred_element_type=F32)


def rms_scale(values):
    return lax.rsqrt(jnp.mean(values * values, axis=-1, keepdims=True) + EPSILON)


def norm_back(upstream, source, scale_rows, gain):
    scaled = upstream * gain
    return scale_rows * scaled - source * scale_rows**3 * jnp.mean(
        scaled * source, axis=-1, keepdims=True
    )


def head_bits():
    count = lax.axis_size("head")
    return [1 << i for i in range(count.bit_length() - 1)]


def head_move(bit):
    count = lax.axis_size("head")
    return ("head", [(i, i ^ bit) for i in range(count)], bit)


def blk_move(steps, flip, link):
    count = lax.axis_size("blk")
    return ("blk", [(i, ((i + 2 * steps) % count) ^ flip) for i in range(count)], link)


def swap_move():
    return blk_move(0, 1, None)


def ring_move(steps):
    return blk_move(steps, 0, "z")


def member_move(flip):
    count = lax.axis_size("blk")
    return ("blk", [(i, i ^ flip) for i in range(count)], "z" if flip > 1 else None)


class Job:
    def __init__(self, steps):
        self.steps = steps
        self.wanted = None
        self.result = None
        self.advance(None)

    def advance(self, got):
        try:
            self.wanted = self.steps.send(got)
        except StopIteration as end:
            self.wanted = None
            self.result = end.value


class Wire:
    def __init__(self, token):
        self.token = token
        self.jobs = []

    def add(self, steps):
        job = Job(steps)
        self.jobs.append(job)
        return job

    def tie(self, *arrays):
        *arrays, self.token = lax.optimization_barrier(arrays + (self.token,))
        return arrays

    def phase(self, items, behind=False, riders=(), along=()):
        items = list(items)
        count = len(items)
        taken = []
        for job in list(riders) + (self.jobs if behind else []):
            if job.wanted is not None:
                taken.append((job, len(items), len(items) + len(job.wanted)))
                items.extend(job.wanted)
        if not items:
            for job, start, end in taken:
                job.advance([])
            return []
        values = self.tie(*[value for value, move in items])
        outs = [lax.ppermute(value, move[0], move[1]) for value, (same, move) in zip(values, items)]
        outs = self.tie(*outs, *along)
        self.along = outs[len(items) :]
        for job, start, end in taken:
            job.advance(outs[start:end])
        self.jobs = [job for job in self.jobs if job.wanted is not None]
        return outs[:count]

    def drive(self, steps, hooks=(), riders=(), behind=None, along=()):
        job = Job(steps)
        riders = list(riders)
        hooks = list(hooks)
        count = 0
        while job.wanted is not None or any(rider.wanted is not None for rider in riders):
            got = self.phase(
                job.wanted or [],
                riders=riders,
                behind=behind is not None and count >= behind,
                along=() if count else along,
            )
            if job.wanted is not None:
                job.advance(got)
            if hooks:
                riders.extend(hooks.pop(0)() or [])
            count += 1
        return job.result


def column_gather(value, blocks=None):
    chips = lax.axis_size("blk") // 2
    near = chips // 2
    blocks = {} if blocks is None else blocks
    fresh = {0: value}
    up = down = value
    for hop in range(1, near + 2):
        items = [(part, swap_move()) for part in fresh.values()]
        if hop <= near:
            items.append((up, ring_move(1)))
        if hop <= chips - 1 - near:
            items.append((down, ring_move(-1)))
        got = yield items
        for (step, part), other in zip(fresh.items(), got):
            blocks[step] = [part, other]
        got = got[len(fresh) :]
        fresh = {}
        if got:
            up = fresh[hop] = got[0]
        if len(got) > 1:
            down = fresh[chips - hop] = got[1]
    return [blocks[step] for step in range(chips)]


def ring_gather(value):
    chips = lax.axis_size("blk") // 2
    blocks = []
    for step in range(chips):
        items = [(value, swap_move())]
        if step < chips - 1:
            items.append((value, ring_move(1)))
        got = yield items
        blocks.append([value, got[0]])
        value = got[-1]
    return blocks


def ring_scatter(part_of):
    chips = lax.axis_size("blk") // 2
    order = list(range(1, chips)) + [0]

    def halves(step):
        part = part_of(step)
        rows = part.shape[0] // 2
        return part[:rows], part[rows:]

    own, other = halves(order[0])
    got = yield [(other.astype(BF16), swap_move())]
    total = own.astype(F32) + got[0].astype(F32)
    for step in order[1:]:
        own, other = halves(step)
        got = yield [(total.astype(BF16), ring_move(1)), (other.astype(BF16), swap_move())]
        total = own.astype(F32) + got[1].astype(F32) + got[0].astype(F32)
    return total


def join_blocks(blocks):
    return [jnp.concatenate(block, axis=0) for block in blocks]


def column_scatter(part_of, apart=False):
    chips = lax.axis_size("blk") // 2
    near = chips // 2
    totals = {}

    def swaps(steps):
        parts = {step: part_of(step) for step in steps}
        half = parts[steps[0]].shape[0] // 2
        items = [(parts[step][half:].astype(BF16), swap_move()) for step in steps]
        return items, {step: part[:half] for step, part in parts.items()}

    def add(own, got):
        for (step, part), other in zip(own.items(), got):
            totals[step] = part.astype(F32) + other.astype(F32) + totals.get(step, 0.0)

    items, own = swaps([near])
    add(own, (yield items))
    for hop in range(near, 0, -1):
        both = hop <= chips - 1 - near
        moves = [(totals[hop].astype(BF16), ring_move(-1))]
        if both:
            moves.append((totals[chips - hop].astype(BF16), ring_move(1)))
        steps = sorted({hop - 1, (chips - hop + 1) % chips})
        if apart:
            got = yield moves
            items, own = swaps(steps)
            add(own, (yield items))
            apart = False
        else:
            items, own = swaps(steps)
            got = yield moves + items
            add(own, got[len(moves) :])
        totals[hop - 1] = totals[hop - 1] + got[0].astype(F32)
        if both:
            step = (chips - hop + 1) % chips
            totals[step] = totals[step] + got[1].astype(F32)
    return totals[0]


def plane_steps(backwards):
    bits = head_bits()
    order = bits[::-1] if backwards else bits
    steps = []
    for weight in range(1, len(bits) + 1):
        step = []
        for place in range(1 << len(bits)):
            if bin(place).count("1") == weight:
                last = [bit for bit in order if place & bit][-1]
                step.append((place, place ^ last, last))
        steps.append(step)
    return steps


def plane_gather(value, backwards):
    pieces = {0: value}
    for step in plane_steps(backwards):
        got = yield [(pieces[source], head_move(bit)) for place, source, bit in step]
        for (place, source, bit), piece in zip(step, got):
            pieces[place] = piece
    return [pieces[i] for i in range(len(pieces))]


def plane_scatter(parts, backwards, pause=False):
    pieces = list(parts)
    for index, step in enumerate(plane_steps(backwards)[::-1]):
        if pause and index == 1:
            yield []
        got = yield [(pieces[place].astype(BF16), head_move(bit)) for place, source, bit in step]
        for (place, source, bit), piece in zip(step, got):
            pieces[source] = pieces[source] + piece.astype(F32)
    return pieces[0]


def sum_everywhere(value):
    chips = lax.axis_size("blk") // 2
    for moves in (
        *([head_move(bit)] for bit in head_bits()),
        [swap_move()],
        [blk_move(steps, 0, None) for steps in range(1, chips)],
    ):
        got = yield [(value, move) for move in moves]
        for part in got:
            value = value + part
    return value


def pick(stack, index):
    return lax.dynamic_index_in_dim(stack, index, 0, keepdims=False)


def token_starts(anchors, lengths):
    ends = jnp.cumsum(lengths)
    seq_starts = ends - lengths
    inside = seq_starts[None, :] <= anchors[:, None]
    return jnp.max(jnp.where(inside, seq_starts[None, :], 0), axis=1)


def rope_tables(places):
    ladder = jnp.arange(HALF, dtype=F32)
    rates = jnp.exp(ladder * (-2.0 * math.log(ROPE_BASE) / HD))
    angles = rates[:, None] * places.astype(F32)[None, :]
    return (jnp.cos(angles), jnp.sin(angles))


def rope_forward(raw, gain, cosine, sine):
    heads = raw.astype(F32)
    scale = lax.rsqrt(jnp.mean(heads * heads, axis=-2, keepdims=True) + EPSILON)
    normed = heads * scale * gain[:, None]
    low, high = normed[..., :HALF, :], normed[..., HALF:, :]
    return jnp.concatenate([low * cosine - high * sine, high * cosine + low * sine], axis=-2)


def rope_backward(raw, gain, cosine, sine, upstream):
    heads = raw.astype(F32)
    scale = lax.rsqrt(jnp.mean(heads * heads, axis=-2, keepdims=True) + EPSILON)
    low, high = upstream[..., :HALF, :], upstream[..., HALF:, :]
    turned = jnp.concatenate([low * cosine + high * sine, high * cosine - low * sine], axis=-2)
    gain_grad = jnp.sum(turned * heads * scale, axis=-1)
    scaled = turned * gain[:, None]
    back = scale * scaled - heads * scale**3 * jnp.mean(scaled * heads, axis=-2, keepdims=True)
    return back, gain_grad


def small_call(kernel, outs, scalars, arrays, scratch=()):
    vmem = pl.BlockSpec(memory_space=pltpu.VMEM)
    return pl.pallas_call(
        kernel,
        in_specs=[pl.BlockSpec(memory_space=pltpu.SMEM)] + [vmem] * len(arrays),
        out_specs=[vmem] * len(outs),
        out_shape=[jax.ShapeDtypeStruct(shape, dtype) for shape, dtype in outs],
        scratch_shapes=[pltpu.VMEM(shape, dtype) for shape, dtype in scratch],
        compiler_params=pltpu.CompilerParams(vmem_limit_bytes=10 * MIB),
        cost_estimate=pl.CostEstimate(
            flops=0,
            bytes_accessed=3 * sum(array.size * array.dtype.itemsize for array in arrays),
            transcendentals=0,
        ),
    )(scalars, *arrays)


def table_kernel(blocks, sequences, index_ref, deal_ref, rate_ref, key_ref, start_ref, cos_ref, sin_ref):
    heads, column = key_ref.shape
    rows = column // blocks
    for place in range(heads):
        for block in range(blocks):
            row = deal_ref[pl.ds(index_ref[place * blocks + block], 1), :]
            key_ref[place : place + 1, block * rows : (block + 1) * rows] = row
    own = key_ref[0:1, :]
    starts = jnp.zeros_like(own)
    first = jnp.int32(0)
    for sequence in range(sequences - 1):
        first = first + index_ref[heads * blocks + sequence]
        starts = jnp.where(own >= first, first, starts)
    start_ref[...] = starts
    angles = rate_ref[:, :1] * (own - starts).astype(F32)
    cos_ref[...] = jnp.cos(angles)
    sin_ref[...] = jnp.sin(angles)


def tables(index, lengths, deals, column, heads):
    rates = np.exp(
        np.arange(HALF, dtype=np.float32) * np.float32(-2.0 * math.log(ROPE_BASE) / HD)
    ).astype(np.float32)
    return small_call(
        functools.partial(table_kernel, column // deals.shape[1], lengths.shape[0]),
        [
            ((heads, column), jnp.int32),
            ((1, column), jnp.int32),
            ((HALF, column), F32),
            ((HALF, column), F32),
        ],
        jnp.concatenate([index, lengths]),
        [deals, jnp.asarray(np.broadcast_to(rates[:, None], (HALF, 128)))],
    )


def put_in_order(out_ref, scalar_ref, pieces, rows, finish):
    base = scalar_ref[0]
    for flip, piece in enumerate(pieces):
        value = piece[...]
        column = value.shape[1]
        if flip & 1:
            cuts = [value[:, i * rows : (i + 1) * rows] for i in range(column // rows)]
            value = jnp.concatenate([cuts[i ^ 1] for i in range(column // rows)], axis=1)
        at = pl.ds(base ^ flip, 1)
        if flip & 2:
            pair = 2 * rows

            @pl.when(scalar_ref[1] == 0)
            def _(at=at, value=value, pair=pair):
                out_ref[at] = jnp.concatenate([value[:, pair:], value[:, :pair]], axis=1)[None]

            @pl.when(scalar_ref[1] != 0)
            def _(at=at, value=value, pair=pair):
                out_ref[at] = jnp.concatenate([value[:, -pair:], value[:, :-pair]], axis=1)[None]

        else:
            out_ref[at] = value[None]
    finish()


def join_members(base, odd, pieces, rows):
    count = len(pieces)

    def kernel(scalar_ref, *refs):
        put_in_order(refs[count], scalar_ref, refs[:count], rows, lambda: None)

    return small_call(
        kernel,
        [((count,) + pieces[0].shape, BF16)],
        jnp.stack([base, odd]).astype(jnp.int32),
        pieces,
    )[0]


def split_blocks(base, blocks, count):
    size = blocks[0].shape[0] // count
    width = blocks[0].shape[1]

    def kernel(scalar_ref, *refs):
        for flip in range(count):
            start = pl.multiple_of((scalar_ref[0] ^ flip) * size, size)
            for index in range(len(blocks)):
                refs[len(blocks) + flip][:, index * width : (index + 1) * width] = refs[index][
                    pl.ds(start, size), :
                ]

    return small_call(
        kernel,
        [((size, width * len(blocks)), BF16)] * count,
        base.reshape(1).astype(jnp.int32),
        blocks,
    )


def rope_kernel(rows, query_rows, key_rows, scalar_ref, *refs):
    pieces = refs[:-6]
    cos_ref, sin_ref, gain_ref, raw_ref, query_ref, pair_ref = refs[-6:]
    count, column = len(pieces), cos_ref.shape[1]
    put_in_order(raw_ref, scalar_ref, pieces, rows, lambda: None)
    cosine, sine = cos_ref[...], sin_ref[...]

    def rotate(parts, gain):
        heads = jnp.concatenate(parts, axis=0).astype(F32)
        scale = lax.rsqrt(jnp.mean(heads * heads, axis=0, keepdims=True) + EPSILON)
        normed = heads * scale * gain
        low, high = normed[:HALF], normed[HALF:]
        turned = jnp.concatenate([low * cosine - high * sine, high * cosine + low * sine], axis=0)
        return turned

    per_head = HD // query_rows
    for head in range(count // per_head):
        parts = [raw_ref[head * per_head + i, :query_rows, :] for i in range(per_head)]
        turned = rotate(parts, gain_ref[:, 0:1]) * EXP2_SCALE
        query_ref[head * column : (head + 1) * column, :] = turned.T.astype(BF16)
    parts = [raw_ref[i, query_rows : query_rows + key_rows, :] for i in range(count)]
    pair_ref[:, :HD] = rotate(parts, gain_ref[:, 1:2]).T.astype(BF16)
    parts = [raw_ref[i, query_rows + key_rows :, :] for i in range(count)]
    pair_ref[:, HD:] = jnp.concatenate(parts, axis=0).astype(F32).T.astype(BF16)


def rope_members(base, odd, pieces, cosine, sine, gains, rows, query_rows, key_rows):
    count, column = len(pieces), cosine.shape[1]
    return small_call(
        functools.partial(rope_kernel, rows, query_rows, key_rows),
        [
            ((count,) + pieces[0].shape, BF16),
            ((count * query_rows // HD * column, HD), BF16),
            ((column, 2 * HD), BF16),
        ],
        jnp.stack([base, odd]).astype(jnp.int32),
        list(pieces) + [cosine, sine, gains],
    )


def mixed_kernel(scalar_ref, in_ref, *refs):
    outs, parts_ref = refs[:-1], refs[-1]
    count, size, column = parts_ref.shape
    for head in range(in_ref.shape[0] // column):
        part = in_ref[head * column : (head + 1) * column, :].T.astype(BF16)
        per_head = HD // size
        for i in range(per_head):
            parts_ref[head * per_head + i] = part[i * size : (i + 1) * size]
    for flip, out_ref in enumerate(outs):
        out_ref[...] = parts_ref[scalar_ref[0] ^ flip]


def mixed_members(base, heads_out, count, column):
    size = heads_out.shape[0] // column * HD // count
    return small_call(
        mixed_kernel,
        [((size, column), BF16)] * count,
        base.reshape(1).astype(jnp.int32),
        [heads_out],
        [((count, size, column), BF16)],
    )


def upstream_members(base, odd, pieces, rows):
    count = len(pieces)
    size, column = pieces[0].shape
    per_head = HD // size

    def kernel(scalar_ref, *refs):
        out_ref, parts_ref = refs[count:]
        put_in_order(parts_ref, scalar_ref, refs[:count], rows, lambda: None)
        for head in range(count // per_head):
            parts = [parts_ref[head * per_head + i] for i in range(per_head)]
            out_ref[head * column : (head + 1) * column, :] = (
                jnp.concatenate(parts, axis=0).astype(F32).T.astype(BF16)
            )

    return small_call(
        kernel,
        [((count // per_head * column, HD), BF16)],
        jnp.stack([base, odd]).astype(jnp.int32),
        pieces,
        [((count, size, column), BF16)],
    )[0]


def light():
    return pl.CostEstimate(flops=1, bytes_accessed=1, transcendentals=0)


def weight_grad_kernel(count, groups, *refs):
    pieces, lefts = refs[:count], refs[count : count + groups]
    out_ref, right_ref = refs[-2:]
    rows = pieces[0].shape[0]

    @pl.when(pl.program_id(0) == 0)
    def _():
        for index in range(count):
            right_ref[index * rows : (index + 1) * rows, :] = pieces[index][...]

    size = out_ref.shape[1]
    for head in range(lefts[0].shape[1] // size):

        @pl.when(pl.program_id(0) == head)
        def _(head=head):
            cut = slice(head * size, (head + 1) * size)
            left = jnp.concatenate([ref[:, cut] for ref in lefts], axis=0)
            out_ref[0] = row_outer(left, right_ref[...]).astype(BF16)


def weight_grads(lefts, pieces, heads, kind, into):
    size = lefts[0].shape[1] // heads
    piece, width = pieces[0].shape
    count = len(pieces)
    specs = [pl.BlockSpec((piece, width), lambda i: (0, 0))] * count
    specs += [pl.BlockSpec(left.shape, lambda i: (0, 0)) for left in lefts]
    operands = list(pieces) + list(lefts)
    aliases = {}
    if into is not None:
        specs.append(pl.BlockSpec(memory_space=pl.ANY))
        aliases = {len(operands): 0}
        operands.append(into)
    return pl.pallas_call(
        functools.partial(weight_grad_kernel, count, len(lefts)),
        grid=(heads,),
        in_specs=specs,
        out_specs=pl.BlockSpec((1, size, width), lambda i: (i, kind, 0)),
        out_shape=jax.ShapeDtypeStruct((heads, 3 * size, width), BF16),
        scratch_shapes=[pltpu.VMEM((count * piece, width), BF16)],
        input_output_aliases=aliases,
        compiler_params=pltpu.CompilerParams(vmem_limit_bytes=20 * MIB),
        cost_estimate=light(),
    )(*operands)


def rope_back_kernel(query_rows, key_rows, count, scalar_ref, *refs):
    raw_ref, dq_ref, cos_ref, sin_ref, gain_ref, dk_ref, dv_ref = refs[:7]
    more = refs[7 : -2 - count]
    outs, gain_out, parts_ref = refs[-2 - count : -2], refs[-2], refs[-1]
    column = cos_ref.shape[1]
    cosine, sine = cos_ref[...], sin_ref[...]

    def back(parts, gain, upstream):
        heads = jnp.concatenate(parts, axis=0).astype(F32)
        scale = lax.rsqrt(jnp.mean(heads * heads, axis=0, keepdims=True) + EPSILON)
        low, high = upstream[:HALF], upstream[HALF:]
        turned = jnp.concatenate([low * cosine + high * sine, high * cosine - low * sine], axis=0)
        gain_grad = jnp.sum(turned * heads * scale, axis=1, keepdims=True)
        scaled = turned * gain
        mean = jnp.mean(scaled * heads, axis=0, keepdims=True)
        return (scale * scaled - heads * (scale * scale * scale * mean)).astype(BF16), gain_grad

    per_head = HD // query_rows
    total = jnp.zeros((HD, 1), F32)
    for head in range(count // per_head):
        at = [head * per_head + i for i in range(per_head)]
        grad, gain_grad = back(
            [raw_ref[i, :query_rows, :] for i in at],
            gain_ref[:, 0:1],
            dq_ref[head * column : (head + 1) * column, :].T,
        )
        total = total + gain_grad
        for place, i in enumerate(at):
            parts_ref[i, :query_rows, :] = grad[place * query_rows : (place + 1) * query_rows]
    gain_out[:, 0:1] = total
    key_grad, value_grad = dk_ref[...], dv_ref[...]
    for ref in more:
        key_grad = key_grad + ref[:, :HD].astype(F32)
        value_grad = value_grad + ref[:, HD:].astype(F32)
    grad, gain_grad = back(
        [raw_ref[i, query_rows : query_rows + key_rows, :] for i in range(count)],
        gain_ref[:, 1:2],
        key_grad.T,
    )
    gain_out[:, 1:2] = gain_grad
    value_grad = value_grad.T.astype(BF16)
    for i in range(count):
        cut = slice(i * key_rows, (i + 1) * key_rows)
        parts_ref[i, query_rows : query_rows + key_rows, :] = grad[cut]
        parts_ref[i, query_rows + key_rows :, :] = value_grad[cut]
    for flip, out_ref in enumerate(outs):
        out_ref[...] = parts_ref[scalar_ref[0] ^ flip]


def rope_back_members(base, raw, dq, cosine, sine, gains, dk, dv, more, query_rows, key_rows):
    count, size, column = raw.shape
    return small_call(
        functools.partial(rope_back_kernel, query_rows, key_rows, count),
        [((size, column), BF16)] * count + [((HD, 2), F32)],
        base.reshape(1).astype(jnp.int32),
        [raw, dq, cosine, sine, gains, dk, dv] + list(more),
        [((count, size, column), BF16)],
    )


def attend_kernel(first, last, *refs):
    refs = list(refs)
    q_ref, k_ref, v_ref, qpos_ref, qlow_ref, kpos_ref = refs[:6]
    outs = refs[6:] if first else refs[7:]
    kpos = kpos_ref[...]
    scores = col_inner(q_ref[...], k_ref[...])
    rows = q_ref.shape[0]
    qpos = jnp.broadcast_to(qpos_ref[...], (8, rows)).T[:, :1]
    qlow = jnp.broadcast_to(qlow_ref[...], (8, rows)).T[:, :1]
    allowed = (kpos <= qpos) & (kpos >= qlow)
    lifted = jnp.where(allowed, jnp.exp2(scores), 0.0).astype(BF16)
    values = jnp.concatenate([v_ref[...], jnp.ones(v_ref.shape, BF16)], axis=1)
    total = dot(lifted, values)
    if not first:
        total = total + refs[6][...]
    if last:
        weight = total[:, HD:]
        outs[0][...] = total[:, :HD] / weight
        outs[1][...] = jnp.log2(weight).T[:8, :]
    else:
        outs[0][...] = total


def attend(query, keys, values, qpos, qlow, kpos, total, last):
    rows, tokens = query.shape[0], keys.shape[0]
    value_at = values.shape[1] // HD - 1
    own = qpos.shape[1]
    block = 256
    wrap = own // block
    first = total is None
    cost = pl.CostEstimate(
        flops=20 * rows * tokens * HD, bytes_accessed=4 * tokens * HD, transcendentals=rows * tokens
    )
    whole = lambda i: (0, 0)
    return pl.pallas_call(
        functools.partial(attend_kernel, first, last),
        grid=(rows // block,),
        in_specs=[
            pl.BlockSpec((block, HD), lambda i: (i, 0)),
            pl.BlockSpec((tokens, HD), whole),
            pl.BlockSpec((tokens, HD), lambda i: (0, value_at)),
            pl.BlockSpec((1, block), lambda i: (0, i % wrap)),
            pl.BlockSpec((1, block), lambda i: (0, i % wrap)),
            pl.BlockSpec((1, tokens), whole),
        ]
        + ([] if first else [pl.BlockSpec((block, 2 * HD), lambda i: (i, 0))]),
        out_specs=[
            pl.BlockSpec((block, HD), lambda i: (i, 0)),
            pl.BlockSpec((8, block), lambda i: (0, i)),
        ]
        if last
        else pl.BlockSpec((block, 2 * HD), lambda i: (i, 0)),
        out_shape=[
            jax.ShapeDtypeStruct((rows, HD), F32),
            jax.ShapeDtypeStruct((8, rows), F32),
        ]
        if last
        else jax.ShapeDtypeStruct((rows, 2 * HD), F32),
        compiler_params=pltpu.CompilerParams(vmem_limit_bytes=14 * MIB),
        cost_estimate=cost,
    )(query, keys, values, qpos, qlow, kpos, *([] if first else [total]))


def attend_back_kernel(
    chunk, own, first, q_ref, g_ref, log_ref, qpos_ref, qlow_ref, k_ref, v_ref, kpos_ref,
    in_ref, extra_ref, dq_ref, dk_ref, dv_ref, *new_ref,
):
    rows = q_ref.shape[0]
    delta_ref = new_ref[0] if first else extra_ref

    @pl.when(pl.program_id(0) == 0)
    def _():
        if first:
            dq_ref[...] = jnp.zeros_like(dq_ref)
            for i in range(rows // chunk):
                at = pl.ds(i * chunk, chunk)
                product = g_ref[at, :].astype(F32) * in_ref[at, :]
                sums = jnp.sum(product.T, axis=0, keepdims=True)
                delta_ref[:, at] = jnp.broadcast_to(sums, (8, chunk))
        else:
            dq_ref[...] = in_ref[...]

    keys = k_ref[...]
    values = v_ref[...]
    kpos = jnp.broadcast_to(kpos_ref[...], (8, keys.shape[0])).T[:, :1]
    key_sum = jnp.zeros(keys.shape, F32)
    value_sum = jnp.zeros(keys.shape, F32)
    for i in range(rows // chunk):
        at = pl.ds(i * chunk, chunk)
        place = pl.ds((i * chunk) % own, chunk)
        query = q_ref[at, :]
        upstream = g_ref[at, :]
        scores = col_inner(keys, query)
        allowed = (kpos <= qpos_ref[:, place]) & (kpos >= qlow_ref[:, place])
        probs = jnp.where(allowed, jnp.exp2(scores - log_ref[0:1, at]), 0.0)
        prob_grad = col_inner(values, upstream)
        score_grad = (probs * (prob_grad - delta_ref[0:1, at])).astype(BF16)
        value_sum = value_sum + dot(probs.astype(BF16), upstream)
        key_sum = key_sum + dot(score_grad, query)
        dq_ref[at, :] += row_outer(score_grad, keys) * SCORE_SCALE
    dk_ref[...] = key_sum * (SCORE_SCALE / EXP2_SCALE)
    dv_ref[...] = value_sum


def attend_back(query, upstream, logs, qpos, qlow, keys, values, kpos, before, out):
    rows, tokens = query.shape[0], keys.shape[0]
    value_at = values.shape[1] // HD - 1
    own = qpos.shape[1]
    block = 512
    first = before is None
    cost = pl.CostEstimate(
        flops=32 * rows * tokens * HD, bytes_accessed=8 * tokens * HD, transcendentals=rows * tokens
    )
    whole = lambda i: (0, 0)
    taken = (out, logs) if first else before
    return pl.pallas_call(
        functools.partial(attend_back_kernel, 512, own, first),
        grid=(tokens // block,),
        in_specs=[
            pl.BlockSpec((rows, HD), whole),
            pl.BlockSpec((rows, HD), whole),
            pl.BlockSpec((8, rows), whole),
            pl.BlockSpec((1, own), whole),
            pl.BlockSpec((1, own), whole),
            pl.BlockSpec((block, HD), lambda i: (i, 0)),
            pl.BlockSpec((block, HD), lambda i: (i, value_at)),
            pl.BlockSpec((1, block), lambda i: (0, i)),
            pl.BlockSpec((rows, HD), whole),
            pl.BlockSpec((8, rows), whole),
        ],
        out_specs=[
            pl.BlockSpec((rows, HD), whole),
            pl.BlockSpec((block, HD), lambda i: (i, 0)),
            pl.BlockSpec((block, HD), lambda i: (i, 0)),
        ]
        + ([pl.BlockSpec((8, rows), whole)] if first else []),
        out_shape=[
            jax.ShapeDtypeStruct((rows, HD), F32),
            jax.ShapeDtypeStruct((tokens, HD), F32),
            jax.ShapeDtypeStruct((tokens, HD), F32),
        ]
        + ([jax.ShapeDtypeStruct((8, rows), F32)] if first else []),
        compiler_params=pltpu.CompilerParams(vmem_limit_bytes=18 * MIB),
        cost_estimate=cost,
    )(query, upstream, logs, qpos, qlow, keys, values, kpos, *taken)


def local(
    inputs,
    dealing,
    lengths,
    input_gain,
    w_query,
    w_key,
    w_value,
    query_gain,
    key_gain,
    w_out,
    hidden_gain,
    w_gate,
    w_up,
    w_down,
    cotangent,
):
    heads, blks = lax.axis_size("head"), lax.axis_size("blk")
    head, blk = lax.axis_index("head"), lax.axis_index("blk")
    shards = heads * blks
    chips = blks // 2
    chip, core = blk // 2, blk % 2
    shard = head * blks + blk
    rows, width = inputs.shape
    column = rows * blks
    pair = 2 * rows
    per_device = QH // blks
    query_rows, key_rows = w_query.shape[1], w_key.shape[1]
    qkv_rows = query_rows + 2 * key_rows
    in_pair = shards // KVH == heads and blks == 2 * heads

    gains = jnp.zeros((2 * width + 2 * HD,), F32)
    hidden_part = jnp.where(head == 0, hidden_gain.astype(F32), 0.0)
    for at, part in (
        (shard * input_gain.shape[0], input_gain),
        (width + blk * hidden_gain.shape[0], hidden_part),
        (2 * width + shard * query_gain.shape[0], query_gain),
        (2 * width + HD + shard * key_gain.shape[0], key_gain),
    ):
        gains = lax.dynamic_update_slice(gains, part.astype(F32), (at,))
    wire = Wire(inputs)

    index = jnp.stack(
        [
            (((chip - step) % chips) * 2 + (core ^ flip)) * heads + (head ^ place)
            for place in range(heads)
            for step in range(chips)
            for flip in range(2)
        ]
    )
    key_places, query_starts, cosine, sine = tables(
        index, lengths, dealing.reshape(blks * heads, rows), column, heads
    )
    query_places = key_places[:1]

    qkv_job = Job(
        plane_gather(jnp.concatenate([w_query.T, w_key.T, w_value.T], axis=0), False)
    )
    gain_job = Job(sum_everywhere(gains.reshape(-1, 128)))
    own_cotangent = lax.dynamic_slice_in_dim(cotangent, head * rows, rows, 0)
    cotangent_job = wire.add(ring_gather(own_cotangent))
    token_blocks = wire.drive(
        column_gather(inputs), riders=[qkv_job], hooks=[lambda: [gain_job]]
    )
    qkv_weights, gains = qkv_job.result, gain_job.result
    token_blocks = [part for parts in token_blocks for part in parts]
    token_blocks[chips:] = wire.tie(*token_blocks[chips:])
    gains = gains.reshape(-1)
    input_norm = gains[:width]
    hidden_norm = gains[width : 2 * width]
    query_norm = gains[2 * width : 2 * width + HD]
    key_norm = gains[2 * width + HD :]
    qkv_weights = jnp.concatenate(qkv_weights, axis=0)
    feed_rows, out_rows = w_down.shape[0], w_out.shape[0]
    out_weights = lax.all_gather(wire.tie(w_out)[0], "head", axis=0, tiled=True)
    column_values = jnp.concatenate(token_blocks, axis=0).astype(F32)
    normed_column = (column_values * rms_scale(column_values) * input_norm).astype(BF16)
    raw = col_inner(qkv_weights, normed_column).astype(BF16)
    wire.phase([], behind=True, along=[raw])
    raw = wire.along[0]
    norms = jnp.stack([query_norm, key_norm], axis=1)

    def reorder(value, index):
        cut = value.reshape(value.shape[:-1] + (blks, rows))
        return jnp.take(cut, index, axis=-2).reshape(value.shape)

    places = jnp.arange(blks)
    to_ring = ((chip - places // 2) % chips) * 2 + ((places % 2) ^ core)

    def gather_members(value):
        return reorder(lax.all_gather(reorder(value, to_ring), "blk", axis=0), to_ring)

    def exchange(pieces, behind=False):
        return [pieces[0]] + wire.phase(
            [(pieces[flip], member_move(flip)) for flip in range(1, heads)], behind
        )

    member = blk % heads
    odd = chip % 2
    if in_pair:
        pieces = exchange(split_blocks(head ^ member, [raw], heads))
        raw, query, key_value = rope_members(
            member, odd, pieces, cosine, sine, norms, rows, query_rows, key_rows
        )
    else:
        raw = raw.reshape(heads, qkv_rows, column)
        by_head = jnp.stack([pick(raw, head ^ place) for place in range(heads)])
        every = jnp.swapaxes(gather_members(by_head), 0, 1)
        every = every.reshape(shards, qkv_rows, column)
        query_all = every[:, :query_rows].reshape(QH, HD, column)
        key_all = every[:, query_rows : query_rows + key_rows].reshape(KVH, HD, column)
        value_all = every[:, query_rows + key_rows :].reshape(KVH, HD, column)
        query_raw = lax.dynamic_slice_in_dim(query_all, blk * per_device, per_device, 0)
        key_raw = pick(key_all, blk * KVH // blks)
        value_raw = pick(value_all, blk * KVH // blks)

        query = (rope_forward(query_raw, query_norm, cosine, sine) * EXP2_SCALE).astype(BF16)
        keys = rope_forward(key_raw, key_norm, cosine, sine).astype(BF16)
        query = jnp.swapaxes(query, 1, 2).reshape(per_device * column, HD)
        key_value = jnp.concatenate([keys.T, value_raw.T], axis=1)

    pairs = {0: key_value}
    key_pieces, value_pieces = dict(pairs), dict(pairs)
    total = None

    def add_column(place, total):
        return attend(
            query,
            key_pieces[place],
            value_pieces[place],
            query_places,
            query_starts,
            key_places[place : place + 1],
            total,
            place == heads - 1,
        )

    ready = [0]
    for forward, backward in zip(plane_steps(False), plane_steps(True)):
        if forward == backward:
            items = [(pairs[source], head_move(bit)) for place, source, bit in forward]
        else:
            items = [
                (key_pieces[source][:, :HD], head_move(bit)) for place, source, bit in forward
            ] + [(value_pieces[source][:, -HD:], head_move(bit)) for place, source, bit in backward]
        for place in ready:
            total = add_column(place, total)
        got = wire.phase(items, behind=True, along=[total])
        total = wire.along[0]
        if ready == [0]:
            late = wire.tie(jnp.concatenate([w_gate.T, w_up.T, w_down], axis=0))[0]
        ready = [place for place, source, bit in forward]
        for index, place in enumerate(ready):
            key_pieces[place] = got[index]
            if forward == backward:
                value_pieces[place] = pairs[place] = got[index]
            else:
                value_pieces[backward[index][0]] = got[len(forward) + index]
    for place in ready:
        total = add_column(place, total)
    heads_out, logs = total

    if in_pair:
        pieces = exchange(mixed_members(member, heads_out, heads, column), True)
        mixed = join_members(member, odd, pieces, rows).reshape(heads * out_rows, column)
    else:
        mixed_heads = jnp.swapaxes(heads_out.astype(BF16).reshape(per_device, column, HD), 1, 2)
        every = gather_members(mixed_heads)
        every = every.reshape(heads, blks, out_rows, column)
        mixed = lax.dynamic_index_in_dim(every, blk, 1).reshape(heads * out_rows, column)
    branch_parts = row_outer(mixed, out_weights)
    branch = wire.drive(
        column_scatter(lambda step: branch_parts[step * pair : (step + 1) * pair])
    )
    while wire.jobs:
        wire.phase([], behind=True)
    token_values = inputs.astype(F32)
    middle = token_values + branch
    scale_two = rms_scale(middle)
    hidden_in = (middle * scale_two * hidden_norm).astype(BF16)

    late = lax.all_gather(late, "head", axis=0)
    hidden_parts = {}
    feed_groups = []
    near = chips // 2
    groups = [sorted({hop, (chips - hop) % chips}) for hop in range(near + 1)]

    def group_pieces(index, parts):
        return [part for step in groups[index] for part in parts[step]]

    feed_weights = []

    def feed_group(index):
        tokens = jnp.concatenate(group_pieces(index, hidden_parts), axis=0)
        upstream = jnp.concatenate(group_pieces(index, cotangent_job.result), axis=0)
        gate_weights, up_weights, down_weights = feed_weights
        act_grad = col_inner(upstream, down_weights)
        gate = col_inner(tokens, gate_weights)
        up_proj = col_inner(tokens, up_weights)
        sigmoid_gate = jax.nn.sigmoid(gate)
        silu_gate = gate * sigmoid_gate
        activated = (silu_gate * up_proj).astype(BF16)
        gate_grad = (
            act_grad * up_proj * sigmoid_gate * (1.0 + gate * (1.0 - sigmoid_gate))
        ).astype(BF16)
        up_grad = (act_grad * silu_gate).astype(BF16)
        back = dot(gate_grad, gate_weights) + dot(up_grad, up_weights)
        down = dot(activated, down_weights)
        feed_groups.append((activated, gate_grad, up_grad, back, down))

    def start_feed():
        feed_weights.extend(wire.along)

    def keep_first():
        feed_group(0)
        feed_groups[0] = wire.tie(*feed_groups[0])

    wire.drive(
        column_gather(hidden_in, hidden_parts),
        hooks=[start_feed, keep_first],
        along=[
            late[:, i * feed_rows : (i + 1) * feed_rows].reshape(-1, width) for i in range(3)
        ],
    )
    for index in range(1, near + 1):
        feed_group(index)

    def group_rows(index, step):
        group = min(step, chips - step)
        at = groups[group].index(step) * pair
        return feed_groups[group][index][at : at + pair]

    hidden_pieces = sum((group_pieces(index, hidden_parts) for index in range(near + 1)), [])
    upstream_pieces = sum(
        (group_pieces(index, cotangent_job.result) for index in range(near + 1)), []
    )
    down_grads = weight_grads([group[0] for group in feed_groups], upstream_pieces, heads, 2, None)
    gate_grads = weight_grads([group[1] for group in feed_groups], hidden_pieces, heads, 0, down_grads)
    feed_grads = [gate_grads]

    def keep_grads():
        downs = [group[4].astype(BF16) for group in feed_groups]
        feed_grads[0], *downs = wire.tie(feed_grads[0], *downs)
        for index, down in enumerate(downs):
            feed_groups[index] = tuple(feed_groups[index][:4]) + (down,)

    def keep_last():
        feed_grads[0] = wire.tie(
            weight_grads([group[2] for group in feed_groups], hidden_pieces, heads, 1, feed_grads[0])
        )[0]

    hidden_grad = wire.drive(
        column_scatter(lambda step: group_rows(3, step), apart=True),
        hooks=[lambda: None] * (near + 1) + [keep_grads],
    )
    hidden_gain_grad = jnp.sum(hidden_grad * middle * scale_two, axis=0)
    middle_grad = own_cotangent.astype(F32) + norm_back(hidden_grad, middle, scale_two, hidden_norm)
    branch_grad = middle_grad.astype(BF16)
    branch_blocks = join_blocks(wire.drive(column_gather(branch_grad), hooks=[keep_last]))
    down_job = wire.add(column_scatter(lambda step: group_rows(4, step)))
    feed_grads = lax.psum_scatter(feed_grads[0], "head", scatter_dimension=0).astype(F32)
    mixed_grads = [col_inner(out_weights, block).astype(BF16) for block in branch_blocks]
    grad_out = dot(mixed, jnp.concatenate(branch_blocks, axis=0)).reshape(heads, out_rows, width)
    out_parts = [pick(grad_out, head ^ place) for place in range(heads)]
    if in_pair:
        pieces = exchange(split_blocks(member, mixed_grads, heads), True)
        upstream = upstream_members(member, odd, pieces, rows)
    else:
        mixed_grad = jnp.concatenate(mixed_grads, axis=1).reshape(heads, out_rows, column)
        every = gather_members(mixed_grad)
        every = jnp.swapaxes(every, 0, 1).reshape(blks, per_device, HD, column)
        upstream = jnp.swapaxes(pick(every, blk), 1, 2).reshape(per_device * column, HD)

    key_grads, value_grads = {}, {}
    carry = None
    for forward, backward in zip(plane_steps(False)[::-1] + [[]], plane_steps(True)[::-1] + [[]]):
        for place in [step[0] for step in forward] if forward else [0]:
            results = attend_back(
                query,
                upstream,
                logs,
                query_places,
                query_starts,
                key_pieces[place],
                value_pieces[place],
                key_places[place : place + 1],
                carry,
                heads_out,
            )
            key_grads[place] = key_grads.get(place, 0.0) + results[1]
            value_grads[place] = value_grads.get(place, 0.0) + results[2]
            carry = (results[0], carry[1] if carry else results[3])
        if not forward:
            break
        if forward == backward:
            items = [
                (
                    jnp.concatenate([key_grads[place], value_grads[place]], axis=1).astype(BF16),
                    head_move(bit),
                )
                for place, source, bit in forward
            ]
        else:
            items = [
                (key_grads[place].astype(BF16), head_move(bit)) for place, source, bit in forward
            ] + [
                (value_grads[place].astype(BF16), head_move(bit))
                for place, source, bit in backward
            ]
        tied = lax.optimization_barrier(tuple(value for value, move in items) + carry)
        items = [(value, move) for value, (ignored, move) in zip(tied, items)]
        carry = tied[len(items) :]
        got = wire.phase(items, behind=True)
        last_parts = got
        if forward[0][1] == 0:
            continue
        for index, (place, source, bit) in enumerate(forward):
            part = got[index][:, :HD].astype(F32)
            key_grads[source] = key_grads.get(source, 0.0) + part
        for index, (place, source, bit) in enumerate(backward):
            part = got[index if forward == backward else len(forward) + index]
            value_grads[source] = value_grads.get(source, 0.0) + part[:, -HD:].astype(F32)
    query_grad = carry[0]

    if in_pair:
        *pieces, gain_grads = rope_back_members(
            member, raw, query_grad, cosine, sine, norms, key_grads[0], value_grads[0], last_parts,
            query_rows, key_rows,
        )
        pieces = exchange(pieces, True)
        raw_grad = join_members(head ^ member, odd, pieces, rows).reshape(-1, column)
    else:
        key_grad = key_grads[0] + sum(part[:, :HD].astype(F32) for part in last_parts)
        value_grad = value_grads[0] + sum(part[:, HD:].astype(F32) for part in last_parts)
        query_grad = jnp.swapaxes(query_grad.reshape(per_device, column, HD), 1, 2)
        query_raw_grad, query_gain_grad = rope_backward(
            query_raw, query_norm, cosine, sine, query_grad
        )
        key_raw_grad, key_gain_grad = rope_backward(key_raw, key_norm, cosine, sine, key_grad.T)
        query_raw_grad = query_raw_grad.astype(BF16)
        key_raw_grad = key_raw_grad.astype(BF16)
        value_raw_grad = value_grad.T.astype(BF16)
        gain_grads = jnp.stack([jnp.sum(query_gain_grad, axis=0), key_gain_grad], axis=1)

        def spread(part, count, index):
            empty = jnp.zeros((count,) + part.shape[1:], BF16)
            return lax.dynamic_update_slice_in_dim(empty, part, index, 0)

        every = jnp.concatenate(
            [
                spread(query_raw_grad, QH, blk * per_device).reshape(shards, query_rows, column),
                spread(key_raw_grad[None], KVH, blk * KVH // blks).reshape(
                    shards, key_rows, column
                ),
                spread(value_raw_grad[None], KVH, blk * KVH // blks).reshape(
                    shards, key_rows, column
                ),
            ],
            axis=1,
        ).reshape(heads, blks, qkv_rows, column)
        every = reorder(jnp.swapaxes(every, 0, 1), to_ring)
        by_head = reorder(lax.psum_scatter(every, "blk", scatter_dimension=0), to_ring)
        raw_grad = jnp.concatenate(
            [pick(by_head, head ^ place) for place in range(heads)], axis=0
        )

    while down_job.wanted is not None:
        wire.phase([], behind=True)
    done = [feed_grads, (middle + down_job.result).astype(BF16)]

    qkv_grad = dot(raw_grad, normed_column)
    input_gain_grad = jnp.sum(qkv_grad * qkv_weights.astype(F32), axis=0) / input_norm
    sums = jnp.concatenate([input_gain_grad, hidden_gain_grad, gain_grads[:, 0], gain_grads[:, 1]])
    qkv_grad = qkv_grad.reshape(heads, qkv_rows, width)
    out_job = Job(plane_scatter(out_parts, True))
    tail = [
        Job(sum_everywhere(sums.reshape(-1, 128))),
        Job(plane_scatter(list(qkv_grad), False, pause=True)),
        out_job,
    ]

    def keep_done():
        done[:] = wire.tie(*done)

    normed_grad = wire.drive(
        ring_scatter(
            lambda step: row_outer(raw_grad[:, step * pair : (step + 1) * pair], qkv_weights)
        ),
        hooks=[lambda: tail] + [lambda: None] * (chips - 3) + [keep_done],
    )
    sums, grad_tail, grad_out = tail[0].result.reshape(-1), tail[1].result, out_job.result
    feed_grads, layer_out = done
    grad_gate, grad_up, grad_down = (
        feed_grads[i * feed_rows : (i + 1) * feed_rows] for i in range(3)
    )
    token_values = wire.token.astype(F32)
    grad_input = middle_grad + norm_back(
        normed_grad, token_values, rms_scale(token_values), input_norm
    )

    def own_part(at, size):
        return lax.dynamic_slice_in_dim(sums, at, size)

    return (
        layer_out,
        grad_input,
        own_part(shard * input_gain.shape[0], input_gain.shape[0]),
        grad_tail[:query_rows].T,
        grad_tail[query_rows : query_rows + key_rows].T,
        grad_tail[query_rows + key_rows :].T,
        own_part(2 * width + shard * query_gain.shape[0], query_gain.shape[0]),
        own_part(2 * width + HD + shard * key_gain.shape[0], key_gain.shape[0]),
        grad_out,
        own_part(width + blk * hidden_gain.shape[0], hidden_gain.shape[0]),
        grad_gate.T,
        grad_up.T,
        grad_down,
    )


def solution(mesh):
    return jax.shard_map(
        local,
        mesh=mesh,
        in_specs=(
            P(("blk", "head"), None),
            P(),
            P(),
            P(("head", "blk")),
            P(None, ("head", "blk")),
            P(None, ("head", "blk")),
            P(None, ("head", "blk")),
            P(("head", "blk")),
            P(("head", "blk")),
            P(("head", "blk"), None),
            P("blk"),
            P(None, ("head", "blk")),
            P(None, ("head", "blk")),
            P(("head", "blk"), None),
            P("blk", None),
        ),
        out_specs=(
            P(("blk", "head"), None),
            P(("blk", "head"), None),
            P(("head", "blk")),
            P(None, ("head", "blk")),
            P(None, ("head", "blk")),
            P(None, ("head", "blk")),
            P(("head", "blk")),
            P(("head", "blk")),
            P(("head", "blk"), None),
            P("blk"),
            P(None, ("head", "blk")),
            P(None, ("head", "blk")),
            P(("head", "blk"), None),
        ),
        check_vma=False,
    )
```

```python
import functools
import math

import jax
import jax.numpy as jnp
import numpy as np
from jax import lax
from jax.experimental import pallas as pl
from jax.experimental.pallas import tpu as pltpu
from jax.sharding import PartitionSpec as P

QH = 16
KVH = 8
HD = 128
HALF = HD // 2
EPSILON = 1e-06
ROPE_BASE = 1000000.0
SCORE_SCALE = HD ** (-0.5)
EXP2_SCALE = SCORE_SCALE * math.log2(math.e)
CONTRACT_ROWS = (((0,), (0,)), ((), ()))
CONTRACT_COLS = (((1,), (1,)), ((), ()))
BF16 = jnp.bfloat16
F32 = jnp.float32
MIB = 1024 * 1024


def dot(left, right):
    return jnp.dot(left, right, preferred_element_type=F32)


def row_outer(left, right):
    return lax.dot_general(left, right, CONTRACT_ROWS, preferred_element_type=F32)


def col_inner(left, right):
    return lax.dot_general(left, right, CONTRACT_COLS, preferred_element_type=F32)


def rms_scale(values):
    return lax.rsqrt(jnp.mean(values * values, axis=-1, keepdims=True) + EPSILON)


def norm_back(upstream, source, scale_rows, gain):
    scaled = upstream * gain
    return scale_rows * scaled - source * scale_rows**3 * jnp.mean(
        scaled * source, axis=-1, keepdims=True
    )


def head_bits():
    count = lax.axis_size("head")
    return [1 << i for i in range(count.bit_length() - 1)]


def head_move(bit):
    count = lax.axis_size("head")
    return ("head", [(i, i ^ bit) for i in range(count)], bit)


def blk_move(steps, flip, link):
    count = lax.axis_size("blk")
    return ("blk", [(i, ((i + 2 * steps) % count) ^ flip) for i in range(count)], link)


def swap_move():
    return blk_move(0, 1, None)


def ring_move(steps):
    return blk_move(steps, 0, "z")


def member_move(flip):
    count = lax.axis_size("blk")
    return ("blk", [(i, i ^ flip) for i in range(count)], "z" if flip > 1 else None)


class Job:
    def __init__(self, steps):
        self.steps = steps
        self.wanted = None
        self.result = None
        self.advance(None)

    def advance(self, got):
        try:
            self.wanted = self.steps.send(got)
        except StopIteration as end:
            self.wanted = None
            self.result = end.value


class Wire:
    def __init__(self, token):
        self.token = token
        self.jobs = []

    def add(self, steps):
        job = Job(steps)
        self.jobs.append(job)
        return job

    def tie(self, *arrays):
        *arrays, self.token = lax.optimization_barrier(arrays + (self.token,))
        return arrays

    def phase(self, items, behind=False, riders=(), along=()):
        items = list(items)
        count = len(items)
        taken = []
        for job in list(riders) + (self.jobs if behind else []):
            if job.wanted is not None:
                taken.append((job, len(items), len(items) + len(job.wanted)))
                items.extend(job.wanted)
        if not items:
            for job, start, end in taken:
                job.advance([])
            return []
        values = self.tie(*[value for value, move in items])
        outs = [lax.ppermute(value, move[0], move[1]) for value, (same, move) in zip(values, items)]
        outs = self.tie(*outs, *along)
        self.along = outs[len(items) :]
        for job, start, end in taken:
            job.advance(outs[start:end])
        self.jobs = [job for job in self.jobs if job.wanted is not None]
        return outs[:count]

    def drive(self, steps, hooks=(), riders=(), behind=None, along=(), beside=0):
        job = Job(steps)
        riders = list(riders)
        hooks = list(hooks)
        count = 0
        while job.wanted is not None or any(rider.wanted is not None for rider in riders):
            got = self.phase(
                job.wanted or [],
                riders=riders,
                behind=behind is not None and count >= behind,
                along=along if count == beside else (),
            )
            if job.wanted is not None:
                job.advance(got)
            if hooks:
                riders.extend(hooks.pop(0)() or [])
            count += 1
        return job.result


def column_gather(value, blocks=None):
    chips = lax.axis_size("blk") // 2
    near = chips // 2
    blocks = {} if blocks is None else blocks
    fresh = {0: value}
    up = down = value
    for hop in range(1, near + 2):
        items = [(part, swap_move()) for part in fresh.values()]
        if hop <= near:
            items.append((up, ring_move(1)))
        if hop <= chips - 1 - near:
            items.append((down, ring_move(-1)))
        got = yield items
        for (step, part), other in zip(fresh.items(), got):
            blocks[step] = [part, other]
        got = got[len(fresh) :]
        fresh = {}
        if got:
            up = fresh[hop] = got[0]
        if len(got) > 1:
            down = fresh[chips - hop] = got[1]
    return [blocks[step] for step in range(chips)]


def ring_gather(value):
    chips = lax.axis_size("blk") // 2
    blocks = []
    for step in range(chips):
        items = [(value, swap_move())]
        if step < chips - 1:
            items.append((value, ring_move(1)))
        got = yield items
        blocks.append([value, got[0]])
        value = got[-1]
    return blocks


def ring_scatter(part_of):
    chips = lax.axis_size("blk") // 2
    order = list(range(1, chips)) + [0]

    def halves(step):
        part = part_of(step)
        rows = part.shape[0] // 2
        return part[:rows], part[rows:]

    own, other = halves(order[0])
    got = yield [(other.astype(BF16), swap_move())]
    total = own.astype(F32) + got[0].astype(F32)
    for step in order[1:]:
        own, other = halves(step)
        got = yield [(total.astype(BF16), ring_move(1)), (other.astype(BF16), swap_move())]
        total = own.astype(F32) + got[1].astype(F32) + got[0].astype(F32)
    return total


def join_blocks(blocks):
    return [jnp.concatenate(block, axis=0) for block in blocks]


def column_scatter(part_of, apart=False):
    chips = lax.axis_size("blk") // 2
    near = chips // 2
    totals = {}

    def swaps(steps):
        parts = {step: part_of(step) for step in steps}
        half = parts[steps[0]].shape[0] // 2
        items = [(parts[step][half:].astype(BF16), swap_move()) for step in steps]
        return items, {step: part[:half] for step, part in parts.items()}

    def add(own, got):
        for (step, part), other in zip(own.items(), got):
            totals[step] = part.astype(F32) + other.astype(F32) + totals.get(step, 0.0)

    items, own = swaps([near])
    add(own, (yield items))
    for hop in range(near, 0, -1):
        both = hop <= chips - 1 - near
        moves = [(totals[hop].astype(BF16), ring_move(-1))]
        if both:
            moves.append((totals[chips - hop].astype(BF16), ring_move(1)))
        steps = sorted({hop - 1, (chips - hop + 1) % chips})
        if apart:
            got = yield moves
            items, own = swaps(steps)
            add(own, (yield items))
            apart = False
        else:
            items, own = swaps(steps)
            got = yield moves + items
            add(own, got[len(moves) :])
        totals[hop - 1] = totals[hop - 1] + got[0].astype(F32)
        if both:
            step = (chips - hop + 1) % chips
            totals[step] = totals[step] + got[1].astype(F32)
    return totals[0]


def plane_steps(backwards):
    bits = head_bits()
    order = bits[::-1] if backwards else bits
    steps = []
    for weight in range(1, len(bits) + 1):
        step = []
        for place in range(1 << len(bits)):
            if bin(place).count("1") == weight:
                last = [bit for bit in order if place & bit][-1]
                step.append((place, place ^ last, last))
        steps.append(step)
    return steps


def plane_gather(value, backwards):
    pieces = {0: value}
    for step in plane_steps(backwards):
        got = yield [(pieces[source], head_move(bit)) for place, source, bit in step]
        for (place, source, bit), piece in zip(step, got):
            pieces[place] = piece
    return [pieces[i] for i in range(len(pieces))]


def plane_scatter(parts, backwards, pause=False):
    pieces = list(parts)
    for index, step in enumerate(plane_steps(backwards)[::-1]):
        if pause and index == 1:
            yield []
        got = yield [(pieces[place].astype(BF16), head_move(bit)) for place, source, bit in step]
        for (place, source, bit), piece in zip(step, got):
            pieces[source] = pieces[source] + piece.astype(F32)
    return pieces[0]


def sum_everywhere(value):
    chips = lax.axis_size("blk") // 2
    for moves in (
        *([head_move(bit)] for bit in head_bits()),
        [swap_move()],
        [blk_move(steps, 0, None) for steps in range(1, chips)],
    ):
        got = yield [(value, move) for move in moves]
        for part in got:
            value = value + part
    return value


def pick(stack, index):
    return lax.dynamic_index_in_dim(stack, index, 0, keepdims=False)


def token_starts(anchors, lengths):
    ends = jnp.cumsum(lengths)
    seq_starts = ends - lengths
    inside = seq_starts[None, :] <= anchors[:, None]
    return jnp.max(jnp.where(inside, seq_starts[None, :], 0), axis=1)


def rope_tables(places):
    ladder = jnp.arange(HALF, dtype=F32)
    rates = jnp.exp(ladder * (-2.0 * math.log(ROPE_BASE) / HD))
    angles = rates[:, None] * places.astype(F32)[None, :]
    return (jnp.cos(angles), jnp.sin(angles))


def rope_forward(raw, gain, cosine, sine):
    heads = raw.astype(F32)
    scale = lax.rsqrt(jnp.mean(heads * heads, axis=-2, keepdims=True) + EPSILON)
    normed = heads * scale * gain[:, None]
    low, high = normed[..., :HALF, :], normed[..., HALF:, :]
    return jnp.concatenate([low * cosine - high * sine, high * cosine + low * sine], axis=-2)


def rope_backward(raw, gain, cosine, sine, upstream):
    heads = raw.astype(F32)
    scale = lax.rsqrt(jnp.mean(heads * heads, axis=-2, keepdims=True) + EPSILON)
    low, high = upstream[..., :HALF, :], upstream[..., HALF:, :]
    turned = jnp.concatenate([low * cosine + high * sine, high * cosine - low * sine], axis=-2)
    gain_grad = jnp.sum(turned * heads * scale, axis=-1)
    scaled = turned * gain[:, None]
    back = scale * scaled - heads * scale**3 * jnp.mean(scaled * heads, axis=-2, keepdims=True)
    return back, gain_grad


def small_call(kernel, outs, scalars, arrays, scratch=()):
    vmem = pl.BlockSpec(memory_space=pltpu.VMEM)
    return pl.pallas_call(
        kernel,
        in_specs=[pl.BlockSpec(memory_space=pltpu.SMEM)] + [vmem] * len(arrays),
        out_specs=[vmem] * len(outs),
        out_shape=[jax.ShapeDtypeStruct(shape, dtype) for shape, dtype in outs],
        scratch_shapes=[pltpu.VMEM(shape, dtype) for shape, dtype in scratch],
        compiler_params=pltpu.CompilerParams(vmem_limit_bytes=10 * MIB),
        cost_estimate=pl.CostEstimate(
            flops=0,
            bytes_accessed=3 * sum(array.size * array.dtype.itemsize for array in arrays),
            transcendentals=0,
        ),
    )(scalars, *arrays)


def table_kernel(blocks, sequences, index_ref, deal_ref, rate_ref, key_ref, start_ref, cos_ref, sin_ref):
    heads, column = key_ref.shape
    rows = column // blocks
    for place in range(heads):
        for block in range(blocks):
            row = deal_ref[pl.ds(index_ref[place * blocks + block], 1), :]
            key_ref[place : place + 1, block * rows : (block + 1) * rows] = row
    own = key_ref[0:1, :]
    starts = jnp.zeros_like(own)
    first = jnp.int32(0)
    for sequence in range(sequences - 1):
        first = first + index_ref[heads * blocks + sequence]
        starts = jnp.where(own >= first, first, starts)
    start_ref[...] = starts
    angles = rate_ref[:, :1] * (own - starts).astype(F32)
    cos_ref[...] = jnp.cos(angles)
    sin_ref[...] = jnp.sin(angles)


def tables(index, lengths, deals, column, heads):
    rates = np.exp(
        np.arange(HALF, dtype=np.float32) * np.float32(-2.0 * math.log(ROPE_BASE) / HD)
    ).astype(np.float32)
    return small_call(
        functools.partial(table_kernel, column // deals.shape[1], lengths.shape[0]),
        [
            ((heads, column), jnp.int32),
            ((1, column), jnp.int32),
            ((HALF, column), F32),
            ((HALF, column), F32),
        ],
        jnp.concatenate([index, lengths]),
        [deals, jnp.asarray(np.broadcast_to(rates[:, None], (HALF, 128)))],
    )


def put_in_order(out_ref, scalar_ref, pieces, rows, finish):
    base = scalar_ref[0]
    for flip, piece in enumerate(pieces):
        value = piece[...]
        column = value.shape[1]
        if flip & 1:
            cuts = [value[:, i * rows : (i + 1) * rows] for i in range(column // rows)]
            value = jnp.concatenate([cuts[i ^ 1] for i in range(column // rows)], axis=1)
        at = pl.ds(base ^ flip, 1)
        if flip & 2:
            pair = 2 * rows

            @pl.when(scalar_ref[1] == 0)
            def _(at=at, value=value, pair=pair):
                out_ref[at] = jnp.concatenate([value[:, pair:], value[:, :pair]], axis=1)[None]

            @pl.when(scalar_ref[1] != 0)
            def _(at=at, value=value, pair=pair):
                out_ref[at] = jnp.concatenate([value[:, -pair:], value[:, :-pair]], axis=1)[None]

        else:
            out_ref[at] = value[None]
    finish()


def join_members(base, odd, pieces, rows):
    count = len(pieces)

    def kernel(scalar_ref, *refs):
        put_in_order(refs[count], scalar_ref, refs[:count], rows, lambda: None)

    return small_call(
        kernel,
        [((count,) + pieces[0].shape, BF16)],
        jnp.stack([base, odd]).astype(jnp.int32),
        pieces,
    )[0]


def split_blocks(base, blocks, count):
    size = blocks[0].shape[0] // count
    width = blocks[0].shape[1]

    def kernel(scalar_ref, *refs):
        for flip in range(count):
            start = pl.multiple_of((scalar_ref[0] ^ flip) * size, size)
            for index in range(len(blocks)):
                refs[len(blocks) + flip][:, index * width : (index + 1) * width] = refs[index][
                    pl.ds(start, size), :
                ]

    return small_call(
        kernel,
        [((size, width * len(blocks)), BF16)] * count,
        base.reshape(1).astype(jnp.int32),
        blocks,
    )


def rope_kernel(rows, query_rows, key_rows, scalar_ref, *refs):
    pieces = refs[:-6]
    cos_ref, sin_ref, gain_ref, raw_ref, query_ref, pair_ref = refs[-6:]
    count, column = len(pieces), cos_ref.shape[1]
    put_in_order(raw_ref, scalar_ref, pieces, rows, lambda: None)
    cosine, sine = cos_ref[...], sin_ref[...]

    def rotate(parts, gain):
        heads = jnp.concatenate(parts, axis=0).astype(F32)
        scale = lax.rsqrt(jnp.mean(heads * heads, axis=0, keepdims=True) + EPSILON)
        normed = heads * scale * gain
        low, high = normed[:HALF], normed[HALF:]
        turned = jnp.concatenate([low * cosine - high * sine, high * cosine + low * sine], axis=0)
        return turned

    per_head = HD // query_rows
    for head in range(count // per_head):
        parts = [raw_ref[head * per_head + i, :query_rows, :] for i in range(per_head)]
        turned = rotate(parts, gain_ref[:, 0:1]) * EXP2_SCALE
        query_ref[head * column : (head + 1) * column, :] = turned.T.astype(BF16)
    parts = [raw_ref[i, query_rows : query_rows + key_rows, :] for i in range(count)]
    pair_ref[:, :HD] = rotate(parts, gain_ref[:, 1:2]).T.astype(BF16)
    parts = [raw_ref[i, query_rows + key_rows :, :] for i in range(count)]
    pair_ref[:, HD:] = jnp.concatenate(parts, axis=0).astype(F32).T.astype(BF16)


def rope_members(base, odd, pieces, cosine, sine, gains, rows, query_rows, key_rows):
    count, column = len(pieces), cosine.shape[1]
    return small_call(
        functools.partial(rope_kernel, rows, query_rows, key_rows),
        [
            ((count,) + pieces[0].shape, BF16),
            ((count * query_rows // HD * column, HD), BF16),
            ((column, 2 * HD), BF16),
        ],
        jnp.stack([base, odd]).astype(jnp.int32),
        list(pieces) + [cosine, sine, gains],
    )


def mixed_kernel(scalar_ref, in_ref, *refs):
    outs, parts_ref = refs[:-1], refs[-1]
    count, size, column = parts_ref.shape
    for head in range(in_ref.shape[0] // column):
        part = in_ref[head * column : (head + 1) * column, :].T.astype(BF16)
        per_head = HD // size
        for i in range(per_head):
            parts_ref[head * per_head + i] = part[i * size : (i + 1) * size]
    for flip, out_ref in enumerate(outs):
        out_ref[...] = parts_ref[scalar_ref[0] ^ flip]


def mixed_members(base, heads_out, count, column):
    size = heads_out.shape[0] // column * HD // count
    return small_call(
        mixed_kernel,
        [((size, column), BF16)] * count,
        base.reshape(1).astype(jnp.int32),
        [heads_out],
        [((count, size, column), BF16)],
    )


def upstream_members(base, odd, pieces, rows):
    count = len(pieces)
    size, column = pieces[0].shape
    per_head = HD // size

    def kernel(scalar_ref, *refs):
        out_ref, parts_ref = refs[count:]
        put_in_order(parts_ref, scalar_ref, refs[:count], rows, lambda: None)
        for head in range(count // per_head):
            parts = [parts_ref[head * per_head + i] for i in range(per_head)]
            out_ref[head * column : (head + 1) * column, :] = (
                jnp.concatenate(parts, axis=0).astype(F32).T.astype(BF16)
            )

    return small_call(
        kernel,
        [((count // per_head * column, HD), BF16)],
        jnp.stack([base, odd]).astype(jnp.int32),
        pieces,
        [((count, size, column), BF16)],
    )[0]


def light():
    return pl.CostEstimate(flops=1, bytes_accessed=1, transcendentals=0)


def feed_kernel(count, *refs):
    tokens = refs[:count]
    grad_ref, gate_ref, up_ref, act_out, gate_out, up_out, back_out, token_ref, total_ref = refs[
        count:
    ]
    step = pl.program_id(0)

    @pl.when(step == 0)
    def _():
        rows = tokens[0].shape[0]
        for index in range(count):
            token_ref[index * rows : (index + 1) * rows, :] = tokens[index][...]
        total_ref[...] = jnp.zeros_like(total_ref)

    gate = col_inner(token_ref[...], gate_ref[...])
    up_proj = col_inner(token_ref[...], up_ref[...])
    act_grad = grad_ref[...]
    sigmoid_gate = jax.nn.sigmoid(gate)
    silu_gate = gate * sigmoid_gate
    gate_grad = (act_grad * up_proj * sigmoid_gate * (1.0 + gate * (1.0 - sigmoid_gate))).astype(
        BF16
    )
    up_grad = (act_grad * silu_gate).astype(BF16)
    act_out[...] = (silu_gate * up_proj).astype(BF16)
    gate_out[...] = gate_grad
    up_out[...] = up_grad
    total_ref[...] += dot(gate_grad, gate_ref[...]) + dot(up_grad, up_ref[...])

    @pl.when(step == pl.num_programs(0) - 1)
    def _():
        back_out[...] = total_ref[...].astype(BF16)


def feed_beside(tokens, act_grad, gate_weights, up_weights):
    piece, width = tokens[0].shape
    rows, hidden = act_grad.shape
    tile = hidden // 3
    part = pl.BlockSpec((rows, tile), lambda i: (0, i))
    weight = pl.BlockSpec((tile, width), lambda i: (i, 0))
    whole = lambda i: (0, 0)
    return pl.pallas_call(
        functools.partial(feed_kernel, len(tokens)),
        grid=(3,),
        in_specs=[pl.BlockSpec((piece, width), whole)] * len(tokens) + [part, weight, weight],
        out_specs=[part] * 3 + [pl.BlockSpec((rows, width), whole)],
        out_shape=[jax.ShapeDtypeStruct((rows, hidden), BF16)] * 3
        + [jax.ShapeDtypeStruct((rows, width), BF16)],
        scratch_shapes=[pltpu.VMEM((rows, width), BF16), pltpu.VMEM((rows, width), F32)],
        compiler_params=pltpu.CompilerParams(vmem_limit_bytes=24 * MIB),
        cost_estimate=light(),
    )(*tokens, act_grad, gate_weights, up_weights)


def weight_grad_kernel(count, groups, *refs):
    pieces, lefts = refs[:count], refs[count : count + groups]
    out_ref, right_ref = refs[-2:]
    rows = pieces[0].shape[0]

    @pl.when(pl.program_id(0) == 0)
    def _():
        for index in range(count):
            right_ref[index * rows : (index + 1) * rows, :] = pieces[index][...]

    size = out_ref.shape[1]
    for head in range(lefts[0].shape[1] // size):

        @pl.when(pl.program_id(0) == head)
        def _(head=head):
            cut = slice(head * size, (head + 1) * size)
            left = jnp.concatenate([ref[:, cut] for ref in lefts], axis=0)
            out_ref[0] = row_outer(left, right_ref[...]).astype(BF16)


def weight_grads(lefts, pieces, heads, kind, into):
    size = lefts[0].shape[1] // heads
    piece, width = pieces[0].shape
    count = len(pieces)
    specs = [pl.BlockSpec((piece, width), lambda i: (0, 0))] * count
    specs += [pl.BlockSpec(left.shape, lambda i: (0, 0)) for left in lefts]
    operands = list(pieces) + list(lefts)
    aliases = {}
    if into is not None:
        specs.append(pl.BlockSpec(memory_space=pl.ANY))
        aliases = {len(operands): 0}
        operands.append(into)
    return pl.pallas_call(
        functools.partial(weight_grad_kernel, count, len(lefts)),
        grid=(heads,),
        in_specs=specs,
        out_specs=pl.BlockSpec((1, size, width), lambda i: (i, kind, 0)),
        out_shape=jax.ShapeDtypeStruct((heads, 3 * size, width), BF16),
        scratch_shapes=[pltpu.VMEM((count * piece, width), BF16)],
        input_output_aliases=aliases,
        compiler_params=pltpu.CompilerParams(vmem_limit_bytes=20 * MIB),
        cost_estimate=light(),
    )(*operands)


def rope_back_kernel(query_rows, key_rows, count, scalar_ref, *refs):
    raw_ref, dq_ref, cos_ref, sin_ref, gain_ref, dk_ref, dv_ref = refs[:7]
    more = refs[7 : -2 - count]
    outs, gain_out, parts_ref = refs[-2 - count : -2], refs[-2], refs[-1]
    column = cos_ref.shape[1]
    cosine, sine = cos_ref[...], sin_ref[...]

    def back(parts, gain, upstream):
        heads = jnp.concatenate(parts, axis=0).astype(F32)
        scale = lax.rsqrt(jnp.mean(heads * heads, axis=0, keepdims=True) + EPSILON)
        low, high = upstream[:HALF], upstream[HALF:]
        turned = jnp.concatenate([low * cosine + high * sine, high * cosine - low * sine], axis=0)
        gain_grad = jnp.sum(turned * heads * scale, axis=1, keepdims=True)
        scaled = turned * gain
        mean = jnp.mean(scaled * heads, axis=0, keepdims=True)
        return (scale * scaled - heads * (scale * scale * scale * mean)).astype(BF16), gain_grad

    per_head = HD // query_rows
    total = jnp.zeros((HD, 1), F32)
    for head in range(count // per_head):
        at = [head * per_head + i for i in range(per_head)]
        grad, gain_grad = back(
            [raw_ref[i, :query_rows, :] for i in at],
            gain_ref[:, 0:1],
            dq_ref[head * column : (head + 1) * column, :].T,
        )
        total = total + gain_grad
        for place, i in enumerate(at):
            parts_ref[i, :query_rows, :] = grad[place * query_rows : (place + 1) * query_rows]
    gain_out[:, 0:1] = total
    key_grad, value_grad = dk_ref[...], dv_ref[...]
    for ref in more:
        key_grad = key_grad + ref[:, :HD].astype(F32)
        value_grad = value_grad + ref[:, HD:].astype(F32)
    grad, gain_grad = back(
        [raw_ref[i, query_rows : query_rows + key_rows, :] for i in range(count)],
        gain_ref[:, 1:2],
        key_grad.T,
    )
    gain_out[:, 1:2] = gain_grad
    value_grad = value_grad.T.astype(BF16)
    for i in range(count):
        cut = slice(i * key_rows, (i + 1) * key_rows)
        parts_ref[i, query_rows : query_rows + key_rows, :] = grad[cut]
        parts_ref[i, query_rows + key_rows :, :] = value_grad[cut]
    for flip, out_ref in enumerate(outs):
        out_ref[...] = parts_ref[scalar_ref[0] ^ flip]


def rope_back_members(base, raw, dq, cosine, sine, gains, dk, dv, more, query_rows, key_rows):
    count, size, column = raw.shape
    return small_call(
        functools.partial(rope_back_kernel, query_rows, key_rows, count),
        [((size, column), BF16)] * count + [((HD, 2), F32)],
        base.reshape(1).astype(jnp.int32),
        [raw, dq, cosine, sine, gains, dk, dv] + list(more),
        [((count, size, column), BF16)],
    )


def attend_kernel(first, last, *refs):
    refs = list(refs)
    q_ref, k_ref, v_ref, qpos_ref, qlow_ref, kpos_ref = refs[:6]
    outs = refs[6:] if first else refs[7:]
    kpos = kpos_ref[...]
    scores = col_inner(q_ref[...], k_ref[...])
    rows = q_ref.shape[0]
    qpos = jnp.broadcast_to(qpos_ref[...], (8, rows)).T[:, :1]
    qlow = jnp.broadcast_to(qlow_ref[...], (8, rows)).T[:, :1]
    allowed = (kpos <= qpos) & (kpos >= qlow)
    lifted = jnp.where(allowed, jnp.exp2(scores), 0.0).astype(BF16)
    values = jnp.concatenate([v_ref[...], jnp.ones(v_ref.shape, BF16)], axis=1)
    total = dot(lifted, values)
    if not first:
        total = total + refs[6][...]
    if last:
        weight = total[:, HD:]
        outs[0][...] = total[:, :HD] / weight
        outs[1][...] = jnp.log2(weight).T[:8, :]
    else:
        outs[0][...] = total


def attend(query, keys, values, qpos, qlow, kpos, total, last):
    rows, tokens = query.shape[0], keys.shape[0]
    value_at = values.shape[1] // HD - 1
    own = qpos.shape[1]
    block = 512
    wrap = own // block
    first = total is None
    cost = pl.CostEstimate(
        flops=20 * rows * tokens * HD, bytes_accessed=4 * tokens * HD, transcendentals=rows * tokens
    )
    whole = lambda i: (0, 0)
    return pl.pallas_call(
        functools.partial(attend_kernel, first, last),
        grid=(rows // block,),
        in_specs=[
            pl.BlockSpec((block, HD), lambda i: (i, 0)),
            pl.BlockSpec((tokens, HD), whole),
            pl.BlockSpec((tokens, HD), lambda i: (0, value_at)),
            pl.BlockSpec((1, block), lambda i: (0, i % wrap)),
            pl.BlockSpec((1, block), lambda i: (0, i % wrap)),
            pl.BlockSpec((1, tokens), whole),
        ]
        + ([] if first else [pl.BlockSpec((block, 2 * HD), lambda i: (i, 0))]),
        out_specs=[
            pl.BlockSpec((block, HD), lambda i: (i, 0)),
            pl.BlockSpec((8, block), lambda i: (0, i)),
        ]
        if last
        else pl.BlockSpec((block, 2 * HD), lambda i: (i, 0)),
        out_shape=[
            jax.ShapeDtypeStruct((rows, HD), F32),
            jax.ShapeDtypeStruct((8, rows), F32),
        ]
        if last
        else jax.ShapeDtypeStruct((rows, 2 * HD), F32),
        compiler_params=pltpu.CompilerParams(vmem_limit_bytes=20 * MIB),
        cost_estimate=cost,
    )(query, keys, values, qpos, qlow, kpos, *([] if first else [total]))


def attend_back_kernel(
    chunk, own, first, q_ref, g_ref, log_ref, qpos_ref, qlow_ref, k_ref, v_ref, kpos_ref,
    in_ref, extra_ref, dq_ref, dk_ref, dv_ref, *new_ref,
):
    rows = q_ref.shape[0]
    delta_ref = new_ref[0] if first else extra_ref

    @pl.when(pl.program_id(0) == 0)
    def _():
        if first:
            dq_ref[...] = jnp.zeros_like(dq_ref)
            for i in range(rows // chunk):
                at = pl.ds(i * chunk, chunk)
                product = g_ref[at, :].astype(F32) * in_ref[at, :]
                sums = jnp.sum(product.T, axis=0, keepdims=True)
                delta_ref[:, at] = jnp.broadcast_to(sums, (8, chunk))
        else:
            dq_ref[...] = in_ref[...]

    keys = k_ref[...]
    values = v_ref[...]
    kpos = jnp.broadcast_to(kpos_ref[...], (8, keys.shape[0])).T[:, :1]
    key_sum = jnp.zeros(keys.shape, F32)
    value_sum = jnp.zeros(keys.shape, F32)
    for i in range(rows // chunk):
        at = pl.ds(i * chunk, chunk)
        place = pl.ds((i * chunk) % own, chunk)
        query = q_ref[at, :]
        upstream = g_ref[at, :]
        scores = col_inner(keys, query)
        allowed = (kpos <= qpos_ref[:, place]) & (kpos >= qlow_ref[:, place])
        probs = jnp.where(allowed, jnp.exp2(scores - log_ref[0:1, at]), 0.0)
        prob_grad = col_inner(values, upstream)
        score_grad = (probs * (prob_grad - delta_ref[0:1, at])).astype(BF16)
        value_sum = value_sum + dot(probs.astype(BF16), upstream)
        key_sum = key_sum + dot(score_grad, query)
        dq_ref[at, :] += row_outer(score_grad, keys) * SCORE_SCALE
    dk_ref[...] = key_sum * (SCORE_SCALE / EXP2_SCALE)
    dv_ref[...] = value_sum


def attend_back(query, upstream, logs, qpos, qlow, keys, values, kpos, before, out):
    rows, tokens = query.shape[0], keys.shape[0]
    value_at = values.shape[1] // HD - 1
    own = qpos.shape[1]
    block = 1024
    first = before is None
    cost = pl.CostEstimate(
        flops=32 * rows * tokens * HD, bytes_accessed=8 * tokens * HD, transcendentals=rows * tokens
    )
    whole = lambda i: (0, 0)
    taken = (out, logs) if first else before
    return pl.pallas_call(
        functools.partial(attend_back_kernel, 512, own, first),
        grid=(tokens // block,),
        in_specs=[
            pl.BlockSpec((rows, HD), whole),
            pl.BlockSpec((rows, HD), whole),
            pl.BlockSpec((8, rows), whole),
            pl.BlockSpec((1, own), whole),
            pl.BlockSpec((1, own), whole),
            pl.BlockSpec((block, HD), lambda i: (i, 0)),
            pl.BlockSpec((block, HD), lambda i: (i, value_at)),
            pl.BlockSpec((1, block), lambda i: (0, i)),
            pl.BlockSpec((rows, HD), whole),
            pl.BlockSpec((8, rows), whole),
        ],
        out_specs=[
            pl.BlockSpec((rows, HD), whole),
            pl.BlockSpec((block, HD), lambda i: (i, 0)),
            pl.BlockSpec((block, HD), lambda i: (i, 0)),
        ]
        + ([pl.BlockSpec((8, rows), whole)] if first else []),
        out_shape=[
            jax.ShapeDtypeStruct((rows, HD), F32),
            jax.ShapeDtypeStruct((tokens, HD), F32),
            jax.ShapeDtypeStruct((tokens, HD), F32),
        ]
        + ([jax.ShapeDtypeStruct((8, rows), F32)] if first else []),
        compiler_params=pltpu.CompilerParams(vmem_limit_bytes=28 * MIB),
        cost_estimate=cost,
    )(query, upstream, logs, qpos, qlow, keys, values, kpos, *taken)


def local(
    inputs,
    dealing,
    lengths,
    input_gain,
    w_query,
    w_key,
    w_value,
    query_gain,
    key_gain,
    w_out,
    hidden_gain,
    w_gate,
    w_up,
    w_down,
    cotangent,
):
    heads, blks = lax.axis_size("head"), lax.axis_size("blk")
    head, blk = lax.axis_index("head"), lax.axis_index("blk")
    shards = heads * blks
    chips = blks // 2
    chip, core = blk // 2, blk % 2
    shard = head * blks + blk
    rows, width = inputs.shape
    column = rows * blks
    pair = 2 * rows
    per_device = QH // blks
    query_rows, key_rows = w_query.shape[1], w_key.shape[1]
    qkv_rows = query_rows + 2 * key_rows
    in_pair = shards // KVH == heads and blks == 2 * heads

    gains = jnp.zeros((2 * width + 2 * HD,), F32)
    hidden_part = jnp.where(head == 0, hidden_gain.astype(F32), 0.0)
    for at, part in (
        (shard * input_gain.shape[0], input_gain),
        (width + blk * hidden_gain.shape[0], hidden_part),
        (2 * width + shard * query_gain.shape[0], query_gain),
        (2 * width + HD + shard * key_gain.shape[0], key_gain),
    ):
        gains = lax.dynamic_update_slice(gains, part.astype(F32), (at,))
    wire = Wire(inputs)

    index = jnp.stack(
        [
            (((chip - step) % chips) * 2 + (core ^ flip)) * heads + (head ^ place)
            for place in range(heads)
            for step in range(chips)
            for flip in range(2)
        ]
    )
    key_places, query_starts, cosine, sine = tables(
        index, lengths, dealing.reshape(blks * heads, rows), column, heads
    )
    query_places = key_places[:1]

    qkv_job = Job(
        plane_gather(jnp.concatenate([w_query.T, w_key.T, w_value.T], axis=0), False)
    )
    gain_job = Job(sum_everywhere(gains.reshape(-1, 128)))
    own_cotangent = lax.dynamic_slice_in_dim(cotangent, head * rows, rows, 0)
    cotangent_job = wire.add(ring_gather(own_cotangent))
    token_blocks = wire.drive(
        column_gather(inputs), riders=[qkv_job], hooks=[lambda: [gain_job]]
    )
    qkv_weights, gains = qkv_job.result, gain_job.result
    token_blocks = [part for parts in token_blocks for part in parts]
    token_blocks[chips:] = wire.tie(*token_blocks[chips:])
    gains = gains.reshape(-1)
    input_norm = gains[:width]
    hidden_norm = gains[width : 2 * width]
    query_norm = gains[2 * width : 2 * width + HD]
    key_norm = gains[2 * width + HD :]
    qkv_weights = jnp.concatenate(qkv_weights, axis=0)
    feed_rows, out_rows = w_down.shape[0], w_out.shape[0]
    out_weights = lax.all_gather(wire.tie(w_out)[0], "head", axis=0, tiled=True)
    column_values = jnp.concatenate(token_blocks, axis=0).astype(F32)
    normed_column = (column_values * rms_scale(column_values) * input_norm).astype(BF16)
    raw = col_inner(qkv_weights, normed_column).astype(BF16)
    wire.phase([], behind=True, along=[raw])
    raw = wire.along[0]
    norms = jnp.stack([query_norm, key_norm], axis=1)

    def reorder(value, index):
        cut = value.reshape(value.shape[:-1] + (blks, rows))
        return jnp.take(cut, index, axis=-2).reshape(value.shape)

    places = jnp.arange(blks)
    to_ring = ((chip - places // 2) % chips) * 2 + ((places % 2) ^ core)

    def gather_members(value):
        return reorder(lax.all_gather(reorder(value, to_ring), "blk", axis=0), to_ring)

    def exchange(pieces, behind=False):
        return [pieces[0]] + wire.phase(
            [(pieces[flip], member_move(flip)) for flip in range(1, heads)], behind
        )

    member = blk % heads
    odd = chip % 2
    if in_pair:
        pieces = exchange(split_blocks(head ^ member, [raw], heads))
        raw, query, key_value = rope_members(
            member, odd, pieces, cosine, sine, norms, rows, query_rows, key_rows
        )
    else:
        raw = raw.reshape(heads, qkv_rows, column)
        by_head = jnp.stack([pick(raw, head ^ place) for place in range(heads)])
        every = jnp.swapaxes(gather_members(by_head), 0, 1)
        every = every.reshape(shards, qkv_rows, column)
        query_all = every[:, :query_rows].reshape(QH, HD, column)
        key_all = every[:, query_rows : query_rows + key_rows].reshape(KVH, HD, column)
        value_all = every[:, query_rows + key_rows :].reshape(KVH, HD, column)
        query_raw = lax.dynamic_slice_in_dim(query_all, blk * per_device, per_device, 0)
        key_raw = pick(key_all, blk * KVH // blks)
        value_raw = pick(value_all, blk * KVH // blks)

        query = (rope_forward(query_raw, query_norm, cosine, sine) * EXP2_SCALE).astype(BF16)
        keys = rope_forward(key_raw, key_norm, cosine, sine).astype(BF16)
        query = jnp.swapaxes(query, 1, 2).reshape(per_device * column, HD)
        key_value = jnp.concatenate([keys.T, value_raw.T], axis=1)

    pairs = {0: key_value}
    key_pieces, value_pieces = dict(pairs), dict(pairs)
    total = None

    def add_column(place, total):
        return attend(
            query,
            key_pieces[place],
            value_pieces[place],
            query_places,
            query_starts,
            key_places[place : place + 1],
            total,
            place == heads - 1,
        )

    ready = [0]
    for forward, backward in zip(plane_steps(False), plane_steps(True)):
        if forward == backward:
            items = [(pairs[source], head_move(bit)) for place, source, bit in forward]
        else:
            items = [
                (key_pieces[source][:, :HD], head_move(bit)) for place, source, bit in forward
            ] + [(value_pieces[source][:, -HD:], head_move(bit)) for place, source, bit in backward]
        for place in ready:
            total = add_column(place, total)
        got = wire.phase(items, behind=True, along=[total])
        total = wire.along[0]
        if ready == [0]:
            late = wire.tie(jnp.concatenate([w_gate.T, w_up.T, w_down], axis=0))[0]
        ready = [place for place, source, bit in forward]
        for index, place in enumerate(ready):
            key_pieces[place] = got[index]
            if forward == backward:
                value_pieces[place] = pairs[place] = got[index]
            else:
                value_pieces[backward[index][0]] = got[len(forward) + index]
    for place in ready:
        total = add_column(place, total)
    heads_out, logs = total

    if in_pair:
        pieces = exchange(mixed_members(member, heads_out, heads, column), True)
        mixed = join_members(member, odd, pieces, rows).reshape(heads * out_rows, column)
    else:
        mixed_heads = jnp.swapaxes(heads_out.astype(BF16).reshape(per_device, column, HD), 1, 2)
        every = gather_members(mixed_heads)
        every = every.reshape(heads, blks, out_rows, column)
        mixed = lax.dynamic_index_in_dim(every, blk, 1).reshape(heads * out_rows, column)
    branch_parts = row_outer(mixed, out_weights)
    branch = wire.drive(
        column_scatter(lambda step: branch_parts[step * pair : (step + 1) * pair])
    )
    while wire.jobs:
        wire.phase([], behind=True)
    token_values = inputs.astype(F32)
    middle = token_values + branch
    scale_two = rms_scale(middle)
    hidden_in = (middle * scale_two * hidden_norm).astype(BF16)

    late = lax.all_gather(late, "head", axis=0)
    hidden_parts = {}
    feed_groups = []
    near = chips // 2
    groups = [sorted({hop, (chips - hop) % chips}) for hop in range(near + 1)]

    def group_pieces(index, parts):
        return [part for step in groups[index] for part in parts[step]]

    feed_weights = []

    def feed_group(index):
        tokens = jnp.concatenate(group_pieces(index, hidden_parts), axis=0)
        upstream = jnp.concatenate(group_pieces(index, cotangent_job.result), axis=0)
        gate_weights, up_weights, down_weights = feed_weights
        act_grad = col_inner(upstream, down_weights)
        if 0 < index < near:
            activated, gate_grad, up_grad, back = feed_beside(
                group_pieces(index, hidden_parts), act_grad, gate_weights, up_weights
            )
            down = dot(activated, down_weights)
            feed_groups.append((activated, gate_grad, up_grad, back, down))
            return
        gate = col_inner(tokens, gate_weights)
        up_proj = col_inner(tokens, up_weights)
        sigmoid_gate = jax.nn.sigmoid(gate)
        silu_gate = gate * sigmoid_gate
        activated = (silu_gate * up_proj).astype(BF16)
        gate_grad = (
            act_grad * up_proj * sigmoid_gate * (1.0 + gate * (1.0 - sigmoid_gate))
        ).astype(BF16)
        up_grad = (act_grad * silu_gate).astype(BF16)
        back = dot(gate_grad, gate_weights) + dot(up_grad, up_weights)
        down = dot(activated, down_weights)
        feed_groups.append((activated, gate_grad, up_grad, back, down))

    def start_feed():
        feed_weights.extend(wire.along)

    def keep_first():
        feed_group(0)
        feed_groups[0] = wire.tie(*feed_groups[0])

    wire.drive(
        column_gather(hidden_in, hidden_parts),
        hooks=[start_feed, keep_first],
        along=[
            late[:, i * feed_rows : (i + 1) * feed_rows].reshape(-1, width) for i in range(3)
        ],
    )
    for index in range(1, near + 1):
        feed_group(index)

    def group_rows(index, step):
        group = min(step, chips - step)
        at = groups[group].index(step) * pair
        return feed_groups[group][index][at : at + pair]

    hidden_pieces = sum((group_pieces(index, hidden_parts) for index in range(near + 1)), [])
    upstream_pieces = sum(
        (group_pieces(index, cotangent_job.result) for index in range(near + 1)), []
    )
    down_grads = weight_grads([group[0] for group in feed_groups], upstream_pieces, heads, 2, None)
    gate_grads = weight_grads([group[1] for group in feed_groups], hidden_pieces, heads, 0, down_grads)
    feed_grads = [gate_grads]

    def keep_grads():
        downs = [group[4].astype(BF16) for group in feed_groups]
        feed_grads[0], *downs = wire.tie(feed_grads[0], *downs)
        for index, down in enumerate(downs):
            feed_groups[index] = tuple(feed_groups[index][:4]) + (down,)

    def keep_last():
        feed_grads[0] = wire.tie(
            weight_grads([group[2] for group in feed_groups], hidden_pieces, heads, 1, feed_grads[0])
        )[0]

    hidden_grad = wire.drive(
        column_scatter(lambda step: group_rows(3, step), apart=True),
        hooks=[lambda: None] * (near + 1) + [keep_grads],
    )
    hidden_gain_grad = jnp.sum(hidden_grad * middle * scale_two, axis=0)
    middle_grad = own_cotangent.astype(F32) + norm_back(hidden_grad, middle, scale_two, hidden_norm)
    branch_grad = middle_grad.astype(BF16)
    branch_blocks = join_blocks(wire.drive(column_gather(branch_grad), hooks=[keep_last]))
    down_job = wire.add(column_scatter(lambda step: group_rows(4, step)))
    feed_grads = lax.psum_scatter(feed_grads[0], "head", scatter_dimension=0).astype(F32)
    mixed_grads = [col_inner(out_weights, block).astype(BF16) for block in branch_blocks]
    grad_out = dot(mixed, jnp.concatenate(branch_blocks, axis=0)).reshape(heads, out_rows, width)
    out_parts = [pick(grad_out, head ^ place) for place in range(heads)]
    if in_pair:
        pieces = exchange(split_blocks(member, mixed_grads, heads), True)
        upstream = upstream_members(member, odd, pieces, rows)
    else:
        mixed_grad = jnp.concatenate(mixed_grads, axis=1).reshape(heads, out_rows, column)
        every = gather_members(mixed_grad)
        every = jnp.swapaxes(every, 0, 1).reshape(blks, per_device, HD, column)
        upstream = jnp.swapaxes(pick(every, blk), 1, 2).reshape(per_device * column, HD)

    key_grads, value_grads = {}, {}
    carry = None
    for forward, backward in zip(plane_steps(False)[::-1] + [[]], plane_steps(True)[::-1] + [[]]):
        for place in [step[0] for step in forward] if forward else [0]:
            results = attend_back(
                query,
                upstream,
                logs,
                query_places,
                query_starts,
                key_pieces[place],
                value_pieces[place],
                key_places[place : place + 1],
                carry,
                heads_out,
            )
            key_grads[place] = key_grads.get(place, 0.0) + results[1]
            value_grads[place] = value_grads.get(place, 0.0) + results[2]
            carry = (results[0], carry[1] if carry else results[3])
        if not forward:
            break
        if forward == backward:
            items = [
                (
                    jnp.concatenate([key_grads[place], value_grads[place]], axis=1).astype(BF16),
                    head_move(bit),
                )
                for place, source, bit in forward
            ]
        else:
            items = [
                (key_grads[place].astype(BF16), head_move(bit)) for place, source, bit in forward
            ] + [
                (value_grads[place].astype(BF16), head_move(bit))
                for place, source, bit in backward
            ]
        tied = lax.optimization_barrier(tuple(value for value, move in items) + carry)
        items = [(value, move) for value, (ignored, move) in zip(tied, items)]
        carry = tied[len(items) :]
        got = wire.phase(items, behind=True)
        last_parts = got
        if forward[0][1] == 0:
            continue
        for index, (place, source, bit) in enumerate(forward):
            part = got[index][:, :HD].astype(F32)
            key_grads[source] = key_grads.get(source, 0.0) + part
        for index, (place, source, bit) in enumerate(backward):
            part = got[index if forward == backward else len(forward) + index]
            value_grads[source] = value_grads.get(source, 0.0) + part[:, -HD:].astype(F32)
    query_grad = carry[0]

    if in_pair:
        *pieces, gain_grads = rope_back_members(
            member, raw, query_grad, cosine, sine, norms, key_grads[0], value_grads[0], last_parts,
            query_rows, key_rows,
        )
        pieces = exchange(pieces, True)
        raw_grad = join_members(head ^ member, odd, pieces, rows).reshape(-1, column)
    else:
        key_grad = key_grads[0] + sum(part[:, :HD].astype(F32) for part in last_parts)
        value_grad = value_grads[0] + sum(part[:, HD:].astype(F32) for part in last_parts)
        query_grad = jnp.swapaxes(query_grad.reshape(per_device, column, HD), 1, 2)
        query_raw_grad, query_gain_grad = rope_backward(
            query_raw, query_norm, cosine, sine, query_grad
        )
        key_raw_grad, key_gain_grad = rope_backward(key_raw, key_norm, cosine, sine, key_grad.T)
        query_raw_grad = query_raw_grad.astype(BF16)
        key_raw_grad = key_raw_grad.astype(BF16)
        value_raw_grad = value_grad.T.astype(BF16)
        gain_grads = jnp.stack([jnp.sum(query_gain_grad, axis=0), key_gain_grad], axis=1)

        def spread(part, count, index):
            empty = jnp.zeros((count,) + part.shape[1:], BF16)
            return lax.dynamic_update_slice_in_dim(empty, part, index, 0)

        every = jnp.concatenate(
            [
                spread(query_raw_grad, QH, blk * per_device).reshape(shards, query_rows, column),
                spread(key_raw_grad[None], KVH, blk * KVH // blks).reshape(
                    shards, key_rows, column
                ),
                spread(value_raw_grad[None], KVH, blk * KVH // blks).reshape(
                    shards, key_rows, column
                ),
            ],
            axis=1,
        ).reshape(heads, blks, qkv_rows, column)
        every = reorder(jnp.swapaxes(every, 0, 1), to_ring)
        by_head = reorder(lax.psum_scatter(every, "blk", scatter_dimension=0), to_ring)
        raw_grad = jnp.concatenate(
            [pick(by_head, head ^ place) for place in range(heads)], axis=0
        )

    while down_job.wanted is not None:
        wire.phase([], behind=True)
    done = [feed_grads, (middle + down_job.result).astype(BF16)]

    qkv_grad = dot(raw_grad, normed_column)
    input_gain_grad = jnp.sum(qkv_grad * qkv_weights.astype(F32), axis=0) / input_norm
    sums = jnp.concatenate([input_gain_grad, hidden_gain_grad, gain_grads[:, 0], gain_grads[:, 1]])
    qkv_grad = qkv_grad.reshape(heads, qkv_rows, width)
    out_job = Job(plane_scatter(out_parts, True))
    tail = [
        Job(sum_everywhere(sums.reshape(-1, 128))),
        Job(plane_scatter(list(qkv_grad), False, pause=True)),
        out_job,
    ]

    def keep_done():
        done[:] = wire.along

    normed_grad = wire.drive(
        ring_scatter(
            lambda step: row_outer(raw_grad[:, step * pair : (step + 1) * pair], qkv_weights)
        ),
        hooks=[lambda: tail] + [lambda: None] * (chips - 3) + [keep_done],
        along=done,
        beside=chips - 2,
    )
    sums, grad_tail, grad_out = tail[0].result.reshape(-1), tail[1].result, out_job.result
    feed_grads, layer_out = done
    grad_gate, grad_up, grad_down = (
        feed_grads[i * feed_rows : (i + 1) * feed_rows] for i in range(3)
    )
    token_values = wire.token.astype(F32)
    grad_input = middle_grad + norm_back(
        normed_grad, token_values, rms_scale(token_values), input_norm
    )

    def own_part(at, size):
        return lax.dynamic_slice_in_dim(sums, at, size)

    return (
        layer_out,
        grad_input,
        own_part(shard * input_gain.shape[0], input_gain.shape[0]),
        grad_tail[:query_rows].T,
        grad_tail[query_rows : query_rows + key_rows].T,
        grad_tail[query_rows + key_rows :].T,
        own_part(2 * width + shard * query_gain.shape[0], query_gain.shape[0]),
        own_part(2 * width + HD + shard * key_gain.shape[0], key_gain.shape[0]),
        grad_out,
        own_part(width + blk * hidden_gain.shape[0], hidden_gain.shape[0]),
        grad_gate.T,
        grad_up.T,
        grad_down,
    )


def solution(mesh):
    return jax.shard_map(
        local,
        mesh=mesh,
        in_specs=(
            P(("blk", "head"), None),
            P(),
            P(),
            P(("head", "blk")),
            P(None, ("head", "blk")),
            P(None, ("head", "blk")),
            P(None, ("head", "blk")),
            P(("head", "blk")),
            P(("head", "blk")),
            P(("head", "blk"), None),
            P("blk"),
            P(None, ("head", "blk")),
            P(None, ("head", "blk")),
            P(("head", "blk"), None),
            P("blk", None),
        ),
        out_specs=(
            P(("blk", "head"), None),
            P(("blk", "head"), None),
            P(("head", "blk")),
            P(None, ("head", "blk")),
            P(None, ("head", "blk")),
            P(None, ("head", "blk")),
            P(("head", "blk")),
            P(("head", "blk")),
            P(("head", "blk"), None),
            P("blk"),
            P(None, ("head", "blk")),
            P(None, ("head", "blk")),
            P(("head", "blk"), None),
        ),
        check_vma=False,
    )
```

```python
import functools
import math

import jax
import jax.numpy as jnp
import numpy as np
from jax import lax
from jax.experimental import pallas as pl
from jax.experimental.pallas import tpu as pltpu
from jax.sharding import PartitionSpec as P

QH = 16
KVH = 8
HD = 128
HALF = HD // 2
EPSILON = 1e-06
ROPE_BASE = 1000000.0
SCORE_SCALE = HD ** (-0.5)
EXP2_SCALE = SCORE_SCALE * math.log2(math.e)
CONTRACT_ROWS = (((0,), (0,)), ((), ()))
CONTRACT_COLS = (((1,), (1,)), ((), ()))
BF16 = jnp.bfloat16
F32 = jnp.float32
MIB = 1024 * 1024


def dot(left, right):
    return jnp.dot(left, right, preferred_element_type=F32)


def row_outer(left, right):
    return lax.dot_general(left, right, CONTRACT_ROWS, preferred_element_type=F32)


def col_inner(left, right):
    return lax.dot_general(left, right, CONTRACT_COLS, preferred_element_type=F32)


def rms_scale(values):
    return lax.rsqrt(jnp.mean(values * values, axis=-1, keepdims=True) + EPSILON)


def norm_back(upstream, source, scale_rows, gain):
    scaled = upstream * gain
    return scale_rows * scaled - source * scale_rows**3 * jnp.mean(
        scaled * source, axis=-1, keepdims=True
    )


def head_bits():
    count = lax.axis_size("head")
    return [1 << i for i in range(count.bit_length() - 1)]


def head_move(bit):
    count = lax.axis_size("head")
    return ("head", [(i, i ^ bit) for i in range(count)], bit)


def blk_move(steps, flip, link):
    count = lax.axis_size("blk")
    return ("blk", [(i, ((i + 2 * steps) % count) ^ flip) for i in range(count)], link)


def swap_move():
    return blk_move(0, 1, None)


def ring_move(steps):
    return blk_move(steps, 0, "z")


def member_move(flip):
    count = lax.axis_size("blk")
    return ("blk", [(i, i ^ flip) for i in range(count)], "z" if flip > 1 else None)


class Job:
    def __init__(self, steps):
        self.steps = steps
        self.wanted = None
        self.result = None
        self.advance(None)

    def advance(self, got):
        try:
            self.wanted = self.steps.send(got)
        except StopIteration as end:
            self.wanted = None
            self.result = end.value


class Wire:
    def __init__(self, token):
        self.token = token
        self.jobs = []

    def add(self, steps):
        job = Job(steps)
        self.jobs.append(job)
        return job

    def tie(self, *arrays):
        *arrays, self.token = lax.optimization_barrier(arrays + (self.token,))
        return arrays

    def phase(self, items, behind=False, riders=(), along=()):
        items = list(items)
        count = len(items)
        taken = []
        for job in list(riders) + (self.jobs if behind else []):
            if job.wanted is not None:
                taken.append((job, len(items), len(items) + len(job.wanted)))
                items.extend(job.wanted)
        if not items:
            for job, start, end in taken:
                job.advance([])
            return []
        values = self.tie(*[value for value, move in items])
        outs = [lax.ppermute(value, move[0], move[1]) for value, (same, move) in zip(values, items)]
        outs = self.tie(*outs, *along)
        self.along = outs[len(items) :]
        for job, start, end in taken:
            job.advance(outs[start:end])
        self.jobs = [job for job in self.jobs if job.wanted is not None]
        return outs[:count]

    def drive(self, steps, hooks=(), riders=(), behind=None, along=(), beside=0):
        job = Job(steps)
        riders = list(riders)
        hooks = list(hooks)
        count = 0
        while job.wanted is not None or any(rider.wanted is not None for rider in riders):
            got = self.phase(
                job.wanted or [],
                riders=riders,
                behind=behind is not None and count >= behind,
                along=along if count == beside else (),
            )
            if job.wanted is not None:
                job.advance(got)
            if hooks:
                riders.extend(hooks.pop(0)() or [])
            count += 1
        return job.result


def column_gather(value, blocks=None):
    chips = lax.axis_size("blk") // 2
    near = chips // 2
    blocks = {} if blocks is None else blocks
    fresh = {0: value}
    up = down = value
    for hop in range(1, near + 2):
        items = [(part, swap_move()) for part in fresh.values()]
        if hop <= near:
            items.append((up, ring_move(1)))
        if hop <= chips - 1 - near:
            items.append((down, ring_move(-1)))
        got = yield items
        for (step, part), other in zip(fresh.items(), got):
            blocks[step] = [part, other]
        got = got[len(fresh) :]
        fresh = {}
        if got:
            up = fresh[hop] = got[0]
        if len(got) > 1:
            down = fresh[chips - hop] = got[1]
    return [blocks[step] for step in range(chips)]


def ring_gather(value):
    chips = lax.axis_size("blk") // 2
    blocks = []
    for step in range(chips):
        items = [(value, swap_move())]
        if step < chips - 1:
            items.append((value, ring_move(1)))
        got = yield items
        blocks.append([value, got[0]])
        value = got[-1]
    return blocks


def ring_scatter(part_of):
    chips = lax.axis_size("blk") // 2
    order = list(range(1, chips)) + [0]

    def halves(step):
        part = part_of(step)
        rows = part.shape[0] // 2
        return part[:rows], part[rows:]

    own, other = halves(order[0])
    got = yield [(other.astype(BF16), swap_move())]
    total = own.astype(F32) + got[0].astype(F32)
    for step in order[1:]:
        own, other = halves(step)
        got = yield [(total.astype(BF16), ring_move(1)), (other.astype(BF16), swap_move())]
        total = own.astype(F32) + got[1].astype(F32) + got[0].astype(F32)
    return total


def join_blocks(blocks):
    return [jnp.concatenate(block, axis=0) for block in blocks]


def column_scatter(part_of, apart=False):
    chips = lax.axis_size("blk") // 2
    near = chips // 2
    totals = {}

    def swaps(steps):
        parts = {step: part_of(step) for step in steps}
        half = parts[steps[0]].shape[0] // 2
        items = [(parts[step][half:].astype(BF16), swap_move()) for step in steps]
        return items, {step: part[:half] for step, part in parts.items()}

    def add(own, got):
        for (step, part), other in zip(own.items(), got):
            totals[step] = part.astype(F32) + other.astype(F32) + totals.get(step, 0.0)

    items, own = swaps([near])
    add(own, (yield items))
    for hop in range(near, 0, -1):
        both = hop <= chips - 1 - near
        moves = [(totals[hop].astype(BF16), ring_move(-1))]
        if both:
            moves.append((totals[chips - hop].astype(BF16), ring_move(1)))
        steps = sorted({hop - 1, (chips - hop + 1) % chips})
        if apart:
            got = yield moves
            items, own = swaps(steps)
            add(own, (yield items))
            apart = False
        else:
            items, own = swaps(steps)
            got = yield moves + items
            add(own, got[len(moves) :])
        totals[hop - 1] = totals[hop - 1] + got[0].astype(F32)
        if both:
            step = (chips - hop + 1) % chips
            totals[step] = totals[step] + got[1].astype(F32)
    return totals[0]


def plane_steps(backwards):
    bits = head_bits()
    order = bits[::-1] if backwards else bits
    steps = []
    for weight in range(1, len(bits) + 1):
        step = []
        for place in range(1 << len(bits)):
            if bin(place).count("1") == weight:
                last = [bit for bit in order if place & bit][-1]
                step.append((place, place ^ last, last))
        steps.append(step)
    return steps


def plane_gather(value, backwards):
    pieces = {0: value}
    for step in plane_steps(backwards):
        got = yield [(pieces[source], head_move(bit)) for place, source, bit in step]
        for (place, source, bit), piece in zip(step, got):
            pieces[place] = piece
    return [pieces[i] for i in range(len(pieces))]


def plane_scatter(parts, backwards, pause=False):
    pieces = list(parts)
    for index, step in enumerate(plane_steps(backwards)[::-1]):
        if pause and index == 1:
            yield []
        got = yield [(pieces[place].astype(BF16), head_move(bit)) for place, source, bit in step]
        for (place, source, bit), piece in zip(step, got):
            pieces[source] = pieces[source] + piece.astype(F32)
    return pieces[0]


def sum_everywhere(value):
    chips = lax.axis_size("blk") // 2
    for moves in (
        *([head_move(bit)] for bit in head_bits()),
        [swap_move()],
        [blk_move(steps, 0, None) for steps in range(1, chips)],
    ):
        got = yield [(value, move) for move in moves]
        for part in got:
            value = value + part
    return value


def pick(stack, index):
    return lax.dynamic_index_in_dim(stack, index, 0, keepdims=False)


def token_starts(anchors, lengths):
    ends = jnp.cumsum(lengths)
    seq_starts = ends - lengths
    inside = seq_starts[None, :] <= anchors[:, None]
    return jnp.max(jnp.where(inside, seq_starts[None, :], 0), axis=1)


def rope_tables(places):
    ladder = jnp.arange(HALF, dtype=F32)
    rates = jnp.exp(ladder * (-2.0 * math.log(ROPE_BASE) / HD))
    angles = rates[:, None] * places.astype(F32)[None, :]
    return (jnp.cos(angles), jnp.sin(angles))


def rope_forward(raw, gain, cosine, sine):
    heads = raw.astype(F32)
    scale = lax.rsqrt(jnp.mean(heads * heads, axis=-2, keepdims=True) + EPSILON)
    normed = heads * scale * gain[:, None]
    low, high = normed[..., :HALF, :], normed[..., HALF:, :]
    return jnp.concatenate([low * cosine - high * sine, high * cosine + low * sine], axis=-2)


def rope_backward(raw, gain, cosine, sine, upstream):
    heads = raw.astype(F32)
    scale = lax.rsqrt(jnp.mean(heads * heads, axis=-2, keepdims=True) + EPSILON)
    low, high = upstream[..., :HALF, :], upstream[..., HALF:, :]
    turned = jnp.concatenate([low * cosine + high * sine, high * cosine - low * sine], axis=-2)
    gain_grad = jnp.sum(turned * heads * scale, axis=-1)
    scaled = turned * gain[:, None]
    back = scale * scaled - heads * scale**3 * jnp.mean(scaled * heads, axis=-2, keepdims=True)
    return back, gain_grad


def small_call(kernel, outs, scalars, arrays, scratch=()):
    vmem = pl.BlockSpec(memory_space=pltpu.VMEM)
    return pl.pallas_call(
        kernel,
        in_specs=[pl.BlockSpec(memory_space=pltpu.SMEM)] + [vmem] * len(arrays),
        out_specs=[vmem] * len(outs),
        out_shape=[jax.ShapeDtypeStruct(shape, dtype) for shape, dtype in outs],
        scratch_shapes=[pltpu.VMEM(shape, dtype) for shape, dtype in scratch],
        compiler_params=pltpu.CompilerParams(vmem_limit_bytes=10 * MIB),
        cost_estimate=pl.CostEstimate(
            flops=0,
            bytes_accessed=3 * sum(array.size * array.dtype.itemsize for array in arrays),
            transcendentals=0,
        ),
    )(scalars, *arrays)


def table_kernel(blocks, sequences, index_ref, deal_ref, rate_ref, key_ref, start_ref, cos_ref, sin_ref):
    heads, column = key_ref.shape
    rows = column // blocks
    for place in range(heads):
        for block in range(blocks):
            row = deal_ref[pl.ds(index_ref[place * blocks + block], 1), :]
            key_ref[place : place + 1, block * rows : (block + 1) * rows] = row
    own = key_ref[0:1, :]
    starts = jnp.zeros_like(own)
    first = jnp.int32(0)
    for sequence in range(sequences - 1):
        first = first + index_ref[heads * blocks + sequence]
        starts = jnp.where(own >= first, first, starts)
    start_ref[...] = starts
    angles = rate_ref[:, :1] * (own - starts).astype(F32)
    cos_ref[...] = jnp.cos(angles)
    sin_ref[...] = jnp.sin(angles)


def tables(index, lengths, deals, column, heads):
    rates = np.exp(
        np.arange(HALF, dtype=np.float32) * np.float32(-2.0 * math.log(ROPE_BASE) / HD)
    ).astype(np.float32)
    return small_call(
        functools.partial(table_kernel, column // deals.shape[1], lengths.shape[0]),
        [
            ((heads, column), jnp.int32),
            ((1, column), jnp.int32),
            ((HALF, column), F32),
            ((HALF, column), F32),
        ],
        jnp.concatenate([index, lengths]),
        [deals, jnp.asarray(np.broadcast_to(rates[:, None], (HALF, 128)))],
    )


def put_in_order(out_ref, scalar_ref, pieces, rows, finish):
    base = scalar_ref[0]
    for flip, piece in enumerate(pieces):
        value = piece[...]
        column = value.shape[1]
        if flip & 1:
            cuts = [value[:, i * rows : (i + 1) * rows] for i in range(column // rows)]
            value = jnp.concatenate([cuts[i ^ 1] for i in range(column // rows)], axis=1)
        at = pl.ds(base ^ flip, 1)
        if flip & 2:
            pair = 2 * rows

            @pl.when(scalar_ref[1] == 0)
            def _(at=at, value=value, pair=pair):
                out_ref[at] = jnp.concatenate([value[:, pair:], value[:, :pair]], axis=1)[None]

            @pl.when(scalar_ref[1] != 0)
            def _(at=at, value=value, pair=pair):
                out_ref[at] = jnp.concatenate([value[:, -pair:], value[:, :-pair]], axis=1)[None]

        else:
            out_ref[at] = value[None]
    finish()


def join_members(base, odd, pieces, rows):
    count = len(pieces)

    def kernel(scalar_ref, *refs):
        put_in_order(refs[count], scalar_ref, refs[:count], rows, lambda: None)

    return small_call(
        kernel,
        [((count,) + pieces[0].shape, BF16)],
        jnp.stack([base, odd]).astype(jnp.int32),
        pieces,
    )[0]


def split_blocks(base, blocks, count):
    size = blocks[0].shape[0] // count
    width = blocks[0].shape[1]

    def kernel(scalar_ref, *refs):
        for flip in range(count):
            start = pl.multiple_of((scalar_ref[0] ^ flip) * size, size)
            for index in range(len(blocks)):
                refs[len(blocks) + flip][:, index * width : (index + 1) * width] = refs[index][
                    pl.ds(start, size), :
                ]

    return small_call(
        kernel,
        [((size, width * len(blocks)), BF16)] * count,
        base.reshape(1).astype(jnp.int32),
        blocks,
    )


def rope_kernel(rows, query_rows, key_rows, scalar_ref, *refs):
    pieces = refs[:-6]
    cos_ref, sin_ref, gain_ref, raw_ref, query_ref, pair_ref = refs[-6:]
    count, column = len(pieces), cos_ref.shape[1]
    put_in_order(raw_ref, scalar_ref, pieces, rows, lambda: None)
    cosine, sine = cos_ref[...], sin_ref[...]

    def rotate(parts, gain):
        heads = jnp.concatenate(parts, axis=0).astype(F32)
        scale = lax.rsqrt(jnp.mean(heads * heads, axis=0, keepdims=True) + EPSILON)
        normed = heads * scale * gain
        low, high = normed[:HALF], normed[HALF:]
        turned = jnp.concatenate([low * cosine - high * sine, high * cosine + low * sine], axis=0)
        return turned

    per_head = HD // query_rows
    for head in range(count // per_head):
        parts = [raw_ref[head * per_head + i, :query_rows, :] for i in range(per_head)]
        turned = rotate(parts, gain_ref[:, 0:1]) * EXP2_SCALE
        query_ref[head * column : (head + 1) * column, :] = turned.T.astype(BF16)
    parts = [raw_ref[i, query_rows : query_rows + key_rows, :] for i in range(count)]
    pair_ref[:, :HD] = rotate(parts, gain_ref[:, 1:2]).T.astype(BF16)
    parts = [raw_ref[i, query_rows + key_rows :, :] for i in range(count)]
    pair_ref[:, HD:] = jnp.concatenate(parts, axis=0).astype(F32).T.astype(BF16)


def rope_members(base, odd, pieces, cosine, sine, gains, rows, query_rows, key_rows):
    count, column = len(pieces), cosine.shape[1]
    return small_call(
        functools.partial(rope_kernel, rows, query_rows, key_rows),
        [
            ((count,) + pieces[0].shape, BF16),
            ((count * query_rows // HD * column, HD), BF16),
            ((column, 2 * HD), BF16),
        ],
        jnp.stack([base, odd]).astype(jnp.int32),
        list(pieces) + [cosine, sine, gains],
    )


def mixed_kernel(scalar_ref, in_ref, *refs):
    outs, parts_ref = refs[:-1], refs[-1]
    count, size, column = parts_ref.shape
    for head in range(in_ref.shape[0] // column):
        part = in_ref[head * column : (head + 1) * column, :].T.astype(BF16)
        per_head = HD // size
        for i in range(per_head):
            parts_ref[head * per_head + i] = part[i * size : (i + 1) * size]
    for flip, out_ref in enumerate(outs):
        out_ref[...] = parts_ref[scalar_ref[0] ^ flip]


def mixed_members(base, heads_out, count, column):
    size = heads_out.shape[0] // column * HD // count
    return small_call(
        mixed_kernel,
        [((size, column), BF16)] * count,
        base.reshape(1).astype(jnp.int32),
        [heads_out],
        [((count, size, column), BF16)],
    )


def upstream_members(base, odd, pieces, rows):
    count = len(pieces)
    size, column = pieces[0].shape
    per_head = HD // size

    def kernel(scalar_ref, *refs):
        out_ref, parts_ref = refs[count:]
        put_in_order(parts_ref, scalar_ref, refs[:count], rows, lambda: None)
        for head in range(count // per_head):
            parts = [parts_ref[head * per_head + i] for i in range(per_head)]
            out_ref[head * column : (head + 1) * column, :] = (
                jnp.concatenate(parts, axis=0).astype(F32).T.astype(BF16)
            )

    return small_call(
        kernel,
        [((count // per_head * column, HD), BF16)],
        jnp.stack([base, odd]).astype(jnp.int32),
        pieces,
        [((count, size, column), BF16)],
    )[0]


def light():
    return pl.CostEstimate(flops=1, bytes_accessed=1, transcendentals=0)


def feed_kernel(count, *refs):
    tokens = refs[:count]
    grad_ref, gate_ref, up_ref, act_out, gate_out, up_out, back_out, token_ref, total_ref = refs[
        count:
    ]
    step = pl.program_id(0)

    @pl.when(step == 0)
    def _():
        rows = tokens[0].shape[0]
        for index in range(count):
            token_ref[index * rows : (index + 1) * rows, :] = tokens[index][...]
        total_ref[...] = jnp.zeros_like(total_ref)

    gate = col_inner(token_ref[...], gate_ref[...])
    up_proj = col_inner(token_ref[...], up_ref[...])
    act_grad = grad_ref[...]
    sigmoid_gate = jax.nn.sigmoid(gate)
    silu_gate = gate * sigmoid_gate
    gate_grad = (act_grad * up_proj * sigmoid_gate * (1.0 + gate * (1.0 - sigmoid_gate))).astype(
        BF16
    )
    up_grad = (act_grad * silu_gate).astype(BF16)
    act_out[...] = (silu_gate * up_proj).astype(BF16)
    gate_out[...] = gate_grad
    up_out[...] = up_grad
    total_ref[...] += dot(gate_grad, gate_ref[...]) + dot(up_grad, up_ref[...])

    @pl.when(step == pl.num_programs(0) - 1)
    def _():
        back_out[...] = total_ref[...].astype(BF16)


def feed_beside(tokens, act_grad, gate_weights, up_weights):
    piece, width = tokens[0].shape
    rows, hidden = act_grad.shape
    tile = hidden // 3
    part = pl.BlockSpec((rows, tile), lambda i: (0, i))
    weight = pl.BlockSpec((tile, width), lambda i: (i, 0))
    whole = lambda i: (0, 0)
    return pl.pallas_call(
        functools.partial(feed_kernel, len(tokens)),
        grid=(3,),
        in_specs=[pl.BlockSpec((piece, width), whole)] * len(tokens) + [part, weight, weight],
        out_specs=[part] * 3 + [pl.BlockSpec((rows, width), whole)],
        out_shape=[jax.ShapeDtypeStruct((rows, hidden), BF16)] * 3
        + [jax.ShapeDtypeStruct((rows, width), BF16)],
        scratch_shapes=[pltpu.VMEM((rows, width), BF16), pltpu.VMEM((rows, width), F32)],
        compiler_params=pltpu.CompilerParams(vmem_limit_bytes=24 * MIB),
        cost_estimate=light(),
    )(*tokens, act_grad, gate_weights, up_weights)


def weight_grad_kernel(count, groups, *refs):
    pieces, lefts = refs[:count], refs[count : count + groups]
    out_ref, right_ref = refs[-2:]
    rows = pieces[0].shape[0]

    @pl.when(pl.program_id(0) == 0)
    def _():
        for index in range(count):
            right_ref[index * rows : (index + 1) * rows, :] = pieces[index][...]

    size = out_ref.shape[1]
    for head in range(lefts[0].shape[1] // size):

        @pl.when(pl.program_id(0) == head)
        def _(head=head):
            cut = slice(head * size, (head + 1) * size)
            left = jnp.concatenate([ref[:, cut] for ref in lefts], axis=0)
            out_ref[0] = row_outer(left, right_ref[...]).astype(BF16)


def weight_grads(lefts, pieces, heads, kind, into):
    size = lefts[0].shape[1] // heads
    piece, width = pieces[0].shape
    count = len(pieces)
    specs = [pl.BlockSpec((piece, width), lambda i: (0, 0))] * count
    specs += [pl.BlockSpec(left.shape, lambda i: (0, 0)) for left in lefts]
    operands = list(pieces) + list(lefts)
    aliases = {}
    if into is not None:
        specs.append(pl.BlockSpec(memory_space=pl.ANY))
        aliases = {len(operands): 0}
        operands.append(into)
    return pl.pallas_call(
        functools.partial(weight_grad_kernel, count, len(lefts)),
        grid=(heads,),
        in_specs=specs,
        out_specs=pl.BlockSpec((1, size, width), lambda i: (i, kind, 0)),
        out_shape=jax.ShapeDtypeStruct((heads, 3 * size, width), BF16),
        scratch_shapes=[pltpu.VMEM((count * piece, width), BF16)],
        input_output_aliases=aliases,
        compiler_params=pltpu.CompilerParams(vmem_limit_bytes=20 * MIB),
        cost_estimate=light(),
    )(*operands)


def rope_back_kernel(query_rows, key_rows, count, scalar_ref, *refs):
    raw_ref, dq_ref, cos_ref, sin_ref, gain_ref, dk_ref, dv_ref = refs[:7]
    more = refs[7 : -2 - count]
    outs, gain_out, parts_ref = refs[-2 - count : -2], refs[-2], refs[-1]
    column = cos_ref.shape[1]
    cosine, sine = cos_ref[...], sin_ref[...]

    def back(parts, gain, upstream):
        heads = jnp.concatenate(parts, axis=0).astype(F32)
        scale = lax.rsqrt(jnp.mean(heads * heads, axis=0, keepdims=True) + EPSILON)
        low, high = upstream[:HALF], upstream[HALF:]
        turned = jnp.concatenate([low * cosine + high * sine, high * cosine - low * sine], axis=0)
        gain_grad = jnp.sum(turned * heads * scale, axis=1, keepdims=True)
        scaled = turned * gain
        mean = jnp.mean(scaled * heads, axis=0, keepdims=True)
        return (scale * scaled - heads * (scale * scale * scale * mean)).astype(BF16), gain_grad

    per_head = HD // query_rows
    total = jnp.zeros((HD, 1), F32)
    for head in range(count // per_head):
        at = [head * per_head + i for i in range(per_head)]
        grad, gain_grad = back(
            [raw_ref[i, :query_rows, :] for i in at],
            gain_ref[:, 0:1],
            dq_ref[head * column : (head + 1) * column, :].T,
        )
        total = total + gain_grad
        for place, i in enumerate(at):
            parts_ref[i, :query_rows, :] = grad[place * query_rows : (place + 1) * query_rows]
    gain_out[:, 0:1] = total
    key_grad, value_grad = dk_ref[...], dv_ref[...]
    for ref in more:
        key_grad = key_grad + ref[:, :HD].astype(F32)
        value_grad = value_grad + ref[:, HD:].astype(F32)
    grad, gain_grad = back(
        [raw_ref[i, query_rows : query_rows + key_rows, :] for i in range(count)],
        gain_ref[:, 1:2],
        key_grad.T,
    )
    gain_out[:, 1:2] = gain_grad
    value_grad = value_grad.T.astype(BF16)
    for i in range(count):
        cut = slice(i * key_rows, (i + 1) * key_rows)
        parts_ref[i, query_rows : query_rows + key_rows, :] = grad[cut]
        parts_ref[i, query_rows + key_rows :, :] = value_grad[cut]
    for flip, out_ref in enumerate(outs):
        out_ref[...] = parts_ref[scalar_ref[0] ^ flip]


def rope_back_members(base, raw, dq, cosine, sine, gains, dk, dv, more, query_rows, key_rows):
    count, size, column = raw.shape
    return small_call(
        functools.partial(rope_back_kernel, query_rows, key_rows, count),
        [((size, column), BF16)] * count + [((HD, 2), F32)],
        base.reshape(1).astype(jnp.int32),
        [raw, dq, cosine, sine, gains, dk, dv] + list(more),
        [((count, size, column), BF16)],
    )


def attend_kernel(first, last, *refs):
    refs = list(refs)
    q_ref, k_ref, v_ref, qpos_ref, qlow_ref, kpos_ref = refs[:6]
    outs = refs[6:] if first else refs[7:]
    kpos = kpos_ref[...]
    scores = col_inner(q_ref[...], k_ref[...])
    rows = q_ref.shape[0]
    qpos = jnp.broadcast_to(qpos_ref[...], (8, rows)).T[:, :1]
    qlow = jnp.broadcast_to(qlow_ref[...], (8, rows)).T[:, :1]
    allowed = (kpos <= qpos) & (kpos >= qlow)
    lifted = jnp.where(allowed, jnp.exp2(scores), 0.0).astype(BF16)
    values = jnp.concatenate([v_ref[...], jnp.ones(v_ref.shape, BF16)], axis=1)
    total = dot(lifted, values)
    if not first:
        total = total + refs[6][...]
    if last:
        weight = total[:, HD:]
        outs[0][...] = total[:, :HD] / weight
        outs[1][...] = jnp.log2(weight).T[:8, :]
    else:
        outs[0][...] = total


def attend(query, keys, values, qpos, qlow, kpos, total, last):
    rows, tokens = query.shape[0], keys.shape[0]
    value_at = values.shape[1] // HD - 1
    own = qpos.shape[1]
    block = 1024
    wrap = own // block
    first = total is None
    cost = pl.CostEstimate(
        flops=20 * rows * tokens * HD, bytes_accessed=4 * tokens * HD, transcendentals=rows * tokens
    )
    whole = lambda i: (0, 0)
    return pl.pallas_call(
        functools.partial(attend_kernel, first, last),
        grid=(rows // block,),
        in_specs=[
            pl.BlockSpec((block, HD), lambda i: (i, 0)),
            pl.BlockSpec((tokens, HD), whole),
            pl.BlockSpec((tokens, HD), lambda i: (0, value_at)),
            pl.BlockSpec((1, block), lambda i: (0, i % wrap)),
            pl.BlockSpec((1, block), lambda i: (0, i % wrap)),
            pl.BlockSpec((1, tokens), whole),
        ]
        + ([] if first else [pl.BlockSpec((block, 2 * HD), lambda i: (i, 0))]),
        out_specs=[
            pl.BlockSpec((block, HD), lambda i: (i, 0)),
            pl.BlockSpec((8, block), lambda i: (0, i)),
        ]
        if last
        else pl.BlockSpec((block, 2 * HD), lambda i: (i, 0)),
        out_shape=[
            jax.ShapeDtypeStruct((rows, HD), F32),
            jax.ShapeDtypeStruct((8, rows), F32),
        ]
        if last
        else jax.ShapeDtypeStruct((rows, 2 * HD), F32),
        compiler_params=pltpu.CompilerParams(vmem_limit_bytes=40 * MIB),
        cost_estimate=cost,
    )(query, keys, values, qpos, qlow, kpos, *([] if first else [total]))


def attend_back_kernel(
    chunk, own, first, q_ref, g_ref, log_ref, qpos_ref, qlow_ref, k_ref, v_ref, kpos_ref,
    in_ref, extra_ref, dq_ref, dk_ref, dv_ref, *new_ref,
):
    rows = q_ref.shape[0]
    delta_ref = new_ref[0] if first else extra_ref

    @pl.when(pl.program_id(0) == 0)
    def _():
        if first:
            dq_ref[...] = jnp.zeros_like(dq_ref)
            for i in range(rows // chunk):
                at = pl.ds(i * chunk, chunk)
                product = g_ref[at, :].astype(F32) * in_ref[at, :]
                sums = jnp.sum(product.T, axis=0, keepdims=True)
                delta_ref[:, at] = jnp.broadcast_to(sums, (8, chunk))
        else:
            dq_ref[...] = in_ref[...]

    keys = k_ref[...]
    values = v_ref[...]
    kpos = jnp.broadcast_to(kpos_ref[...], (8, keys.shape[0])).T[:, :1]
    key_sum = jnp.zeros(keys.shape, F32)
    value_sum = jnp.zeros(keys.shape, F32)
    for i in range(rows // chunk):
        at = pl.ds(i * chunk, chunk)
        place = pl.ds((i * chunk) % own, chunk)
        query = q_ref[at, :]
        upstream = g_ref[at, :]
        scores = col_inner(keys, query)
        allowed = (kpos <= qpos_ref[:, place]) & (kpos >= qlow_ref[:, place])
        probs = jnp.where(allowed, jnp.exp2(scores - log_ref[0:1, at]), 0.0)
        prob_grad = col_inner(values, upstream)
        score_grad = (probs * (prob_grad - delta_ref[0:1, at])).astype(BF16)
        value_sum = value_sum + dot(probs.astype(BF16), upstream)
        key_sum = key_sum + dot(score_grad, query)
        dq_ref[at, :] += row_outer(score_grad, keys) * SCORE_SCALE
    dk_ref[...] = key_sum * (SCORE_SCALE / EXP2_SCALE)
    dv_ref[...] = value_sum


def attend_back(query, upstream, logs, qpos, qlow, keys, values, kpos, before, out):
    rows, tokens = query.shape[0], keys.shape[0]
    value_at = values.shape[1] // HD - 1
    own = qpos.shape[1]
    block = 1024
    first = before is None
    cost = pl.CostEstimate(
        flops=32 * rows * tokens * HD, bytes_accessed=8 * tokens * HD, transcendentals=rows * tokens
    )
    whole = lambda i: (0, 0)
    taken = (out, logs) if first else before
    return pl.pallas_call(
        functools.partial(attend_back_kernel, 512, own, first),
        grid=(tokens // block,),
        in_specs=[
            pl.BlockSpec((rows, HD), whole),
            pl.BlockSpec((rows, HD), whole),
            pl.BlockSpec((8, rows), whole),
            pl.BlockSpec((1, own), whole),
            pl.BlockSpec((1, own), whole),
            pl.BlockSpec((block, HD), lambda i: (i, 0)),
            pl.BlockSpec((block, HD), lambda i: (i, value_at)),
            pl.BlockSpec((1, block), lambda i: (0, i)),
            pl.BlockSpec((rows, HD), whole),
            pl.BlockSpec((8, rows), whole),
        ],
        out_specs=[
            pl.BlockSpec((rows, HD), whole),
            pl.BlockSpec((block, HD), lambda i: (i, 0)),
            pl.BlockSpec((block, HD), lambda i: (i, 0)),
        ]
        + ([pl.BlockSpec((8, rows), whole)] if first else []),
        out_shape=[
            jax.ShapeDtypeStruct((rows, HD), F32),
            jax.ShapeDtypeStruct((tokens, HD), F32),
            jax.ShapeDtypeStruct((tokens, HD), F32),
        ]
        + ([jax.ShapeDtypeStruct((8, rows), F32)] if first else []),
        compiler_params=pltpu.CompilerParams(vmem_limit_bytes=28 * MIB),
        cost_estimate=cost,
    )(query, upstream, logs, qpos, qlow, keys, values, kpos, *taken)


def local(
    inputs,
    dealing,
    lengths,
    input_gain,
    w_query,
    w_key,
    w_value,
    query_gain,
    key_gain,
    w_out,
    hidden_gain,
    w_gate,
    w_up,
    w_down,
    cotangent,
):
    heads, blks = lax.axis_size("head"), lax.axis_size("blk")
    head, blk = lax.axis_index("head"), lax.axis_index("blk")
    shards = heads * blks
    chips = blks // 2
    chip, core = blk // 2, blk % 2
    shard = head * blks + blk
    rows, width = inputs.shape
    column = rows * blks
    pair = 2 * rows
    per_device = QH // blks
    query_rows, key_rows = w_query.shape[1], w_key.shape[1]
    qkv_rows = query_rows + 2 * key_rows
    in_pair = shards // KVH == heads and blks == 2 * heads

    gains = jnp.zeros((2 * width + 2 * HD,), F32)
    hidden_part = jnp.where(head == 0, hidden_gain.astype(F32), 0.0)
    for at, part in (
        (shard * input_gain.shape[0], input_gain),
        (width + blk * hidden_gain.shape[0], hidden_part),
        (2 * width + shard * query_gain.shape[0], query_gain),
        (2 * width + HD + shard * key_gain.shape[0], key_gain),
    ):
        gains = lax.dynamic_update_slice(gains, part.astype(F32), (at,))
    wire = Wire(inputs)

    index = jnp.stack(
        [
            (((chip - step) % chips) * 2 + (core ^ flip)) * heads + (head ^ place)
            for place in range(heads)
            for step in range(chips)
            for flip in range(2)
        ]
    )
    key_places, query_starts, cosine, sine = tables(
        index, lengths, dealing.reshape(blks * heads, rows), column, heads
    )
    query_places = key_places[:1]

    qkv_job = Job(
        plane_gather(jnp.concatenate([w_query.T, w_key.T, w_value.T], axis=0), False)
    )
    gain_job = Job(sum_everywhere(gains.reshape(-1, 128)))
    own_cotangent = lax.dynamic_slice_in_dim(cotangent, head * rows, rows, 0)
    cotangent_job = wire.add(ring_gather(own_cotangent))
    token_blocks = wire.drive(
        column_gather(inputs), riders=[qkv_job], hooks=[lambda: [gain_job]]
    )
    qkv_weights, gains = qkv_job.result, gain_job.result
    token_blocks = [part for parts in token_blocks for part in parts]
    token_blocks[chips:] = wire.tie(*token_blocks[chips:])
    gains = gains.reshape(-1)
    input_norm = gains[:width]
    hidden_norm = gains[width : 2 * width]
    query_norm = gains[2 * width : 2 * width + HD]
    key_norm = gains[2 * width + HD :]
    qkv_weights = jnp.concatenate(qkv_weights, axis=0)
    feed_rows, out_rows = w_down.shape[0], w_out.shape[0]
    out_weights = lax.all_gather(wire.tie(w_out)[0], "head", axis=0, tiled=True)
    column_values = jnp.concatenate(token_blocks, axis=0).astype(F32)
    normed_column = (column_values * rms_scale(column_values) * input_norm).astype(BF16)
    raw = col_inner(qkv_weights, normed_column).astype(BF16)
    wire.phase([], behind=True, along=[raw])
    raw = wire.along[0]
    norms = jnp.stack([query_norm, key_norm], axis=1)

    def reorder(value, index):
        cut = value.reshape(value.shape[:-1] + (blks, rows))
        return jnp.take(cut, index, axis=-2).reshape(value.shape)

    places = jnp.arange(blks)
    to_ring = ((chip - places // 2) % chips) * 2 + ((places % 2) ^ core)

    def gather_members(value):
        return reorder(lax.all_gather(reorder(value, to_ring), "blk", axis=0), to_ring)

    def exchange(pieces, behind=False):
        return [pieces[0]] + wire.phase(
            [(pieces[flip], member_move(flip)) for flip in range(1, heads)], behind
        )

    member = blk % heads
    odd = chip % 2
    if in_pair:
        pieces = exchange(split_blocks(head ^ member, [raw], heads))
        raw, query, key_value = rope_members(
            member, odd, pieces, cosine, sine, norms, rows, query_rows, key_rows
        )
    else:
        raw = raw.reshape(heads, qkv_rows, column)
        by_head = jnp.stack([pick(raw, head ^ place) for place in range(heads)])
        every = jnp.swapaxes(gather_members(by_head), 0, 1)
        every = every.reshape(shards, qkv_rows, column)
        query_all = every[:, :query_rows].reshape(QH, HD, column)
        key_all = every[:, query_rows : query_rows + key_rows].reshape(KVH, HD, column)
        value_all = every[:, query_rows + key_rows :].reshape(KVH, HD, column)
        query_raw = lax.dynamic_slice_in_dim(query_all, blk * per_device, per_device, 0)
        key_raw = pick(key_all, blk * KVH // blks)
        value_raw = pick(value_all, blk * KVH // blks)

        query = (rope_forward(query_raw, query_norm, cosine, sine) * EXP2_SCALE).astype(BF16)
        keys = rope_forward(key_raw, key_norm, cosine, sine).astype(BF16)
        query = jnp.swapaxes(query, 1, 2).reshape(per_device * column, HD)
        key_value = jnp.concatenate([keys.T, value_raw.T], axis=1)

    pairs = {0: key_value}
    key_pieces, value_pieces = dict(pairs), dict(pairs)
    total = None

    def add_column(place, total):
        return attend(
            query,
            key_pieces[place],
            value_pieces[place],
            query_places,
            query_starts,
            key_places[place : place + 1],
            total,
            place == heads - 1,
        )

    ready = [0]
    for forward, backward in zip(plane_steps(False), plane_steps(True)):
        if forward == backward:
            items = [(pairs[source], head_move(bit)) for place, source, bit in forward]
        else:
            items = [
                (key_pieces[source][:, :HD], head_move(bit)) for place, source, bit in forward
            ] + [(value_pieces[source][:, -HD:], head_move(bit)) for place, source, bit in backward]
        for place in ready:
            total = add_column(place, total)
        got = wire.phase(items, behind=True, along=[total])
        total = wire.along[0]
        if ready == [0]:
            late = wire.tie(jnp.concatenate([w_gate.T, w_up.T, w_down], axis=0))[0]
        ready = [place for place, source, bit in forward]
        for index, place in enumerate(ready):
            key_pieces[place] = got[index]
            if forward == backward:
                value_pieces[place] = pairs[place] = got[index]
            else:
                value_pieces[backward[index][0]] = got[len(forward) + index]
    for place in ready:
        total = add_column(place, total)
    heads_out, logs = total

    if in_pair:
        pieces = exchange(mixed_members(member, heads_out, heads, column), True)
        mixed = join_members(member, odd, pieces, rows).reshape(heads * out_rows, column)
    else:
        mixed_heads = jnp.swapaxes(heads_out.astype(BF16).reshape(per_device, column, HD), 1, 2)
        every = gather_members(mixed_heads)
        every = every.reshape(heads, blks, out_rows, column)
        mixed = lax.dynamic_index_in_dim(every, blk, 1).reshape(heads * out_rows, column)
    branch_parts = row_outer(mixed, out_weights)
    branch = wire.drive(
        column_scatter(lambda step: branch_parts[step * pair : (step + 1) * pair])
    )
    while wire.jobs:
        wire.phase([], behind=True)
    token_values = inputs.astype(F32)
    middle = token_values + branch
    scale_two = rms_scale(middle)
    hidden_in = (middle * scale_two * hidden_norm).astype(BF16)

    late = lax.all_gather(late, "head", axis=0)
    hidden_parts = {}
    feed_groups = []
    near = chips // 2
    groups = [sorted({hop, (chips - hop) % chips}) for hop in range(near + 1)]

    def group_pieces(index, parts):
        return [part for step in groups[index] for part in parts[step]]

    feed_weights = []

    def feed_group(index):
        tokens = jnp.concatenate(group_pieces(index, hidden_parts), axis=0)
        upstream = jnp.concatenate(group_pieces(index, cotangent_job.result), axis=0)
        gate_weights, up_weights, down_weights = feed_weights
        act_grad = col_inner(upstream, down_weights)
        if 0 < index < near:
            activated, gate_grad, up_grad, back = feed_beside(
                group_pieces(index, hidden_parts), act_grad, gate_weights, up_weights
            )
            down = dot(activated, down_weights)
            feed_groups.append((activated, gate_grad, up_grad, back, down))
            return
        gate = col_inner(tokens, gate_weights)
        up_proj = col_inner(tokens, up_weights)
        sigmoid_gate = jax.nn.sigmoid(gate)
        silu_gate = gate * sigmoid_gate
        activated = (silu_gate * up_proj).astype(BF16)
        gate_grad = (
            act_grad * up_proj * sigmoid_gate * (1.0 + gate * (1.0 - sigmoid_gate))
        ).astype(BF16)
        up_grad = (act_grad * silu_gate).astype(BF16)
        back = dot(gate_grad, gate_weights) + dot(up_grad, up_weights)
        down = dot(activated, down_weights)
        feed_groups.append((activated, gate_grad, up_grad, back, down))

    def start_feed():
        feed_weights.extend(wire.along)

    def keep_first():
        feed_group(0)
        feed_groups[0] = wire.tie(*feed_groups[0])

    wire.drive(
        column_gather(hidden_in, hidden_parts),
        hooks=[start_feed, keep_first],
        along=[
            late[:, i * feed_rows : (i + 1) * feed_rows].reshape(-1, width) for i in range(3)
        ],
    )
    for index in range(1, near + 1):
        feed_group(index)

    def group_rows(index, step):
        group = min(step, chips - step)
        at = groups[group].index(step) * pair
        return feed_groups[group][index][at : at + pair]

    hidden_pieces = sum((group_pieces(index, hidden_parts) for index in range(near + 1)), [])
    upstream_pieces = sum(
        (group_pieces(index, cotangent_job.result) for index in range(near + 1)), []
    )
    down_grads = weight_grads([group[0] for group in feed_groups], upstream_pieces, heads, 2, None)
    gate_grads = weight_grads([group[1] for group in feed_groups], hidden_pieces, heads, 0, down_grads)
    feed_grads = [gate_grads]

    def keep_grads():
        downs = [group[4].astype(BF16) for group in feed_groups]
        feed_grads[0], *downs = wire.tie(feed_grads[0], *downs)
        for index, down in enumerate(downs):
            feed_groups[index] = tuple(feed_groups[index][:4]) + (down,)

    def keep_last():
        feed_grads[0] = wire.tie(
            weight_grads([group[2] for group in feed_groups], hidden_pieces, heads, 1, feed_grads[0])
        )[0]

    hidden_grad = wire.drive(
        column_scatter(lambda step: group_rows(3, step), apart=True),
        hooks=[lambda: None] * (near + 1) + [keep_grads],
    )
    hidden_gain_grad = jnp.sum(hidden_grad * middle * scale_two, axis=0)
    middle_grad = own_cotangent.astype(F32) + norm_back(hidden_grad, middle, scale_two, hidden_norm)
    branch_grad = middle_grad.astype(BF16)
    branch_blocks = join_blocks(wire.drive(column_gather(branch_grad), hooks=[keep_last]))
    down_job = wire.add(column_scatter(lambda step: group_rows(4, step)))
    feed_grads = lax.psum_scatter(feed_grads[0], "head", scatter_dimension=0).astype(F32)
    mixed_grads = [col_inner(out_weights, block).astype(BF16) for block in branch_blocks]
    grad_out = dot(mixed, jnp.concatenate(branch_blocks, axis=0)).reshape(heads, out_rows, width)
    out_parts = [pick(grad_out, head ^ place) for place in range(heads)]
    if in_pair:
        pieces = exchange(split_blocks(member, mixed_grads, heads), True)
        upstream = upstream_members(member, odd, pieces, rows)
    else:
        mixed_grad = jnp.concatenate(mixed_grads, axis=1).reshape(heads, out_rows, column)
        every = gather_members(mixed_grad)
        every = jnp.swapaxes(every, 0, 1).reshape(blks, per_device, HD, column)
        upstream = jnp.swapaxes(pick(every, blk), 1, 2).reshape(per_device * column, HD)

    key_grads, value_grads = {}, {}
    carry = None
    for forward, backward in zip(plane_steps(False)[::-1] + [[]], plane_steps(True)[::-1] + [[]]):
        for place in [step[0] for step in forward] if forward else [0]:
            results = attend_back(
                query,
                upstream,
                logs,
                query_places,
                query_starts,
                key_pieces[place],
                value_pieces[place],
                key_places[place : place + 1],
                carry,
                heads_out,
            )
            key_grads[place] = key_grads.get(place, 0.0) + results[1]
            value_grads[place] = value_grads.get(place, 0.0) + results[2]
            carry = (results[0], carry[1] if carry else results[3])
        if not forward:
            break
        if forward == backward:
            items = [
                (
                    jnp.concatenate([key_grads[place], value_grads[place]], axis=1).astype(BF16),
                    head_move(bit),
                )
                for place, source, bit in forward
            ]
        else:
            items = [
                (key_grads[place].astype(BF16), head_move(bit)) for place, source, bit in forward
            ] + [
                (value_grads[place].astype(BF16), head_move(bit))
                for place, source, bit in backward
            ]
        tied = lax.optimization_barrier(tuple(value for value, move in items) + carry)
        items = [(value, move) for value, (ignored, move) in zip(tied, items)]
        carry = tied[len(items) :]
        got = wire.phase(items, behind=True)
        last_parts = got
        if forward[0][1] == 0:
            continue
        for index, (place, source, bit) in enumerate(forward):
            part = got[index][:, :HD].astype(F32)
            key_grads[source] = key_grads.get(source, 0.0) + part
        for index, (place, source, bit) in enumerate(backward):
            part = got[index if forward == backward else len(forward) + index]
            value_grads[source] = value_grads.get(source, 0.0) + part[:, -HD:].astype(F32)
    query_grad = carry[0]

    if in_pair:
        *pieces, gain_grads = rope_back_members(
            member, raw, query_grad, cosine, sine, norms, key_grads[0], value_grads[0], last_parts,
            query_rows, key_rows,
        )
        pieces = exchange(pieces, True)
        raw_grad = join_members(head ^ member, odd, pieces, rows).reshape(-1, column)
    else:
        key_grad = key_grads[0] + sum(part[:, :HD].astype(F32) for part in last_parts)
        value_grad = value_grads[0] + sum(part[:, HD:].astype(F32) for part in last_parts)
        query_grad = jnp.swapaxes(query_grad.reshape(per_device, column, HD), 1, 2)
        query_raw_grad, query_gain_grad = rope_backward(
            query_raw, query_norm, cosine, sine, query_grad
        )
        key_raw_grad, key_gain_grad = rope_backward(key_raw, key_norm, cosine, sine, key_grad.T)
        query_raw_grad = query_raw_grad.astype(BF16)
        key_raw_grad = key_raw_grad.astype(BF16)
        value_raw_grad = value_grad.T.astype(BF16)
        gain_grads = jnp.stack([jnp.sum(query_gain_grad, axis=0), key_gain_grad], axis=1)

        def spread(part, count, index):
            empty = jnp.zeros((count,) + part.shape[1:], BF16)
            return lax.dynamic_update_slice_in_dim(empty, part, index, 0)

        every = jnp.concatenate(
            [
                spread(query_raw_grad, QH, blk * per_device).reshape(shards, query_rows, column),
                spread(key_raw_grad[None], KVH, blk * KVH // blks).reshape(
                    shards, key_rows, column
                ),
                spread(value_raw_grad[None], KVH, blk * KVH // blks).reshape(
                    shards, key_rows, column
                ),
            ],
            axis=1,
        ).reshape(heads, blks, qkv_rows, column)
        every = reorder(jnp.swapaxes(every, 0, 1), to_ring)
        by_head = reorder(lax.psum_scatter(every, "blk", scatter_dimension=0), to_ring)
        raw_grad = jnp.concatenate(
            [pick(by_head, head ^ place) for place in range(heads)], axis=0
        )

    while down_job.wanted is not None:
        wire.phase([], behind=True)
    done = [feed_grads, (middle + down_job.result).astype(BF16)]

    qkv_grad = dot(raw_grad, normed_column)
    input_gain_grad = jnp.sum(qkv_grad * qkv_weights.astype(F32), axis=0) / input_norm
    sums = jnp.concatenate([input_gain_grad, hidden_gain_grad, gain_grads[:, 0], gain_grads[:, 1]])
    qkv_grad = qkv_grad.reshape(heads, qkv_rows, width)
    out_job = Job(plane_scatter(out_parts, True))
    tail = [
        Job(sum_everywhere(sums.reshape(-1, 128))),
        Job(plane_scatter(list(qkv_grad), False, pause=True)),
        out_job,
    ]

    def keep_done():
        done[:] = wire.along

    normed_grad = wire.drive(
        ring_scatter(
            lambda step: row_outer(raw_grad[:, step * pair : (step + 1) * pair], qkv_weights)
        ),
        hooks=[lambda: tail] + [lambda: None] * (chips - 3) + [keep_done],
        along=done,
        beside=chips - 2,
    )
    sums, grad_tail, grad_out = tail[0].result.reshape(-1), tail[1].result, out_job.result
    feed_grads, layer_out = done
    grad_gate, grad_up, grad_down = (
        feed_grads[i * feed_rows : (i + 1) * feed_rows] for i in range(3)
    )
    token_values = wire.token.astype(F32)
    grad_input = middle_grad + norm_back(
        normed_grad, token_values, rms_scale(token_values), input_norm
    )

    def own_part(at, size):
        return lax.dynamic_slice_in_dim(sums, at, size)

    return (
        layer_out,
        grad_input,
        own_part(shard * input_gain.shape[0], input_gain.shape[0]),
        grad_tail[:query_rows].T,
        grad_tail[query_rows : query_rows + key_rows].T,
        grad_tail[query_rows + key_rows :].T,
        own_part(2 * width + shard * query_gain.shape[0], query_gain.shape[0]),
        own_part(2 * width + HD + shard * key_gain.shape[0], key_gain.shape[0]),
        grad_out,
        own_part(width + blk * hidden_gain.shape[0], hidden_gain.shape[0]),
        grad_gate.T,
        grad_up.T,
        grad_down,
    )


def solution(mesh):
    return jax.shard_map(
        local,
        mesh=mesh,
        in_specs=(
            P(("blk", "head"), None),
            P(),
            P(),
            P(("head", "blk")),
            P(None, ("head", "blk")),
            P(None, ("head", "blk")),
            P(None, ("head", "blk")),
            P(("head", "blk")),
            P(("head", "blk")),
            P(("head", "blk"), None),
            P("blk"),
            P(None, ("head", "blk")),
            P(None, ("head", "blk")),
            P(("head", "blk"), None),
            P("blk", None),
        ),
        out_specs=(
            P(("blk", "head"), None),
            P(("blk", "head"), None),
            P(("head", "blk")),
            P(None, ("head", "blk")),
            P(None, ("head", "blk")),
            P(None, ("head", "blk")),
            P(("head", "blk")),
            P(("head", "blk")),
            P(("head", "blk"), None),
            P("blk"),
            P(None, ("head", "blk")),
            P(None, ("head", "blk")),
            P(("head", "blk"), None),
        ),
        check_vma=False,
    )
```
